128 devices in a mesh: expert: 32 (over z, x, core), head: 4 (over y).
Axes of the slice: x: 4, y: 4, z: 4, core: 2. Of those that a mesh axis runs over, the one named last changes fastest.
Arguments:
- tokens: bfloat16 [32768, 1024], P(('expert', 'head')), may hold values from -6 to 6
- cotangent: bfloat16 [32768, 1024], P(('expert', 'head')), may hold values from -6 to 6
- routes: int32 [32768, 8], P(('expert', 'head')), may hold values from 0 to 31, all different within a row; in each aligned block of 256 rows (0 to 255, 256 to 511, ...) at most 96 rows name the same one
- lengths: int32 [32, 8], P('expert'), may hold values from 1 to 896, as said below
- gain_attn: float32 [1024], replicated, may hold values from 0.5 to 1.5
- w_query: bfloat16 [1024, 1024], P(None, 'head'), may hold values from -0.1875 to 0.1875
- w_key: bfloat16 [1024, 512], P(None, 'head'), may hold values from -0.1875 to 0.1875
- w_value: bfloat16 [1024, 512], P(None, 'head'), may hold values from -0.1875 to 0.1875
- w_output: bfloat16 [1024, 1024], P('head'), may hold values from -1.5 to 1.5
- gain_mix: float32 [1024], replicated, may hold values from 0.5 to 1.5
- w_router: float32 [1024, 32], replicated, may hold values from -0.09375 to 0.09375
- gate_weight: bfloat16 [32, 1024, 512], P('expert'), may hold values from -0.1875 to 0.1875
- up_weight: bfloat16 [32, 1024, 512], P('expert'), may hold values from -0.1875 to 0.1875
- down_weight: bfloat16 [32, 512, 1024], P('expert'), may hold values from -1.5 to 1.5
Outputs:
- output: bfloat16 [32768, 1024], P(('expert', 'head'))
- grad_tokens: float32 [32768, 1024], P(('expert', 'head'))
- grad_gain_attn: float32 [1024], replicated
- grad_w_query: float32 [1024, 1024], P(None, 'head')
- grad_w_key: float32 [1024, 512], P(None, 'head')
- grad_w_value: float32 [1024, 512], P(None, 'head')
- grad_w_output: float32 [1024, 1024], P('head')
- grad_gain_mix: float32 [1024], replicated
- grad_w_router: float32 [1024, 32], replicated
- grad_w_gate: float32 [32, 1024, 512], P('expert')
- grad_w_up: float32 [32, 1024, 512], P('expert')
- grad_w_down: float32 [32, 512, 1024], P('expert')
The draws below stay inside these ranges and needn't reach their ends.
Inputs may be any that keep to these rules, and one draw needn't show every extreme that they name: `routes`: each row names 8 different experts. Among the 256 rows of one device no expert is named by more than 96 rows, a bound that some block reaches of them. Row g lists the lengths of the 8 sequences packed in order into the 1024 tokens of group g; they sum to 1024, and one of them has length 896.
All inputs are finite; a program needn't handle non-finite values.
Results may differ from the reference program's by a relative error of at most 0.03.
Values may be sent and summed in bfloat16 or wider, within the bound.
No kernel may reach another device: no remote copies, remote signals or barrier semaphores. Data moves between devices by JAX's collectives and lax.ppermute only.
A program may use at most 256 MiB of HBM per device.

```python
import math
import jax
import jax.numpy as jnp
import numpy as np
from jax import lax

D = 1024
HEADS = 16
KV_HEADS = 8
HEAD_DIM = 64
FF = 512
TOPK = 8
ROWS = 256
NSEQ = 8
EXPERTS = 32
GROUP = 1024
GROUPS = 32
TOKENS = 32768
CAP = 96


def draw_lengths(key, part):
    key = jax.random.fold_in(key, 7)
    spare = ROWS // 2
    longest = GROUP - spare

    def one_group(sub_key):
        first_key, second_key = jax.random.split(sub_key)
        cut_points = jnp.sort(jax.random.permutation(first_key, spare - 1)[:NSEQ - 2] + 1).astype(jnp.int32)
        bounds = jnp.concatenate([jnp.zeros((1,), jnp.int32), cut_points, jnp.full((1,), spare, jnp.int32)])
        short_lens = bounds[1:] - bounds[:-1]
        long_slot = jax.random.randint(second_key, (), 0, NSEQ)
        slot_pos = jnp.arange(NSEQ, dtype=jnp.int32)
        before = short_lens[jnp.clip(slot_pos, 0, NSEQ - 2)]
        behind = short_lens[jnp.clip(slot_pos - 1, 0, NSEQ - 2)]
        return jnp.where(slot_pos < long_slot, before, jnp.where(slot_pos == long_slot, longest, behind)).astype(jnp.int32)
    return jax.vmap(one_group)(jax.random.split(key, GROUPS))


def block_scale(own_key, dims, shards, low, high):
    gain, own = 1.0, jax.random.fold_in(own_key, 6)
    for axis_at, blocks in shards:
        draws = jnp.exp(jax.random.uniform(jax.random.fold_in(own, axis_at), (blocks,), jnp.float32, low / len(shards), high / len(shards)))
        gain = gain * jnp.repeat(draws, dims[axis_at] // blocks).reshape([-1 if axis == axis_at else 1 for axis in range(len(dims))])
    return gain


def deal_out(rng, own, number, rows, number_of, top, most, lean):
    ranking = jax.random.permutation(rng, number_of)
    heavy_load, common = shares(number_of, rows * top, most, lean, True), shares(number_of, rows * top, most, lean, False)
    places = jnp.arange(number_of)

    def named(sizes, rotation):
        used = int((sizes > 0).sum())
        fixed = max(1, used // 4)
        shifted = fixed + (places - fixed + rotation * (used - fixed)) % max(1, number_of - fixed)
        return jnp.zeros((number_of,), jnp.int32).at[ranking[jnp.where(places < fixed, places, shifted)]].set(jnp.asarray(sizes, jnp.int32))

    sizes = jnp.where(number % 4 == 0, named(heavy_load, number // 4), named(common, number - number // 4 - 1))
    mixed = jax.random.permutation(jax.random.fold_in(own, 3), number_of)
    source_of, taker = mixed[0:number_of // 2 * 2:2], mixed[1:number_of // 2 * 2:2]
    room = jnp.minimum(sizes[source_of] - 1, most - sizes[taker]) // 2
    room = jnp.where((source_of == ranking[0]) | (taker == ranking[0]) | (sizes[taker] == 0), 0, jnp.maximum(room, 0))
    shifted = jax.random.randint(jax.random.fold_in(own, 4), (number_of // 2,), 0, 1 << 20) % (room + 1)
    sizes = sizes.at[source_of].add(-shifted).at[taker].add(shifted)
    labels = jnp.searchsorted(jnp.cumsum(sizes), jnp.arange(rows * top), side="right").astype(jnp.int32)
    listing = labels.reshape(top, rows).T
    listing = listing[jax.random.permutation(jax.random.fold_in(own, 1), rows)]
    rotation = jax.random.randint(jax.random.fold_in(own, 2), (rows, 1), 0, top)
    return jnp.take_along_axis(listing, (jnp.arange(top)[None, :] + rotation) % top, axis=1)


def shares(number_of, total, bound, lean, full):
    weights = [(1 << 20) // math.isqrt(grade ** lean) + 1 for grade in range(1, number_of + 1)]
    largest = bound if full else min(bound, max(-(-total // number_of), total * weights[0] // sum(weights)))
    least = 1 if total - largest >= number_of - 1 else 0
    counts, spare = [largest] + [least] * (number_of - 1), total - largest - least * (number_of - 1)
    while spare > 0:
        movable = [i for i in range(1, number_of) if counts[i] < largest] or [i for i in range(1, number_of) if counts[i] < bound]
        mass, remaining = sum([weights[i] for i in movable]), spare
        for i in movable:
            extra = min(bound - counts[i], max(1, remaining * weights[i] // mass), spare)
            counts[i] = counts[i] + extra
            spare = spare - extra
    return np.array(counts)


def gaussian(stream_key, extent, width, bound, shards=(), held_as=jnp.bfloat16):
    entries = jax.random.normal(stream_key, extent, jnp.float32) * width
    if len(shards) > 0:
        entries = block_scale(stream_key, extent, shards, -0.22, 0.18) * entries
    return jnp.clip(entries, min=-bound, max=bound).astype(held_as)


def setup_inputs(seed: int = 0) -> dict:
    key_list = jax.random.split(jax.random.key(seed), 15)
    tokens = gaussian(key_list[0], (TOKENS, D), 1.0, 6.0, ((0, 128),))
    cotangent = gaussian(key_list[1], (TOKENS, D), 1.0, 6.0, ((0, 128),))
    routes_keys = jax.random.split(jax.random.fold_in(key_list[2], 1), TOKENS // ROWS)
    routes_turns = jax.random.permutation(jax.random.fold_in(key_list[2], 3), TOKENS // ROWS)
    routes = jax.vmap(lambda own, number: deal_out(jax.random.fold_in(key_list[2], 2), own, number, ROWS, EXPERTS, TOPK, CAP, 2))(routes_keys, routes_turns).reshape((TOKENS, TOPK))
    lengths = draw_lengths(jax.random.fold_in(key_list[14], 71), 0)
    gain_attn = jnp.clip(1.0 + 0.1 * jax.random.normal(key_list[4], (D,), jnp.float32), 0.5, 1.5)
    w_query = gaussian(key_list[5], (D, HEADS * HEAD_DIM), D ** -0.5, 0.1875, ((1, 4),))
    w_key = gaussian(key_list[6], (D, KV_HEADS * HEAD_DIM), D ** -0.5, 0.1875, ((1, 4),))
    w_value = gaussian(key_list[7], (D, KV_HEADS * HEAD_DIM), D ** -0.5, 0.1875, ((1, 4),))
    w_output = gaussian(key_list[8], (HEADS * HEAD_DIM, D), (max(HEADS * HEAD_DIM // 64, 1)) ** -0.5, 1.5, ((0, 4),))
    gain_mix = jnp.clip(1.0 + 0.1 * jax.random.normal(key_list[9], (D,), jnp.float32), 0.5, 1.5)
    w_router = gaussian(key_list[10], (D, EXPERTS), (4 * D) ** -0.5, 0.09375, (), jnp.float32)
    gate_weight = gaussian(key_list[11], (EXPERTS, D, FF), D ** -0.5, 0.1875, ((0, 32),))
    up_weight = gaussian(key_list[12], (EXPERTS, D, FF), D ** -0.5, 0.1875, ((0, 32),))
    down_weight = gaussian(key_list[13], (EXPERTS, FF, D), (max(FF // 32, 1)) ** -0.5, 1.5, ((0, 32),))
    return dict(tokens=tokens, cotangent=cotangent, routes=routes, lengths=lengths, gain_attn=gain_attn, w_query=w_query, w_key=w_key, w_value=w_value, w_output=w_output, gain_mix=gain_mix, w_router=w_router, gate_weight=gate_weight, up_weight=up_weight, down_weight=down_weight)


@jax.custom_vjp
def low(v):
    return lax.optimization_barrier(v.astype(jnp.bfloat16)).astype(jnp.float32)

@jax.custom_vjp
def low_back(v):
    return v

def low_keep(v):
    return (low(v), None)

def low_pass(kept, grad):
    return (grad,)

def back_keep(v):
    return (v, None)

def back_low(kept, grad):
    return (low(grad),)
low.defvjp(low_keep, low_pass)
low_back.defvjp(back_keep, back_low)
eps_norm = 1e-06
rope_base = 10000.0
mask_fill = -1000000000.0
highest = lax.Precision.HIGHEST

def rms_scale(values, gain_vec):
    return values * lax.rsqrt(lax.optimization_barrier(jnp.mean(values * values, axis=-1, keepdims=True)) + eps_norm) * gain_vec

def rotate(values, position):
    half_dim = values.shape[-1] // 2
    frequency = rope_base ** (-2.0 * jnp.arange(half_dim, dtype=jnp.float32) / values.shape[-1])
    angles = position.astype(jnp.float32)[:, None] * frequency[None, :]
    cosine = jnp.cos(angles)[:, None, :]
    sine_vals = jnp.sin(angles)[:, None, :]
    front_half = values[..., :half_dim]
    back_half = values[..., half_dim:]
    return jnp.concatenate([front_half * cosine - back_half * sine_vals, back_half * cosine + front_half * sine_vals], axis=-1)

def doc_layout(seq_lengths, group_rows):
    seq_ends = jnp.cumsum(seq_lengths, dtype=jnp.int32)
    starts = seq_ends - seq_lengths
    row_index = jnp.arange(group_rows, dtype=jnp.int32)
    segment = lax.optimization_barrier(jnp.sum((row_index[:, None] >= seq_ends[None, :]).astype(jnp.int32), axis=1, dtype=jnp.int32))
    in_seq = segment[:, None] == jnp.arange(seq_lengths.shape[0], dtype=jnp.int32)[None, :]
    beginning = lax.optimization_barrier(jnp.sum(jnp.where(in_seq, starts[None, :], 0), axis=1, dtype=jnp.int32))
    return (segment, row_index - beginning, row_index)

def group_layer(resid, seq_lengths, route, gain_first, query_mat, key_mat, value_mat, output_mat, gain_second, router_mat, gate_mats, up_mats, down_mats):
    group_rows = resid.shape[0]
    segment, position, row_index = doc_layout(seq_lengths, group_rows)
    normed_first = low(rms_scale(resid, gain_first))
    query_raw = low_back(jnp.dot(normed_first, query_mat, precision=highest)).reshape(group_rows, HEADS, HEAD_DIM)
    key_raw = low_back(jnp.dot(normed_first, key_mat, precision=highest)).reshape(group_rows, KV_HEADS, HEAD_DIM)
    value_low = low(low_back(jnp.dot(normed_first, value_mat, precision=highest))).reshape(group_rows, KV_HEADS, HEAD_DIM)
    query_low = low(rotate(query_raw, position)).reshape(group_rows, KV_HEADS, HEADS // KV_HEADS, HEAD_DIM)
    key_low = low(rotate(key_raw, position))
    scores = low_back(jnp.einsum('gkrd,skd->krgs', query_low, key_low, precision=highest) * HEAD_DIM ** (-0.5))
    allowed = (segment[:, None] == segment[None, :]) & (row_index[None, :] <= row_index[:, None])
    masked = jnp.where(allowed, scores, mask_fill)
    row_peak = lax.optimization_barrier(jnp.max(masked, axis=-1, keepdims=True))
    lifted = jnp.exp(masked - row_peak)
    attn_weights = lifted / lax.optimization_barrier(jnp.sum(lifted, axis=-1, keepdims=True))
    mixed = jnp.einsum('krgs,skd->gkrd', low(attn_weights), value_low, precision=highest).reshape(group_rows, HEADS * HEAD_DIM)
    mixed_low = low(low_back(mixed))
    hidden_first = resid + low_back(jnp.dot(mixed_low, output_mat, precision=highest))
    normed_second = rms_scale(hidden_first, gain_second)
    logits = jnp.dot(normed_second, router_mat, precision=highest)
    gates = jax.nn.softmax(jnp.take_along_axis(logits, route, axis=1), axis=1)
    chosen = (route[:, :, None] == jnp.arange(gate_mats.shape[0], dtype=jnp.int32)[None, None, :]).astype(jnp.float32)
    share = lax.optimization_barrier(jnp.sum(gates[:, :, None] * chosen, axis=1))
    inputs = low(normed_second)

    def one_expert(running, expert_item):
        gate_mat, up_mat, down_mat, column = expert_item
        entry = low_back(inputs)
        gate_pre = low_back(jnp.dot(entry, gate_mat, precision=highest))
        up_pre = low_back(jnp.dot(entry, up_mat, precision=highest))
        active = low(jax.nn.silu(gate_pre) * up_pre)
        produced = low(low_back(jnp.dot(active, down_mat, precision=highest)))
        return (running + column[:, None] * produced, None)
    mixture, _ = lax.scan(jax.checkpoint(one_expert), jnp.zeros_like(hidden_first), (gate_mats, up_mats, down_mats, share.T))
    return hidden_first + mixture

def reference(tokens, cotangent, routes, lengths, gain_attn, w_query, w_key, w_value, w_output, gain_mix, w_router, gate_weight, up_weight, down_weight):
    group_count = lengths.shape[0]
    model_width = tokens.shape[1]
    shaped = tokens.astype(jnp.float32).reshape(group_count, -1, model_width)
    routed = routes.reshape(group_count, -1, routes.shape[1])

    def layer(block_in, gain_first, query_mat, key_mat, value_mat, output_mat, gain_second, router_mat, gate_mats, up_mats, down_mats):

        def per_group(group_item):
            return group_layer(group_item[0], group_item[1], group_item[2], gain_first, query_mat, key_mat, value_mat, output_mat, gain_second, router_mat, gate_mats, up_mats, down_mats)
        return lax.map(jax.checkpoint(per_group), (block_in, lengths, routed))
    result, pullback = jax.vjp(layer, shaped, gain_attn.astype(jnp.float32), w_query.astype(jnp.float32), w_key.astype(jnp.float32), w_value.astype(jnp.float32), w_output.astype(jnp.float32), gain_mix.astype(jnp.float32), w_router.astype(jnp.float32), gate_weight.astype(jnp.float32), up_weight.astype(jnp.float32), down_weight.astype(jnp.float32))
    grads = pullback(cotangent.astype(jnp.float32).reshape(group_count, -1, model_width))
    return (result.reshape(-1, model_width).astype(jnp.bfloat16), grads[0].reshape(-1, model_width), grads[1], grads[2], grads[3], grads[4], grads[5], grads[6], grads[7], grads[8], grads[9], grads[10])
```

```python
import jax
import jax.numpy as jnp
from jax import lax
from jax.sharding import PartitionSpec as P

HEAD_DIM = 64


eps_norm = 1e-06
rope_base = 10000.0
mask_fill = -1000000000.0


def all_rows(array, axis):
    length = lax.axis_size(axis)
    sent = jnp.broadcast_to(array[None], (length, *array.shape))
    arrived = lax.all_to_all(sent, axis, 0, 0, tiled=True)
    return arrived.reshape(length * array.shape[0], *array.shape[1:])


def swap(array, axis):
    return lax.all_to_all(array, axis, 0, 0, tiled=True)


def sum_at_owner(array, axis):
    length = lax.axis_size(axis)
    arrived = swap(array.reshape(length, array.shape[0] // length, *array.shape[1:]), axis)
    return arrived.astype(jnp.float32).sum(axis=0)


def rms_scale(values, gain_vec):
    return (
        values * lax.rsqrt(jnp.mean(values * values, axis=-1, keepdims=True) + eps_norm) * gain_vec
    )


def rotate(values, cosine, sine_vals):
    half_dim = values.shape[-1] // 2
    front_half = values[..., :half_dim]
    back_half = values[..., half_dim:]
    return jnp.concatenate(
        [front_half * cosine - back_half * sine_vals, back_half * cosine + front_half * sine_vals],
        axis=-1,
    )


def doc_layout(seq_lengths, group_rows):
    seq_ends = jnp.cumsum(seq_lengths, dtype=jnp.int32)
    row_index = jnp.arange(group_rows, dtype=jnp.int32)
    beginning = jnp.max(
        jnp.where(row_index[:, None] >= seq_ends[None, :], seq_ends[None, :], 0), axis=1
    )
    return beginning, row_index


def wide(spec, left, right):
    return jnp.einsum(spec, left, right, preferred_element_type=jnp.float32)


def body(
    tokens,
    cotangent,
    routes,
    lengths,
    gain_attn,
    w_query,
    w_key,
    w_value,
    w_output,
    gain_mix,
    w_router,
    gate_weight,
    up_weight,
    down_weight,
):
    bf16 = jnp.bfloat16
    row_count, model_width = tokens.shape
    pick_count = routes.shape[1]
    head_count = lax.axis_size("head")
    expert_count = lax.axis_size("expert")
    group_rows = row_count * head_count
    query_heads = w_query.shape[1] // HEAD_DIM
    key_heads = w_key.shape[1] // HEAD_DIM
    repeat_count = query_heads // key_heads
    score_scale = HEAD_DIM ** (-0.5)
    capacity = min(row_count, 3 * row_count * pick_count // (2 * expert_count))
    gate_mat, up_mat, down_mat = gate_weight[0], up_weight[0], down_weight[0]

    chosen = jnp.any(
        routes[:, :, None] == jnp.arange(expert_count, dtype=jnp.int32)[None, None, :], axis=1
    )
    earlier = jnp.arange(row_count)[:, None] > jnp.arange(row_count)[None, :]
    rank_in = jnp.dot(earlier.astype(bf16), chosen.astype(bf16), preferred_element_type=jnp.float32)
    slot_of = jnp.where(chosen, rank_in, -1.0).T
    picks = slot_of[:, None, :] == jnp.arange(capacity, dtype=jnp.float32)[None, :, None]
    picks_low = picks.astype(bf16).reshape(expert_count * capacity, row_count)

    def dispatch(rows):
        taken = jnp.dot(picks_low, rows, preferred_element_type=jnp.float32).astype(bf16)
        return swap(taken.reshape(expert_count, capacity, model_width), "expert")

    def collect(slots):
        return lax.dot_general(
            picks_low,
            slots.reshape(expert_count * capacity, model_width),
            (((0,), (0,)), ((), ())),
            preferred_element_type=jnp.float32,
        )

    grad_arrived = dispatch(cotangent)

    beginning, row_index = doc_layout(lengths[0], group_rows)
    position = row_index - beginning
    allowed = (row_index[None, :] >= beginning[:, None]) & (
        row_index[None, :] <= row_index[:, None]
    )
    half_dim = HEAD_DIM // 2
    frequency = rope_base ** (-2.0 * jnp.arange(half_dim, dtype=jnp.float32) / HEAD_DIM)
    angles = position.astype(jnp.float32)[:, None] * frequency[None, :]
    cosine = jnp.cos(angles)[:, None, :]
    sine_vals = jnp.sin(angles)[:, None, :]

    resid_full = all_rows(tokens, "head").astype(jnp.float32)
    full_rows = rms_scale(resid_full, gain_attn).astype(bf16)
    query_raw = jnp.dot(full_rows, w_query, preferred_element_type=jnp.float32).reshape(
        group_rows, query_heads, HEAD_DIM
    )
    key_raw = jnp.dot(full_rows, w_key, preferred_element_type=jnp.float32).reshape(
        group_rows, key_heads, HEAD_DIM
    )
    value_low = (
        jnp.dot(full_rows, w_value, preferred_element_type=jnp.float32)
        .astype(bf16)
        .reshape(group_rows, key_heads, HEAD_DIM)
    )
    query_low = (
        rotate(query_raw, cosine, sine_vals)
        .astype(bf16)
        .reshape(group_rows, key_heads, repeat_count, HEAD_DIM)
    )
    key_low = rotate(key_raw, cosine, sine_vals).astype(bf16)

    def masked_scores():
        product = wide("gkrd,skd->krgs", query_low, key_low) * score_scale
        return jnp.where(allowed, product, mask_fill)

    scores = masked_scores()
    row_peak = jnp.max(scores, axis=-1, keepdims=True)
    lifted = jnp.exp(scores - row_peak)
    row_total = jnp.sum(lifted, axis=-1, keepdims=True)
    log_total = row_peak + jnp.log(row_total)
    weights_low = (lifted / row_total).astype(bf16)
    mixed_low = (
        wide("krgs,skd->gkrd", weights_low, value_low)
        .reshape(group_rows, query_heads * HEAD_DIM)
        .astype(bf16)
    )
    attn_out = sum_at_owner(
        jnp.dot(mixed_low, w_output, preferred_element_type=jnp.float32).astype(bf16), "head"
    )
    resid = tokens.astype(jnp.float32)
    hidden_first = resid + attn_out
    normed_second = rms_scale(hidden_first, gain_mix)
    inputs_arrived = dispatch(normed_second.astype(bf16))
    logits = jnp.dot(normed_second, w_router)
    peak = jnp.max(jnp.where(chosen, logits, -jnp.inf), axis=1, keepdims=True)
    raised = jnp.where(chosen, jnp.exp(jnp.minimum(logits - peak, 0.0)), 0.0)
    share = raised / jnp.sum(raised, axis=1, keepdims=True)
    gate_slot = jnp.sum(jnp.where(picks, share.T[:, None, :], 0.0), axis=2)
    gate_arrived = swap(gate_slot, "expert").reshape(expert_count * capacity, 1)

    rows_in = inputs_arrived.reshape(expert_count * capacity, model_width)
    rows_grad = grad_arrived.reshape(expert_count * capacity, model_width)
    gate_pre = jnp.dot(rows_in, gate_mat, preferred_element_type=jnp.float32)
    up_pre = jnp.dot(rows_in, up_mat, preferred_element_type=jnp.float32)
    silu_at, silu_pull = jax.vjp(jax.nn.silu, gate_pre)
    active = (silu_at * up_pre).astype(bf16)
    produced = jnp.dot(active, down_mat, preferred_element_type=jnp.float32).astype(bf16)
    wide_grad = rows_grad.astype(jnp.float32)
    gate_grad_slot = jnp.sum(wide_grad * produced.astype(jnp.float32), axis=1)
    grad_produced = (wide_grad * gate_arrived).astype(bf16)
    grad_active = wide("zy,my->zm", grad_produced, down_mat)
    grad_up_pre = (grad_active * silu_at).astype(bf16)
    grad_gate_pre = silu_pull(grad_active * up_pre)[0].astype(bf16)
    grad_inputs = (
        wide("kn,sn->ks", grad_gate_pre, gate_mat) + wide("kn,sn->ks", grad_up_pre, up_mat)
    ).astype(bf16)
    gate_grad_back = swap(gate_grad_slot.reshape(expert_count, capacity), "expert")
    grad_back = swap(grad_inputs.reshape(expert_count, capacity, model_width), "expert")
    grad_w_down = wide("zm,zy->my", active, grad_produced)
    grad_w_gate = wide("ns,ny->sy", rows_in, grad_gate_pre)
    grad_w_up = wide("ns,ny->sy", rows_in, grad_up_pre)

    grad_share = jnp.sum(jnp.where(picks, gate_grad_back[:, :, None], 0.0), axis=1).T
    grad_logits = share * (grad_share - jnp.sum(share * grad_share, axis=1, keepdims=True))
    grad_router_part = wide("td,te->de", normed_second, grad_logits)
    grad_normed2 = collect(grad_back) + wide("te,de->td", grad_logits, w_router)
    _, second_pull = jax.vjp(rms_scale, hidden_first, gain_mix)
    grad_from_norm, grad_gain_mix_part = second_pull(grad_normed2)
    grad_hidden = cotangent.astype(jnp.float32) + grad_from_norm
    grad_full = all_rows(grad_hidden.astype(bf16), "head")

    produced_held, _ = lax.optimization_barrier((produced, grad_back))
    returned = swap(produced_held.reshape(expert_count, capacity, model_width), "expert")

    grad_w_output = wide("gm,gd->md", mixed_low, grad_full)
    grad_mixed = (
        wide("gd,md->gm", grad_full, w_output)
        .astype(bf16)
        .reshape(group_rows, key_heads, repeat_count, HEAD_DIM)
    )
    attn_weights = jnp.exp(masked_scores() - log_total)
    grad_weights = wide("gkrd,skd->krgs", grad_mixed, value_low)
    grad_value = wide("krgs,gkrd->skd", attn_weights.astype(bf16), grad_mixed)
    inner = jnp.sum(attn_weights * grad_weights, axis=-1, keepdims=True)
    grad_scores = (attn_weights * (grad_weights - inner)).astype(bf16)
    grad_query_rot = wide("krgs,skd->gkrd", grad_scores, key_low) * score_scale
    grad_key_rot = wide("krgs,gkrd->skd", grad_scores, query_low) * score_scale
    grad_query = (
        rotate(grad_query_rot.reshape(group_rows, query_heads, HEAD_DIM), cosine, -sine_vals)
        .reshape(group_rows, -1)
        .astype(bf16)
    )
    grad_key = rotate(grad_key_rot, cosine, -sine_vals).reshape(group_rows, -1).astype(bf16)
    grad_value_low = grad_value.reshape(group_rows, -1).astype(bf16)
    total_term = wide("gm,dm->gd", grad_query, w_query)
    total_term = total_term + wide("gm,dm->gd", grad_key, w_key)
    total_term = total_term + wide("gm,dm->gd", grad_value_low, w_value)
    grad_normed1 = sum_at_owner(total_term.astype(bf16), "head")
    grad_w_query = wide("gd,gm->dm", full_rows, grad_query)
    grad_w_key = wide("gd,gm->dm", full_rows, grad_key)
    grad_w_value = wide("gd,gm->dm", full_rows, grad_value_low)
    _, first_pull = jax.vjp(rms_scale, resid, gain_attn)
    grad_from_first, grad_gain_attn_part = first_pull(grad_normed1)
    grad_tokens = grad_hidden + grad_from_first
    gated = (picks_low.reshape(expert_count, capacity, row_count) * share.T[:, None, :]).astype(
        bf16
    )
    mixture = lax.dot_general(
        gated.reshape(expert_count * capacity, row_count),
        returned.reshape(expert_count * capacity, model_width),
        (((0,), (0,)), ((), ())),
        preferred_element_type=jnp.float32,
    )
    output = (hidden_first + mixture).astype(bf16)

    def summed(part, axis):
        return lax.psum(part.astype(bf16), axis).astype(jnp.float32)

    return (
        output,
        grad_tokens,
        summed(grad_gain_attn_part, ("expert", "head")),
        summed(grad_w_query, "expert"),
        summed(grad_w_key, "expert"),
        summed(grad_w_value, "expert"),
        summed(grad_w_output, "expert"),
        summed(grad_gain_mix_part, ("expert", "head")),
        summed(grad_router_part, ("expert", "head")),
        summed(grad_w_gate, "head")[None],
        summed(grad_w_up, "head")[None],
        summed(grad_w_down, "head")[None],
    )


def solution(mesh):
    rows = P(("expert", "head"), None)
    per_expert = P("expert", None, None)
    columns = P(None, "head")
    in_specs = (
        rows,
        rows,
        rows,
        P("expert", None),
        P(),
        columns,
        columns,
        columns,
        P("head", None),
        P(),
        P(),
        per_expert,
        per_expert,
        per_expert,
    )
    out_specs = (
        rows,
        rows,
        P(),
        columns,
        columns,
        columns,
        P("head", None),
        P(),
        P(),
        per_expert,
        per_expert,
        per_expert,
    )
    return jax.shard_map(body, mesh=mesh, in_specs=in_specs, out_specs=out_specs, check_vma=False)
```

```python
import functools

import jax
import jax.numpy as jnp
from jax import lax
from jax.experimental import pallas as pl
from jax.experimental.pallas import tpu as pltpu
from jax.sharding import PartitionSpec as P

HEAD_DIM = 64
SIDE = 4
LANES = 128
MIB = 1024 * 1024

eps_norm = 1e-06
rope_base = 10000.0
mask_fill = -1000000000.0

bf16 = jnp.bfloat16
f32 = jnp.float32


def dot(left, right):
    return lax.dot_general(left, right, (((1,), (0,)), ((), ())), preferred_element_type=f32)


def dot_rows(left, right):
    return lax.dot_general(left, right, (((1,), (1,)), ((), ())), preferred_element_type=f32)


def dot_cols(left, right):
    return lax.dot_general(left, right, (((0,), (0,)), ((), ())), preferred_element_type=f32)


def call(kernel, out_shapes, args, specs=None, grid=None, out_specs=None, scratch=(), flops=0, vmem=60, aliases=None):
    moved = sum(a.size * a.dtype.itemsize for a in args)
    moved += sum(s.size * s.dtype.itemsize for s in out_shapes)
    whole = pl.BlockSpec(memory_space=pltpu.VMEM)
    settings = {} if grid is None else {"grid": grid}
    return pl.pallas_call(
        kernel,
        out_shape=out_shapes,
        in_specs=specs or [whole] * len(args),
        out_specs=out_specs or [whole] * len(out_shapes),
        scratch_shapes=list(scratch),
        input_output_aliases=aliases or {},
        compiler_params=pltpu.CompilerParams(vmem_limit_bytes=vmem * MIB),
        cost_estimate=pl.CostEstimate(flops=flops, bytes_accessed=moved, transcendentals=0),
        **settings,
    )(*args)


def array(shape, dtype):
    return jax.ShapeDtypeStruct(shape, dtype)


CHIPS = ("z", "x")
PLANE = ("z", "x", "core")


def line_shift(values, step):
    pairs = [(i, (i + step) % SIDE) for i in range(SIDE)]
    return lax.ppermute(values, "head", pairs)


def plane_shift(first, values, step):
    pairs = []
    for i in range(2 * SIDE * SIDE):
        z, x, core = i // (2 * SIDE), i // 2 % SIDE, i % 2
        if (core == 0) == first:
            z = (z + step) % SIDE
        else:
            x = (x + step) % SIDE
        pairs.append((i, (z * SIDE + x) * 2 + core))
    return lax.ppermute(values, PLANE, pairs)


shift_u = functools.partial(plane_shift, True)
shift_w = functools.partial(plane_shift, False)


def swap_core(values):
    return lax.ppermute(values, "core", [(0, 1), (1, 0)])


def after(values, *earlier):
    return lax.optimization_barrier((values, *earlier))[0]


def ring_gather(block, shift, *between):
    half = block.shape[0] // 32 * 16
    from_before, from_after = shift(block, 1), shift(block, -1)
    if between:
        from_before, from_after, *_ = lax.optimization_barrier((from_before, from_after, *between))
    far_lo, far_hi = shift(from_before[:half], 1), shift(from_after[half:], -1)
    return block, from_after, far_lo, far_hi, from_before


def direct_swap(parts, shift):
    return [parts[0], shift(parts[3], -1), shift(parts[2], 2), shift(parts[1], 1)]


def ring_sum(parts, shift):
    before_high, after_low = shift(parts[1][1], 1), shift(parts[3][0], -1)
    low_in, high_in = shift(parts[2][0], 1), shift(parts[2][1], -1)
    up = (parts[1][0].astype(f32) + low_in.astype(f32)).astype(bf16)
    down = (parts[3][1].astype(f32) + high_in.astype(f32)).astype(bf16)
    before_low, after_high = shift(up, 1), shift(down, -1)
    return (before_low, before_high), (after_low, after_high)


def swap_all(values, axes):
    return lax.all_to_all(values, axes, 0, 0, tiled=True)


def all_blocks(block, axes):
    count = lax.axis_size(axes)
    return swap_all(jnp.broadcast_to(block[None], (count, *block.shape)), axes)


def rope(values, cosine, sine_signed):
    lane = lax.broadcasted_iota(jnp.int32, cosine.shape, 1)
    front = lane % HEAD_DIM < HEAD_DIM // 2
    out = []
    for at in range(0, values.shape[1], LANES):
        part = values[:, at : at + LANES]
        partner = jnp.where(
            front,
            pltpu.roll(part, LANES - HEAD_DIM // 2, 1),
            pltpu.roll(part, HEAD_DIM // 2, 1),
        )
        out.append(part * cosine + partner * sine_signed)
    return jnp.concatenate(out, axis=1)


def place(at, distance, rows):
    return pl.ds(pl.multiple_of((at[3] + distance) % SIDE * rows, rows), rows)


def attend_kernel(
    at, own, from_after, far_lo, far_hi, from_before, gain, weights, cosine, sine, starts,
    normed_out, query_out, key_out, value_out, mixed_out, log_out, mixed_0, mixed_1, mixed_2, mixed_3,
    rows_in, normed, query, key, value, mixed, log_total, sems,
):
    rows = own.shape[0]
    width = query.shape[1]
    kept = (normed, query, key, value, mixed, log_total)
    outs = (normed_out, query_out, key_out, value_out, mixed_out, log_out)

    def keep(i, n):
        here = pl.ds(i * rows, rows)
        return pltpu.make_async_copy(kept[n].at[here, :], outs[n].at[here, :], sems.at[i, n])

    rows_in[place(at, 0, rows), :] = own[...]
    rows_in[place(at, 1, rows), :] = from_after[...]
    rows_in[place(at, 3, rows), :] = from_before[...]
    half = rows // 2
    far = (at[3] + 2) % SIDE * rows
    rows_in[pl.ds(pl.multiple_of(far, half), half), :] = far_lo[...]
    rows_in[pl.ds(pl.multiple_of(far + half, half), half), :] = far_hi[...]
    head_of = lax.broadcasted_iota(jnp.int32, (rows, width), 1) // HEAD_DIM
    lane = lax.broadcasted_iota(jnp.int32, (rows, LANES), 1)
    for i in range(SIDE):
        here = slice(i * rows, (i + 1) * rows)
        extent = (i + 1) * rows
        x = rows_in[here, :].astype(f32)
        scale = lax.rsqrt(jnp.mean(x * x, axis=1, keepdims=True) + eps_norm)
        low = (x * scale * gain[...]).astype(bf16)
        normed[here, :] = low
        raw = dot(low, weights[...])
        q = rope(raw[:, :width], cosine[here, :], sine[here, :]).astype(bf16)
        q = q * jnp.asarray(HEAD_DIM**-0.5, bf16)
        query[here, :] = q
        key[here, :] = rope(raw[:, width : 2 * width], cosine[here, :], sine[here, :]).astype(bf16)
        value[here, :] = raw[:, 2 * width :].astype(bf16)
        column = lax.broadcasted_iota(jnp.int32, (rows, extent), 1)
        row = i * rows + lax.broadcasted_iota(jnp.int32, (rows, extent), 0)
        bias = jnp.where((column >= starts[here, :]) & (column <= row), 0.0, mask_fill)
        total = jnp.zeros((rows, width), f32)
        logs = jnp.zeros((rows, LANES), f32)
        for h in range(width // HEAD_DIM):
            q_h = jnp.where(head_of == h, q, jnp.zeros_like(q))
            scores = dot_rows(q_h, key[:extent, :]) + bias
            peak = jnp.max(scores, axis=1, keepdims=True)
            lifted = jnp.exp(scores - peak)
            summed = jnp.sum(lifted, axis=1, keepdims=True)
            probs = (lifted * (1.0 / summed)).astype(bf16)
            total = jnp.where(head_of == h, dot(probs, value[:extent, :]), total)
            logs = jnp.where(lane == h, peak + jnp.log(summed), logs)
        mixed[here, :] = total.astype(bf16)
        log_total[here, :] = logs
        for n in range(len(kept)):
            keep(i, n).start()
    for d, out in enumerate((mixed_0, mixed_1, mixed_2, mixed_3)):
        out[...] = mixed[place(at, d, rows), :]
    for i in range(SIDE):
        for n in range(len(kept)):
            keep(i, n).wait()


def attend_back_kernel(
    at, part_0, part_1, part_2a, part_2b, part_3, w_output, query, key, value, mixed, log_total, starts, cosine, sine,
    grads, out_0, out_1, out_2, out_3, grad_in, grad_query,
):
    rows, width = out_0.shape[0], query.shape[1]
    length = rows * SIDE
    heads = width // HEAD_DIM
    for d, part in ((0, part_0), (1, part_1), (3, part_3)):
        grad_in[place(at, d, rows), :] = dot_rows(part[:rows, :], w_output[...]).astype(bf16)
    cut = part_2a.shape[0]
    far = (at[3] + 2) % SIDE * rows
    low = pl.ds(pl.multiple_of(far, 16), cut)
    grad_in[low, :] = dot_rows(part_2a[...], w_output[...]).astype(bf16)
    high = pl.ds(pl.multiple_of(far + cut, 16), rows - cut)
    grad_in[high, :] = dot_rows(part_2b[: rows - cut, :], w_output[...]).astype(bf16)
    both = grad_in[...].astype(f32) * mixed[...].astype(f32)
    both_hi = both.astype(bf16)
    both_lo = (both - both_hi.astype(f32)).astype(bf16)
    marks = lax.broadcasted_iota(jnp.int32, (8, width), 1) // HEAD_DIM
    marks = (marks == lax.broadcasted_iota(jnp.int32, (8, width), 0)).astype(bf16)
    inner = dot_rows(marks, both_hi) + dot_rows(marks, both_lo)
    logs = jnp.transpose(log_total[...])
    head_of = lax.broadcasted_iota(jnp.int32, (rows, width), 1) // HEAD_DIM
    lane = lax.broadcasted_iota(jnp.int32, (rows, LANES), 1)
    for j in range(SIDE):
        here = slice(j * rows, (j + 1) * rows)
        first = j * rows
        extent = length - first
        key_at = first + lax.broadcasted_iota(jnp.int32, (rows, extent), 0)
        query_at = first + lax.broadcasted_iota(jnp.int32, (rows, extent), 1)
        allowed = (key_at >= starts[:, first:]) & (key_at <= query_at)
        bias = jnp.where(allowed, 0.0, mask_fill)
        k_here, v_here = key[here, :], value[here, :]
        q_there, g_there = query[first:, :], grad_in[first:, :]
        grad_k = jnp.zeros((rows, width), f32)
        grad_v = jnp.zeros((rows, width), f32)
        grad_q = None
        for h in range(heads):
            mine = head_of == h
            k_h = jnp.where(mine, k_here, jnp.zeros_like(k_here))
            v_h = jnp.where(mine, v_here, jnp.zeros_like(v_here))
            probs = jnp.exp(dot_rows(k_h, q_there) + bias - logs[h : h + 1, first:])
            slopes = probs * (dot_rows(v_h, g_there) - inner[h : h + 1, first:])
            probs_low, slopes_low = probs.astype(bf16), slopes.astype(bf16)
            grad_v = jnp.where(mine, dot(probs_low, g_there), grad_v)
            grad_k = jnp.where(mine, dot(slopes_low, q_there), grad_k)
            term = dot_cols(slopes_low, k_h)
            grad_q = term if grad_q is None else grad_q + term
        if j == 0:
            grad_query[...] = grad_q
        else:
            grad_query[first:, :] = grad_query[first:, :] + grad_q
        compact = []
        for values, turn in ((grad_k, True), (grad_v, False)):
            halves = []
            for lane_at in (0, LANES):
                part = values[:, lane_at : lane_at + LANES]
                part = part + pltpu.roll(part, HEAD_DIM, 1)
                halves.append(rope(part, cosine[here, :], -sine[here, :]) if turn else part)
            compact.append(jnp.where(lane < HEAD_DIM, halves[0], halves[1]).astype(bf16))
        grads[here, width : width + LANES] = compact[0]
        grads[here, width + LANES :] = compact[1]
        turned_q = rope(grad_query[here, :], cosine[here, :], -sine[here, :])
        grads[here, :width] = (turned_q * HEAD_DIM**-0.5).astype(bf16)
    for d, out in enumerate((out_0, out_1, out_2, out_3)):
        out[...] = grads[place(at, d, rows), :]


def join_kernel(
    at, mixed_0, mixed_1, mixed_2, mixed_3, weights, tokens, gain, hidden_out, inputs_out,
):
    hidden = tokens[...].astype(f32)
    for d, part in enumerate((mixed_0, mixed_1, mixed_2, mixed_3)):
        hidden = hidden + dot(part[...], weights[(at[3] + d) % SIDE])
    scale = lax.rsqrt(jnp.mean(hidden * hidden, axis=1, keepdims=True) + eps_norm)
    hidden_out[...] = hidden
    inputs_out[...] = (hidden * scale * gain[...]).astype(bf16)


def expert_kernel(capacity, distance, at, x_a, x_b, g_all, router, *refs):
    own, sib = refs[:3], refs[3:6]
    (grad_lo, grad_hi, share_out, mix_all, rows_out, grads_out, active_out, slopes_out,
     x_blocks, g_blocks, w_gate, w_up, w_down, share, slots, gate_rows, g_rows, marks, grad_slots, mix_slots,
     grad_blocks, mix_blocks, x_sem, g_sem, w_sem, mix_sem, grad_sem) = refs[6 if distance == 0 else 7 :]
    step = pl.program_id(0)
    rows = x_a.shape[0]
    picks = 8
    experts = share_out.shape[0]
    taken = g_blocks.shape[1]
    z, x, core = at[0], at[1], at[2]
    me = (z * SIDE + x) * 2 + core
    ids = (me, me + 1 - 2 * core)
    first_core = core == 0
    u, w = jnp.where(first_core, z, x), jnp.where(first_core, x, z)
    x_from = (x_a, *[x_b.at[pl.ds(b * rows, rows), :] for b in range(SIDE - 1)])

    def source(b):
        there, away = (u + b) % SIDE, (w + distance) % SIDE
        return jnp.where(first_core, there * SIDE + away, away * SIDE + there)

    def x_copy(b):
        return pltpu.make_async_copy(x_from[b], x_blocks.at[b], x_sem.at[b])

    def g_copy(b):
        there = pl.ds(pl.multiple_of(source(b) * taken, taken), taken)
        return pltpu.make_async_copy(g_all.at[there, :], g_blocks.at[b], g_sem.at[b])

    def w_copy(e, n):
        there = (w_gate, w_up, w_down)[n].at[e]
        return pltpu.make_async_copy((own, sib)[e][n].at[0], there, w_sem.at[e, n])

    def mix_copy(b):
        there = pl.ds(pl.multiple_of(source(b) * rows, rows), rows)
        return pltpu.make_async_copy(mix_blocks.at[b], mix_all.at[there, :], mix_sem.at[b])

    def grad_copy(b):
        out = grad_lo if b < SIDE // 2 else grad_hi
        there = pl.ds(b % (SIDE // 2) * taken, taken)
        return pltpu.make_async_copy(grad_blocks.at[b], out.at[there, :], grad_sem.at[b])

    @pl.when(step == 0)
    def _():
        for b in range(SIDE):
            x_copy(b).start()
            g_copy(b).start()
        for e in range(2):
            for n in range(3):
                w_copy(e, n).start()
        gate_rows[...] = jnp.zeros_like(gate_rows)
        expert = lax.broadcasted_iota(jnp.int32, (experts, rows), 0)
        token = lax.broadcasted_iota(jnp.int32, (rows, rows), 0)
        earlier = token < lax.broadcasted_iota(jnp.int32, (rows, rows), 1)
        earlier = earlier.astype(f32).astype(bf16)
        for b in range(SIDE):
            here = slice(b * rows, (b + 1) * rows)
            x_copy(b).wait()
            g_copy(b).wait()
            named = g_blocks[b, rows : rows + picks, :rows].astype(f32).astype(jnp.int32)
            used = jnp.zeros((experts, rows), f32)
            for p in range(picks):
                used = jnp.where(named[p : p + 1, :] == expert, 1.0, used)
            rank = jnp.where(used > 0, dot(used.astype(bf16), earlier), -1.0)
            logits = jnp.transpose(dot(x_blocks[b], router[...]))[:experts, :]
            peak = jnp.max(jnp.where(used > 0, logits, mask_fill), axis=0, keepdims=True)
            raised = jnp.where(used > 0, jnp.exp(jnp.minimum(logits - peak, 0.0)), 0.0)
            ratio = raised / jnp.sum(raised, axis=0, keepdims=True)
            if b == 0:
                share_out[...] = ratio
            for e in range(2):
                mine = expert == ids[e]
                share[e : e + 1, here] = jnp.sum(jnp.where(mine, ratio, 0.0), axis=0, keepdims=True)
                slots[e : e + 1, here] = jnp.sum(jnp.where(mine, rank, 0.0), axis=0, keepdims=True)
        for n in range(3):
            w_copy(0, n).wait()

    @pl.when(step == 1)
    def _():
        for n in range(3):
            w_copy(1, n).wait()

    slot_index = lax.broadcasted_iota(jnp.int32, (capacity, rows), 0).astype(f32)
    shares, slots_here = share[pl.ds(step, 1), :], slots[pl.ds(step, 1), :]
    target = pl.ds(pl.multiple_of(step * capacity, capacity), capacity)
    expert_row = lax.broadcasted_iota(jnp.int32, (experts, rows), 0)
    expert_row = expert_row == jnp.where(step == 0, ids[0], ids[1])
    gates, masks = [], []
    for b in range(SIDE):
        here = slice(b * rows, (b + 1) * rows)
        there = slice(b * capacity, (b + 1) * capacity)
        mask = slot_index == slots_here[:, here]
        masks.append(mask)
        mark = mask.astype(f32).astype(bf16)
        marks[b, target, :] = mark
        rows_out[0, there, :] = dot(mark, x_blocks[b]).astype(bf16)
        g_rows[there, :] = dot(mark, g_blocks[b, :rows, :]).astype(bf16)
        gates.append(jnp.sum(jnp.where(mask, shares[:, here], 0.0), axis=1, keepdims=True))
    gate = jnp.concatenate(gates, axis=0)
    x = rows_out[0]
    gate_pre = dot(x, w_gate[step])
    up_pre = dot(x, w_up[step])
    sigmoid = 1.0 / (1.0 + jnp.exp(-gate_pre))
    silu = gate_pre * sigmoid
    active = (silu * up_pre).astype(bf16)
    active_out[0] = active
    produced = dot(active, w_down[step]).astype(bf16).astype(f32)
    wide_g = g_rows[...].astype(f32)
    products = jnp.sum(wide_g * produced, axis=1, keepdims=True)
    grad_produced = (gate * wide_g).astype(bf16)
    grads_out[0] = grad_produced
    mix = (gate * produced).astype(bf16)
    grad_active = dot_rows(grad_produced, w_down[step])
    grad_up = (grad_active * silu).astype(bf16)
    slope = sigmoid * (1.0 + gate_pre * (1.0 - sigmoid))
    grad_gate = (grad_active * up_pre * slope).astype(bf16)
    width = grad_gate.shape[1]
    slopes_out[0, :, :width] = grad_gate
    slopes_out[0, :, width:] = grad_up
    grad_x = (dot_rows(grad_gate, w_gate[step]) + dot_rows(grad_up, w_up[step])).astype(bf16)
    for b in range(SIDE):
        there = slice(b * capacity, (b + 1) * capacity)
        grad_slots[b, target, :] = grad_x[there, :]
        mix_slots[b, target, :] = mix[there, :]
        row = jnp.sum(jnp.where(masks[b], products[there, :], 0.0), axis=0, keepdims=True)
        gate_rows[b] = jnp.where(expert_row, row, gate_rows[b])

    @pl.when(step == 1)
    def _():
        for b in range(SIDE):
            grad_blocks[b, :rows, :] = dot_cols(marks[b], grad_slots[b]).astype(bf16)
            full = gate_rows[b]
            high = full.astype(bf16)
            low = (full - high.astype(f32)).astype(bf16)
            parts = [part[i : i + 16, :] for part in (high, low) for i in range(0, experts, 16)]
            tail = jnp.concatenate(parts, axis=1)
            grad_blocks[b, rows:, : tail.shape[1]] = tail
            if tail.shape[1] < grad_blocks.shape[2]:
                grad_blocks[b, rows:, tail.shape[1] :] = jnp.zeros_like(
                    grad_blocks[b, rows:, tail.shape[1] :]
                )
            grad_copy(b).start()
            mix_blocks[b] = dot_cols(marks[b], mix_slots[b]).astype(bf16)
            mix_copy(b).start()
        for b in range(SIDE):
            grad_copy(b).wait()
            mix_copy(b).wait()


def expert_weights_kernel(*refs):
    out = refs[-1]
    groups = [refs[4 * i : 4 * i + 4] for i in range(SIDE)]
    for name in range(2):
        total = None
        for rows_in, grads, active, slopes in groups:
            term = dot_cols(rows_in[0], slopes[0]) if name == 0 else dot_cols(active[0], grads[0])
            total = term if total is None else total + term
        at = 0 if name == 0 else out.shape[1]
        out[at : at + total.shape[0], :] = total.astype(bf16)


def fold_kernel(own_lo, own_hi, before_lo, before_hi, after_lo, after_hi, *outs):
    rows = outs[0].shape[0]
    for i, out in enumerate(outs):
        part = slice(i % 2 * rows, (i % 2 + 1) * rows)
        refs = (own_lo, before_lo, after_lo) if i < 2 else (own_hi, before_hi, after_hi)
        out[...] = sum(ref[part, :].astype(f32) for ref in refs).astype(bf16)


def turn_kernel(
    term_0, term_1, term_2, term_3, shares, router, inputs, hidden_in, gain, cotangent, grad_hidden_out, out,
):
    experts, rows = shares.shape
    total = sum(ref[...].astype(f32) for ref in (term_0, term_1, term_2, term_3))
    tail = [total[rows:, i * rows : (i + 1) * rows] for i in range(experts // 8)]
    count = len(tail) // 2
    grad_share = jnp.concatenate([tail[i] + tail[i + count] for i in range(count)], axis=0)
    share = shares[...]
    grad_logits = share * (grad_share - jnp.sum(share * grad_share, axis=0, keepdims=True))
    grad_logits = grad_logits.astype(bf16)
    out[rows : rows + experts, :] = dot(grad_logits, inputs[...]).astype(bf16)
    grad = total[:rows, :] + dot_cols(grad_logits, router[...])
    hidden = hidden_in[...]
    scale = lax.rsqrt(jnp.mean(hidden * hidden, axis=1, keepdims=True) + eps_norm)
    gain_row = jnp.sum(grad * hidden * scale, axis=0, keepdims=True)
    row = lax.broadcasted_iota(jnp.int32, (16, grad.shape[1]), 0)
    out[rows + experts :, :] = jnp.where(row == 0, gain_row, 0.0).astype(bf16)
    grad = grad * gain[...]
    inner = jnp.mean(grad * hidden, axis=1, keepdims=True)
    grad = cotangent[...].astype(f32) + scale * grad - hidden * (scale * scale * scale * inner)
    grad_hidden_out[...] = grad
    out[:rows, :] = grad.astype(bf16)


def finish_kernel(at, g_0, g_1, g_2, g_3, weights, tokens, gain, grad_hidden, out):
    grad = dot_rows(g_0[...], weights[at[3]])
    for d, part in ((1, g_1), (2, g_2), (3, g_3)):
        grad = grad + dot_rows(part[...], weights[(at[3] + d) % SIDE])
    grad = grad * gain[...]
    x = tokens[...].astype(f32)
    scale = lax.rsqrt(jnp.mean(x * x, axis=1, keepdims=True) + eps_norm)
    inner = jnp.mean(grad * x, axis=1, keepdims=True)
    out[...] = grad_hidden[...] + scale * grad - x * (scale * scale * scale * inner)


def pack_kernel(
    at, normed, grads, mixed, part_0, part_1, part_2a, part_2b, part_3, w_own, gain, out, smalls,
):
    count, _, half = out.shape
    rows = mixed.shape[0] // SIDE
    cut = part_2a.shape[0]
    inner = dot_cols(normed[...], grads[...])
    outer = jnp.zeros((mixed.shape[1], normed.shape[1]), f32)
    for d, part in ((0, part_0), (1, part_1), (3, part_3)):
        outer = outer + dot_cols(mixed[place(at, d, rows), :], part[:rows, :])
        smalls[(at[3] + d) % SIDE] = part[rows:, :].astype(f32)
    far = (at[3] + 2) % SIDE * rows
    low = pl.ds(pl.multiple_of(far, 16), cut)
    outer = outer + dot_cols(mixed[low, :], part_2a[...])
    high = pl.ds(pl.multiple_of(far + cut, 16), rows - cut)
    outer = outer + dot_cols(mixed[high, :], part_2b[: rows - cut, :])
    smalls[(at[3] + 2) % SIDE] = part_2b[rows - cut :, :].astype(f32)
    small = smalls[0] + smalls[1] + smalls[2] + smalls[3]
    along = inner * w_own[...].astype(f32)
    along_hi = along.astype(bf16)
    along_lo = (along - along_hi.astype(f32)).astype(bf16)
    ones = jnp.ones((8, along.shape[1]), bf16)
    gain_1 = (dot_rows(ones, along_hi) + dot_rows(ones, along_lo)) / gain[...]
    gain_1, gain_2 = gain_1[0:1, :], small[count : count + 1, :]
    row = lax.broadcasted_iota(jnp.int32, (16, half), 0)
    gains = jnp.zeros((16, half), f32)
    for i, part in enumerate((gain_2[:, :half], gain_2[:, half:], gain_1[:, :half], gain_1[:, half:])):
        gains = jnp.where(row == 2 + i, part, gains)
    inner, outer = inner.astype(bf16), outer.astype(bf16)
    tall, short = inner.shape[0] // count, outer.shape[0] // count
    for c in range(count):
        out[c, :tall, :] = inner[c * tall : (c + 1) * tall, :]
        part = outer[c * short : (c + 1) * short, :].astype(f32)
        part = jnp.concatenate([part[:, :half], part[:, half:]], axis=0)
        out[c, tall : tall + 2 * short, :] = part.astype(bf16)
        last = jnp.where(row == 0, small[c : c + 1, :half], gains)
        last = jnp.where(row == 1, small[c : c + 1, half:], last)
        out[c, tall + 2 * short :, :] = last.astype(bf16)


def share_kernel(parts, out, last):
    total = parts[0].astype(f32)
    for i in range(1, parts.shape[0]):
        total = total + parts[i].astype(f32)
    last[...] = total[-16:, :]
    low = total.astype(bf16)
    for i in range(out.shape[0]):
        out[i] = low


def unpack_kernel(
    at, parts, last_0, last_1, last_2, last_3, query_out, key_out, value_out, output_out, router_out, gain_1_out, gain_2_out, lasts,
):
    count, size, half = parts.shape
    tall = query_out.shape[0] // count
    short = output_out.shape[0] // count
    width = query_out.shape[1]
    rows = []
    for c in range(count):
        here = slice(c * tall, (c + 1) * tall)
        part = parts[c].astype(f32)
        query_out[here, :] = part[:tall, :width]
        key_out[here, :] = part[:tall, width : width + key_out.shape[1]]
        value_out[here, :] = part[:tall, width + key_out.shape[1] :]
        here = slice(c * short, (c + 1) * short)
        output_out[here, :half] = part[tall : tall + short, :]
        output_out[here, half:] = part[tall + short : tall + 2 * short, :]
        last = part[tall + 2 * short :, :]
        rows.append(jnp.concatenate([last[0:1, :], last[1:2, :]], axis=1))
    router_out[...] = jnp.concatenate(rows, axis=0)
    for d, part in enumerate((last_0, last_1, last_2, last_3)):
        lasts[(at[3] + d) % SIDE] = part[...]
    total = lasts[0] + lasts[1] + lasts[2] + lasts[3]
    gain_1_out[:, :half] = total[4:5, :]
    gain_1_out[:, half:] = total[5:6, :]
    gain_2_out[:, :half] = last_0[2:3, :]
    gain_2_out[:, half:] = last_0[3:4, :]


def quarters_kernel(at, own, sib, *refs):
    outs, total = refs[:-1], refs[-1]
    total[...] = (own[...].astype(f32) + sib[...].astype(f32)).astype(bf16)
    rows = outs[0].shape[0]
    for i, out in enumerate(outs):
        start = (at[3] + i // 2) % SIDE * (2 * rows) + i % 2 * rows
        out[...] = total[pl.ds(pl.multiple_of(start, rows), rows), :]


def owned_kernel(own_lo, own_hi, before_lo, before_hi, after_lo, after_hi, out):
    rows = own_lo.shape[0]
    out[:rows, :] = sum(ref[...].astype(f32) for ref in (own_lo, before_lo, after_lo)).astype(bf16)
    out[rows:, :] = sum(ref[...].astype(f32) for ref in (own_hi, before_hi, after_hi)).astype(bf16)


def expert_unpack_kernel(at, own, from_after, far_lo, far_hi, from_before, gate_out, up_out, down_out, whole):
    rows = own.shape[0]
    half = far_lo.shape[0]
    whole[place(at, 0, rows), :] = own[...]
    whole[place(at, 1, rows), :] = from_after[...]
    whole[place(at, 3, rows), :] = from_before[...]
    far = (at[3] + 2) % SIDE * rows
    whole[pl.ds(pl.multiple_of(far, half), half), :] = far_lo[...]
    whole[pl.ds(pl.multiple_of(far + half, half), half), :] = far_hi[...]
    depth, width = gate_out.shape[1:]
    gate_out[0] = whole[:depth, :width].astype(f32)
    up_out[0] = whole[:depth, width:].astype(f32)
    down_out[0] = whole[depth:, :].astype(f32)


def body(
    tokens,
    cotangent,
    routes,
    lengths,
    gain_attn,
    w_query,
    w_key,
    w_value,
    w_output,
    gain_mix,
    w_router,
    gate_weight,
    up_weight,
    down_weight,
):
    rows, depth = tokens.shape
    picks = routes.shape[1]
    experts = lax.axis_size(PLANE)
    length = rows * SIDE
    width = w_query.shape[1]
    hidden_units = gate_weight.shape[2]
    capacity = min(rows, 3 * rows * picks // (2 * experts))
    core, y = lax.axis_index("core"), lax.axis_index("head")
    z, x = lax.axis_index("z"), lax.axis_index("x")
    at = jnp.stack([z, x, core, y]).astype(jnp.int32)
    gain_1, gain_2 = gain_attn[None, :], gain_mix[None, :]
    smem = pl.BlockSpec(memory_space=pltpu.SMEM)
    vmem = pl.BlockSpec(memory_space=pltpu.VMEM)
    anywhere = pl.BlockSpec(memory_space=pl.ANY)
    hbm = pl.BlockSpec(memory_space=pltpu.HBM)

    ends = jnp.cumsum(lengths[0], dtype=jnp.int32)
    index = jnp.arange(length, dtype=jnp.int32)
    starts = jnp.max(jnp.where(index[:, None] >= ends[None, :], ends[None, :], 0), axis=1)
    lane = jnp.arange(LANES)
    frequency = rope_base ** (-2.0 * (lane % (HEAD_DIM // 2)).astype(f32) / HEAD_DIM)
    angles = (index - starts).astype(f32)[:, None] * frequency[None, :]
    cosine = jnp.cos(angles)
    sine = jnp.sin(angles) * jnp.where(lane % HEAD_DIM < HEAD_DIM // 2, -1.0, 1.0)[None, :]

    def doubled(columns):
        heads = [columns[:, i : i + HEAD_DIM] for i in range(0, columns.shape[1], HEAD_DIM)]
        return jnp.concatenate([head for one in heads for head in (one, one)], axis=1)

    w_all = jnp.concatenate([w_query, doubled(w_key), doubled(w_value)], axis=1)
    w_own = jnp.concatenate([w_query, w_key, w_value], axis=1)
    router_rows = w_router.T.astype(bf16)
    router_wide = jnp.pad(w_router, ((0, 0), (0, LANES - experts))).astype(bf16)
    own_weights = [gate_weight, up_weight, down_weight]
    sib_weights = [swap_core(a) for a in own_weights]
    made = (w_all, cosine, sine, starts, w_own, router_rows, router_wide, *sib_weights)
    token_parts = ring_gather(tokens, line_shift, *made)
    named = jnp.pad(routes.T.astype(bf16), ((0, 16 - picks), (0, depth - rows)))
    grad_plane = lax.all_gather(
        jnp.concatenate([cotangent, named], axis=0), CHIPS, axis=0, tiled=True
    )
    output_all = all_blocks(after(w_output, *token_parts[2:4]), "head")

    normed, query, key, value, mixed, log_total, *mixed_out = call(
        attend_kernel,
        [
            array((length, depth), bf16),
            *[array((length, width), bf16)] * 4,
            array((length, LANES), f32),
            *[array((rows, width), bf16)] * SIDE,
        ],
        [at, *token_parts, gain_1, w_all, cosine, sine, starts[:, None]],
        specs=[smem] + [vmem] * 10,
        out_specs=[hbm] * 6 + [vmem] * 4,
        scratch=[
            *[pltpu.VMEM((length, depth), bf16)] * 2,
            *[pltpu.VMEM((length, width), bf16)] * 4,
            pltpu.VMEM((length, LANES), f32),
            pltpu.SemaphoreType.DMA((SIDE, 6)),
        ],
        flops=12 * 10**9,
    )
    mixed_in = direct_swap(mixed_out, line_shift)
    hidden, inputs = call(
        join_kernel,
        [array((rows, depth), f32), array((rows, depth), bf16)],
        [at, *mixed_in, output_all, tokens, gain_2],
        specs=[smem] + [vmem] * 7,
        flops=3 * 10**9,
    )

    u_rest = [shift_u(inputs, -1), shift_u(inputs, 2), shift_u(inputs, 1)]
    before_own, after_own = shift_w(inputs, 1), shift_w(inputs, -1)
    u_rest = jnp.concatenate(u_rest, axis=0)
    before_rest, after_rest = shift_w(u_rest, 1), shift_w(u_rest, -1)
    slots = SIDE * capacity
    half = array((length // 2 + 32, depth), bf16)

    def experts_on(distance, x_parts, mix_in):
        outs = [
            half,
            half,
            array((experts, rows), f32),
            array((SIDE * length, depth), bf16),
            array((2, slots, depth), bf16),
            array((2, slots, depth), bf16),
            array((2, slots, hidden_units), bf16),
            array((2, slots, 2 * hidden_units), bf16),
        ]
        args = [at, *x_parts, grad_plane, router_wide, *own_weights, *sib_weights]

        def fixed(a):
            return pl.BlockSpec(a.shape, lambda e: (0,) * len(a.shape))

        def by_expert(a):
            return pl.BlockSpec((1, *a.shape[1:]), lambda e: (e, 0, 0))

        specs = [smem, *[anywhere] * 3, fixed(router_wide), *[anywhere] * 6]
        aliases = {}
        if mix_in is not None:
            aliases = {len(args): 3}
            args.append(mix_in)
            specs.append(anywhere)
        return call(
            functools.partial(expert_kernel, capacity, distance),
            outs,
            args,
            specs=specs,
            grid=(2,),
            out_specs=[hbm, hbm, fixed(outs[2]), hbm, *map(by_expert, outs[4:])],
            scratch=[
                pltpu.VMEM((SIDE, rows, depth), bf16),
                pltpu.VMEM((SIDE, rows + 16, depth), bf16),
                pltpu.VMEM((2, depth, hidden_units), bf16),
                pltpu.VMEM((2, depth, hidden_units), bf16),
                pltpu.VMEM((2, hidden_units, depth), bf16),
                pltpu.VMEM((8, length), f32),
                pltpu.VMEM((8, length), f32),
                pltpu.VMEM((SIDE, experts, rows), f32),
                pltpu.VMEM((slots, depth), bf16),
                pltpu.VMEM((SIDE, 2 * capacity, rows), bf16),
                pltpu.VMEM((SIDE, 2 * capacity, depth), bf16),
                pltpu.VMEM((SIDE, 2 * capacity, depth), bf16),
                pltpu.VMEM((SIDE, rows + 16, depth), bf16),
                pltpu.VMEM((SIDE, rows, depth), bf16),
                pltpu.SemaphoreType.DMA((SIDE,)),
                pltpu.SemaphoreType.DMA((SIDE,)),
                pltpu.SemaphoreType.DMA((2, 3)),
                pltpu.SemaphoreType.DMA((SIDE,)),
                pltpu.SemaphoreType.DMA((SIDE,)),
            ],
            flops=18 * 10**9,
            aliases=aliases,
        )

    column = experts_on(0, [inputs, u_rest], None)
    far_own = shift_w(after(before_own, column[2]), 1)
    far_rest = shift_w(after(after_rest, column[2]), -1)
    right = experts_on(1, [after_own, after_rest], column[3])
    far = experts_on(2, [far_own, far_rest], right[3])
    left = experts_on(3, [before_own, before_rest], far[3])
    results = [column, right, far, left]
    mix_all = left[3]

    weight_rows = depth + hidden_units
    flat = [a for r in results for a in r[4:]]

    def expert_weights(e, earlier):
        return call(
            expert_weights_kernel,
            [array((weight_rows, depth), bf16)],
            [after(flat[0], earlier), *flat[1:]],
            specs=[pl.BlockSpec((1, *a.shape[1:]), lambda i: (e, 0, 0)) for a in flat],
            grid=(1,),
            out_specs=[pl.BlockSpec((weight_rows, depth), lambda i: (0, 0))],
            flops=10 * 10**9,
        )[0]

    sib_grads = expert_weights(1, mix_all)
    own_grads = expert_weights(0, sib_grads)
    from_before, from_after = ring_sum([(r[0], r[1]) for r in results], shift_w)
    folded = call(
        fold_kernel,
        [array((rows + 16, depth), bf16)] * SIDE,
        [after(column[0], own_grads), column[1], *from_before, *from_after],
        flops=2 * 10**9,
    )
    grad_terms = direct_swap(folded, shift_u)

    grad_hidden, grad_low = call(
        turn_kernel,
        [array((rows, depth), f32), array((rows + experts + 16, depth), bf16)],
        [*grad_terms, column[2], router_rows, inputs, hidden, gain_2, cotangent],
        flops=4 * 10**9,
    )
    grad_parts = ring_gather(grad_low, line_shift)
    sib_sums = swap_core(sib_grads)
    grads, *grads_out = call(
        attend_back_kernel,
        [array((length, 2 * width), bf16), *[array((rows, 2 * width), bf16)] * SIDE],
        [
            after(at, sib_sums),
            *grad_parts,
            w_output,
            query,
            key,
            value,
            mixed,
            log_total,
            starts[None, :],
            cosine,
            sine,
        ],
        specs=[smem] + [vmem] * 14,
        scratch=[pltpu.VMEM((length, width), bf16), pltpu.VMEM((length, width), f32)],
        flops=12 * 10**9,
    )
    grads_in = direct_swap(grads_out, line_shift)
    w_parts = lax.all_gather(after(w_own, inputs), "head", axis=0)

    tall, short = depth // experts, width // experts
    size = tall + 2 * short + 16
    packed = call(
        pack_kernel,
        [array((experts, size, depth // 2), bf16)],
        [at, normed, grads, mixed, *grad_parts, w_own, gain_1],
        specs=[smem] + [vmem] * 10,
        scratch=[pltpu.VMEM((SIDE, experts + 16, depth), f32)],
        flops=8 * 10**9,
    )[0]
    packed = after(packed, *grads_in)
    grad_tokens = call(
        finish_kernel,
        [array((rows, depth), f32)],
        [after(at, packed), *grads_in, w_parts, tokens, gain_1, grad_hidden],
        specs=[smem] + [vmem] * 8,
        flops=4 * 10**9,
    )[0]
    eighth = weight_rows // (2 * SIDE)
    quarters = call(
        quarters_kernel,
        [array((eighth, depth), bf16)] * (2 * SIDE),
        [after(at, grad_tokens), own_grads, sib_sums],
        specs=[smem] + [vmem] * 2,
        scratch=[pltpu.VMEM((weight_rows, depth), bf16)],
        flops=3 * 10**9,
    )
    pairs = [(quarters[2 * d], quarters[2 * d + 1]) for d in range(SIDE)]
    from_before, from_after = ring_sum(pairs, line_shift)
    shared, last = call(
        share_kernel,
        [array(packed.shape, bf16), array((16, depth // 2), f32)],
        [after(swap_all(packed, PLANE), *from_before, *from_after)],
        flops=2 * 10**9,
    )
    lasts = [last, line_shift(last, -1), line_shift(last, 2), line_shift(last, 1)]
    expert_owned = call(
        owned_kernel,
        [array((2 * eighth, depth), bf16)],
        [*pairs[0], *from_before, *from_after],
        flops=10**9,
    )[0]
    expert_parts = ring_gather(expert_owned, line_shift)
    expert_totals = call(
        expert_unpack_kernel,
        [
            array((1, depth, hidden_units), f32),
            array((1, depth, hidden_units), f32),
            array((1, hidden_units, depth), f32),
        ],
        [at, *expert_parts],
        specs=[smem] + [vmem] * 5,
        scratch=[pltpu.VMEM((weight_rows, depth), bf16)],
        flops=4 * 10**9,
    )
    gathered = after(swap_all(shared, PLANE), *lasts, *expert_totals)
    grad_query, grad_key, grad_value, grad_output, grad_router, grad_gain_1, grad_gain_2 = call(
        unpack_kernel,
        [
            array((depth, width), f32),
            array((depth, LANES), f32),
            array((depth, LANES), f32),
            array((width, depth), f32),
            array((experts, depth), f32),
            array((1, depth), f32),
            array((1, depth), f32),
        ],
        [at, gathered, *lasts],
        specs=[smem] + [vmem] * 5,
        scratch=[pltpu.VMEM((SIDE, 16, depth // 2), f32)],
        flops=4 * 10**9,
    )

    mixture = lax.psum_scatter(after(mix_all, *folded), CHIPS, scatter_dimension=0, tiled=True)
    output = (hidden + mixture.astype(f32)).astype(bf16)

    return (
        output,
        grad_tokens,
        grad_gain_1[0],
        grad_query,
        grad_key,
        grad_value,
        grad_output,
        grad_gain_2[0],
        grad_router.T,
        *expert_totals,
    )


def solution(mesh):
    axes = (*PLANE, "head")
    mesh = jax.sharding.Mesh(mesh.devices.reshape(SIDE, SIDE, 2, SIDE), axes)
    rows = P(axes, None)
    per_expert = P(PLANE, None, None)
    columns = P(None, "head")
    in_specs = (
        rows,
        rows,
        rows,
        P(PLANE, None),
        P(),
        columns,
        columns,
        columns,
        P("head", None),
        P(),
        P(),
        per_expert,
        per_expert,
        per_expert,
    )
    out_specs = (
        rows,
        rows,
        P(),
        columns,
        columns,
        columns,
        P("head", None),
        P(),
        P(),
        per_expert,
        per_expert,
        per_expert,
    )
    return jax.shard_map(body, mesh=mesh, in_specs=in_specs, out_specs=out_specs, check_vma=False)
```

```python
import functools

import jax
import jax.numpy as jnp
from jax import lax
from jax.experimental import pallas as pl
from jax.experimental.pallas import tpu as pltpu
from jax.sharding import PartitionSpec as P

HEAD_DIM = 64
SIDE = 4
LANES = 128
MIB = 1024 * 1024

eps_norm = 1e-06
rope_base = 10000.0
mask_fill = -1000000000.0

bf16 = jnp.bfloat16
f32 = jnp.float32


def dot(left, right):
    return lax.dot_general(left, right, (((1,), (0,)), ((), ())), preferred_element_type=f32)


def dot_rows(left, right):
    return lax.dot_general(left, right, (((1,), (1,)), ((), ())), preferred_element_type=f32)


def dot_cols(left, right):
    return lax.dot_general(left, right, (((0,), (0,)), ((), ())), preferred_element_type=f32)


def call(kernel, out_shapes, args, specs=None, out_specs=None, scratch=(), flops=0, vmem=60):
    moved = sum(a.size * a.dtype.itemsize for a in args)
    moved += sum(s.size * s.dtype.itemsize for s in out_shapes)
    whole = pl.BlockSpec(memory_space=pltpu.VMEM)
    return pl.pallas_call(
        kernel,
        out_shape=out_shapes,
        in_specs=specs or [whole] * len(args),
        out_specs=out_specs or [whole] * len(out_shapes),
        scratch_shapes=list(scratch),
        compiler_params=pltpu.CompilerParams(vmem_limit_bytes=vmem * MIB),
        cost_estimate=pl.CostEstimate(flops=flops, bytes_accessed=moved, transcendentals=0),
    )(*args)


def array(shape, dtype):
    return jax.ShapeDtypeStruct(shape, dtype)


CHIPS = ("z", "x")
PLANE = ("z", "x", "core")


def line_shift(values, step):
    pairs = [(i, (i + step) % SIDE) for i in range(SIDE)]
    return lax.ppermute(values, "head", pairs)


def plane_shift(first, values, step):
    pairs = []
    for i in range(2 * SIDE * SIDE):
        z, x, core = i // (2 * SIDE), i // 2 % SIDE, i % 2
        if (core == 0) == first:
            z = (z + step) % SIDE
        else:
            x = (x + step) % SIDE
        pairs.append((i, (z * SIDE + x) * 2 + core))
    return lax.ppermute(values, PLANE, pairs)


shift_u = functools.partial(plane_shift, True)
shift_w = functools.partial(plane_shift, False)


def swap_core(values):
    return lax.ppermute(values, "core", [(0, 1), (1, 0)])


def together(*values):
    return lax.optimization_barrier(values)


def ring_gather(block, shift, *between):
    half = block.shape[0] // 32 * 16
    from_before, from_after = shift(block, 1), shift(block, -1)
    from_before, from_after, *between = together(from_before, from_after, *between)
    far_lo, far_hi = shift(from_before[:half], 1), shift(from_after[half:], -1)
    parts = [block, from_after, far_lo, far_hi, from_before]
    return (parts, between) if between else parts


def direct_swap(parts, shift):
    return [parts[0], shift(parts[3], -1), shift(parts[2], 2), shift(parts[1], 1)]


def ring_sum(parts, shift):
    before_high, after_low = shift(parts[1][1], 1), shift(parts[3][0], -1)
    low_in, high_in = shift(parts[2][0], 1), shift(parts[2][1], -1)
    up = (parts[1][0].astype(f32) + low_in.astype(f32)).astype(bf16)
    down = (parts[3][1].astype(f32) + high_in.astype(f32)).astype(bf16)
    before_low, after_high = shift(up, 1), shift(down, -1)
    return (before_low, before_high), (after_low, after_high), (up, down)


def swap_all(values, axes):
    return lax.all_to_all(values, axes, 0, 0, tiled=True)


def all_blocks(block, axes):
    count = lax.axis_size(axes)
    return swap_all(jnp.broadcast_to(block[None], (count, *block.shape)), axes)


def rope(values, cosine, sine_signed):
    lane = lax.broadcasted_iota(jnp.int32, cosine.shape, 1)
    front = lane % HEAD_DIM < HEAD_DIM // 2
    out = []
    for at in range(0, values.shape[1], LANES):
        part = values[:, at : at + LANES]
        partner = jnp.where(
            front,
            pltpu.roll(part, LANES - HEAD_DIM // 2, 1),
            pltpu.roll(part, HEAD_DIM // 2, 1),
        )
        out.append(part * cosine + partner * sine_signed)
    return jnp.concatenate(out, axis=1)


def twice(values):
    lane = lax.broadcasted_iota(jnp.int32, values.shape, 1)
    swapped = pltpu.roll(values, HEAD_DIM, 1)
    first = lane < HEAD_DIM
    return jnp.concatenate(
        [jnp.where(first, values, swapped), jnp.where(first, swapped, values)], axis=1
    )


def place(at, distance, rows):
    return pl.ds(pl.multiple_of((at[3] + distance) % SIDE * rows, rows), rows)


def attend_kernel(
    at, own, from_after, far_lo, far_hi, from_before, gain, w_query, w_key, w_value, cosine, sine, starts,
    normed_out, query_out, key_out, value_out, mixed_out, log_out, mixed_0, mixed_1, mixed_2, mixed_3,
    rows_in, normed, query, key, value, mixed, log_total, sems,
):
    rows = own.shape[0]
    width = query.shape[1]
    kept = (normed, query, key, value, mixed, log_total)
    outs = (normed_out, query_out, key_out, value_out, mixed_out, log_out)

    def keep(i, n):
        here = pl.ds(i * rows, rows)
        return pltpu.make_async_copy(kept[n].at[here, :], outs[n].at[here, :], sems.at[i, n])

    rows_in[place(at, 0, rows), :] = own[...]
    rows_in[place(at, 1, rows), :] = from_after[...]
    rows_in[place(at, 3, rows), :] = from_before[...]
    half = rows // 2
    far = (at[3] + 2) % SIDE * rows
    rows_in[pl.ds(pl.multiple_of(far, half), half), :] = far_lo[...]
    rows_in[pl.ds(pl.multiple_of(far + half, half), half), :] = far_hi[...]
    head_of = lax.broadcasted_iota(jnp.int32, (rows, width), 1) // HEAD_DIM
    lane = lax.broadcasted_iota(jnp.int32, (rows, LANES), 1)
    for i in range(SIDE):
        here = slice(i * rows, (i + 1) * rows)
        extent = (i + 1) * rows
        x = rows_in[here, :].astype(f32)
        scale = lax.rsqrt(jnp.mean(x * x, axis=1, keepdims=True) + eps_norm)
        low = (x * scale * gain[...]).astype(bf16)
        normed[here, :] = low
        q = rope(dot(low, w_query[...]), cosine[here, :], sine[here, :]).astype(bf16)
        q = q * jnp.asarray(HEAD_DIM**-0.5, bf16)
        query[here, :] = q
        raw = rope(dot(low, w_key[...]), cosine[here, :], sine[here, :])
        key[here, :] = twice(raw).astype(bf16)
        value[here, :] = twice(dot(low, w_value[...])).astype(bf16)
        column = lax.broadcasted_iota(jnp.int32, (rows, extent), 1)
        row = i * rows + lax.broadcasted_iota(jnp.int32, (rows, extent), 0)
        bias = jnp.where((column >= starts[here, :]) & (column <= row), 0.0, mask_fill)
        total = jnp.zeros((rows, width), f32)
        logs = jnp.zeros((rows, LANES), f32)
        for h in range(width // HEAD_DIM):
            q_h = jnp.where(head_of == h, q, jnp.zeros_like(q))
            scores = dot_rows(q_h, key[:extent, :]) + bias
            peak = jnp.max(scores, axis=1, keepdims=True)
            lifted = jnp.exp(scores - peak)
            summed = jnp.sum(lifted, axis=1, keepdims=True)
            probs = (lifted * (1.0 / summed)).astype(bf16)
            total = jnp.where(head_of == h, dot(probs, value[:extent, :]), total)
            logs = jnp.where(lane == h, peak + jnp.log(summed), logs)
        mixed[here, :] = total.astype(bf16)
        log_total[here, :] = logs
        for n in range(len(kept)):
            keep(i, n).start()
    for d, out in enumerate((mixed_0, mixed_1, mixed_2, mixed_3)):
        out[...] = mixed[place(at, d, rows), :]
    for i in range(SIDE):
        for n in range(len(kept)):
            keep(i, n).wait()


def attend_back_kernel(
    at, part_0, part_1, part_2a, part_2b, part_3, w_output, query, key, value, mixed, log_total, starts, cosine, sine,
    grads, out_0, out_1, out_2, out_3, grad_in, grad_query,
):
    rows, width = out_0.shape[0], query.shape[1]
    length = rows * SIDE
    heads = width // HEAD_DIM
    for d, part in ((0, part_0), (1, part_1), (3, part_3)):
        grad_in[place(at, d, rows), :] = dot_rows(part[:rows, :], w_output[...]).astype(bf16)
    cut = part_2a.shape[0]
    far = (at[3] + 2) % SIDE * rows
    low = pl.ds(pl.multiple_of(far, 16), cut)
    grad_in[low, :] = dot_rows(part_2a[...], w_output[...]).astype(bf16)
    high = pl.ds(pl.multiple_of(far + cut, 16), rows - cut)
    grad_in[high, :] = dot_rows(part_2b[: rows - cut, :], w_output[...]).astype(bf16)
    both = grad_in[...].astype(f32) * mixed[...].astype(f32)
    both_hi = both.astype(bf16)
    both_lo = (both - both_hi.astype(f32)).astype(bf16)
    marks = lax.broadcasted_iota(jnp.int32, (8, width), 1) // HEAD_DIM
    marks = (marks == lax.broadcasted_iota(jnp.int32, (8, width), 0)).astype(bf16)
    inner = dot_rows(marks, both_hi) + dot_rows(marks, both_lo)
    logs = jnp.transpose(log_total[...])
    head_of = lax.broadcasted_iota(jnp.int32, (rows, width), 1) // HEAD_DIM
    lane = lax.broadcasted_iota(jnp.int32, (rows, LANES), 1)
    for j in range(SIDE):
        here = slice(j * rows, (j + 1) * rows)
        first = j * rows
        extent = length - first
        key_at = first + lax.broadcasted_iota(jnp.int32, (rows, extent), 0)
        query_at = first + lax.broadcasted_iota(jnp.int32, (rows, extent), 1)
        allowed = (key_at >= starts[:, first:]) & (key_at <= query_at)
        bias = jnp.where(allowed, 0.0, mask_fill)
        k_here, v_here = key[here, :], value[here, :]
        q_there, g_there = query[first:, :], grad_in[first:, :]
        grad_k = jnp.zeros((rows, width), f32)
        grad_v = jnp.zeros((rows, width), f32)
        grad_q = None
        for h in range(heads):
            mine = head_of == h
            k_h = jnp.where(mine, k_here, jnp.zeros_like(k_here))
            v_h = jnp.where(mine, v_here, jnp.zeros_like(v_here))
            probs = jnp.exp(dot_rows(k_h, q_there) + bias - logs[h : h + 1, first:])
            slopes = probs * (dot_rows(v_h, g_there) - inner[h : h + 1, first:])
            probs_low, slopes_low = probs.astype(bf16), slopes.astype(bf16)
            grad_v = jnp.where(mine, dot(probs_low, g_there), grad_v)
            grad_k = jnp.where(mine, dot(slopes_low, q_there), grad_k)
            term = dot_cols(slopes_low, k_h)
            grad_q = term if grad_q is None else grad_q + term
        if j == 0:
            grad_query[...] = grad_q
        else:
            grad_query[first:, :] = grad_query[first:, :] + grad_q
        compact = []
        for values, turn in ((grad_k, True), (grad_v, False)):
            halves = []
            for lane_at in (0, LANES):
                part = values[:, lane_at : lane_at + LANES]
                part = part + pltpu.roll(part, HEAD_DIM, 1)
                halves.append(rope(part, cosine[here, :], -sine[here, :]) if turn else part)
            compact.append(jnp.where(lane < HEAD_DIM, halves[0], halves[1]).astype(bf16))
        grads[here, width : width + LANES] = compact[0]
        grads[here, width + LANES :] = compact[1]
        turned_q = rope(grad_query[here, :], cosine[here, :], -sine[here, :])
        grads[here, :width] = (turned_q * HEAD_DIM**-0.5).astype(bf16)
    for d, out in enumerate((out_0, out_1, out_2, out_3)):
        out[...] = grads[place(at, d, rows), :]


def join_kernel(
    at, mixed_0, mixed_1, mixed_2, mixed_3, weights, sib_weights, tokens, gain, hidden_out, inputs_out,
):
    half = weights.shape[1]
    mine = pl.ds(pl.multiple_of(at[2] * half, half), half)
    other = pl.ds(pl.multiple_of((1 - at[2]) * half, half), half)
    hidden = tokens[...].astype(f32)
    for d, part in enumerate((mixed_0, mixed_1, mixed_2, mixed_3)):
        owner = (at[3] + d) % SIDE
        hidden = hidden + dot(part[:, mine], weights[owner])
        hidden = hidden + dot(part[:, other], sib_weights[owner])
    scale = lax.rsqrt(jnp.mean(hidden * hidden, axis=1, keepdims=True) + eps_norm)
    hidden_out[...] = hidden
    inputs_out[...] = (hidden * scale * gain[...]).astype(bf16)


def expert_kernel(capacity, at, x_a, x_b, g_a, g_b, router, *refs):
    own, sib = refs[:3], refs[3:6]
    (grad_lo, grad_hi, share_out, mix_out, rows_out, grads_out, active_out, slopes_out,
     x_blocks, g_blocks, w_gate, w_up, w_down, taken_x, taken_g, grads, active, slopes, marks, grad_slots, mix_slots,
     grad_blocks, mix_blocks, x_sem, g_sem, w_sem, mix_sem, grad_sem, save_sem) = refs[6:]
    rows = x_a.shape[0]
    picks = 8
    experts = share_out.shape[0]
    taken = g_blocks.shape[1]
    z, x, core = at[0], at[1], at[2]
    me = (z * SIDE + x) * 2 + core
    ids = (me, me + 1 - 2 * core)
    x_from = (x_a, *[x_b.at[pl.ds(b * rows, rows), :] for b in range(SIDE - 1)])
    g_from = (g_a, *[g_b.at[pl.ds(b * taken, taken), :] for b in range(SIDE - 1)])
    saved = ((taken_x, rows_out), (grads, grads_out), (active, active_out), (slopes, slopes_out))

    def x_copy(b):
        return pltpu.make_async_copy(x_from[b], x_blocks.at[b], x_sem.at[b])

    def g_copy(b):
        return pltpu.make_async_copy(g_from[b], g_blocks.at[b], g_sem.at[b])

    def w_copy(e, n):
        there = (w_gate, w_up, w_down)[n].at[e]
        return pltpu.make_async_copy((own, sib)[e][n].at[0], there, w_sem.at[e, n])

    def mix_copy(b):
        there = mix_out.at[pl.ds(b * rows, rows), :]
        return pltpu.make_async_copy(mix_blocks.at[b], there, mix_sem.at[b])

    def grad_copy(b):
        out = grad_lo if b < SIDE // 2 else grad_hi
        there = pl.ds(b % (SIDE // 2) * taken, taken)
        return pltpu.make_async_copy(grad_blocks.at[b], out.at[there, :], grad_sem.at[b])

    def save(e, n):
        return pltpu.make_async_copy(saved[n][0].at[e], saved[n][1].at[e], save_sem.at[e, n])

    for b in range(SIDE):
        g_copy(b).start()
        x_copy(b).start()
    for e in range(2):
        for n in range(3):
            w_copy(e, n).start()

    expert = lax.broadcasted_iota(jnp.int32, (experts, rows), 0)
    token = lax.broadcasted_iota(jnp.int32, (rows, rows), 0)
    earlier = token < lax.broadcasted_iota(jnp.int32, (rows, rows), 1)
    earlier = earlier.astype(f32).astype(bf16)
    slot = lax.broadcasted_iota(jnp.int32, (capacity, rows), 0).astype(f32)
    gates, masks = ([], []), ([], [])
    for b in range(SIDE):
        there = slice(b * capacity, (b + 1) * capacity)
        g_copy(b).wait()
        named = g_blocks[b, rows : rows + picks, :rows].astype(f32).astype(jnp.int32)
        used = jnp.zeros((experts, rows), f32)
        for p in range(picks):
            used = jnp.where(named[p : p + 1, :] == expert, 1.0, used)
        rank = jnp.where(used > 0, dot(used.astype(bf16), earlier), -1.0)
        x_copy(b).wait()
        logits = jnp.transpose(dot(x_blocks[b], router[...]))[:experts, :]
        peak = jnp.max(jnp.where(used > 0, logits, mask_fill), axis=0, keepdims=True)
        raised = jnp.where(used > 0, jnp.exp(jnp.minimum(logits - peak, 0.0)), 0.0)
        ratio = raised / jnp.sum(raised, axis=0, keepdims=True)
        if b == 0:
            share_out[...] = ratio
        for e in range(2):
            mine = expert == ids[e]
            place_row = jnp.sum(jnp.where(mine, rank, 0.0), axis=0, keepdims=True)
            share_row = jnp.sum(jnp.where(mine, ratio, 0.0), axis=0, keepdims=True)
            mask = slot == place_row
            masks[e].append(mask)
            marks[b, e * capacity : (e + 1) * capacity, :] = mask.astype(f32).astype(bf16)
            gates[e].append(jnp.sum(jnp.where(mask, share_row, 0.0), axis=1, keepdims=True))
        both = dot(marks[b], x_blocks[b]).astype(bf16)
        taken_x[0, there, :], taken_x[1, there, :] = both[:capacity, :], both[capacity:, :]
        both = dot(marks[b], g_blocks[b, :rows, :]).astype(bf16)
        taken_g[0, there, :], taken_g[1, there, :] = both[:capacity, :], both[capacity:, :]
    products = []
    for e in range(2):
        save(e, 0).start()
        gate = jnp.concatenate(gates[e], axis=0)
        here = slice(e * capacity, (e + 1) * capacity)
        w_copy(e, 0).wait()
        w_copy(e, 1).wait()
        gate_pre = dot(taken_x[e], w_gate[e])
        up_pre = dot(taken_x[e], w_up[e])
        sigmoid = 1.0 / (1.0 + jnp.exp(-gate_pre))
        silu = gate_pre * sigmoid
        active[e] = (silu * up_pre).astype(bf16)
        save(e, 2).start()
        w_copy(e, 2).wait()
        produced = dot(active[e], w_down[e]).astype(bf16).astype(f32)
        wide_g = taken_g[e].astype(f32)
        products.append(jnp.sum(wide_g * produced, axis=1, keepdims=True))
        grads[e] = (gate * wide_g).astype(bf16)
        save(e, 1).start()
        mix = (gate * produced).astype(bf16)
        for b in range(SIDE):
            mix_slots[b, here, :] = mix[b * capacity : (b + 1) * capacity, :]
            if e == 1:
                mix_blocks[b] = dot_cols(marks[b], mix_slots[b]).astype(bf16)
                mix_copy(b).start()
        grad_active = dot_rows(grads[e], w_down[e])
        grad_up = (grad_active * silu).astype(bf16)
        slope = sigmoid * (1.0 + gate_pre * (1.0 - sigmoid))
        grad_gate = (grad_active * up_pre * slope).astype(bf16)
        width = grad_gate.shape[1]
        slopes[e, :, :width] = grad_gate
        slopes[e, :, width:] = grad_up
        save(e, 3).start()
        grad_x = (dot_rows(grad_gate, w_gate[e]) + dot_rows(grad_up, w_up[e])).astype(bf16)
        for b in range(SIDE):
            grad_slots[b, here, :] = grad_x[b * capacity : (b + 1) * capacity, :]
    for b in range(SIDE):
        there = slice(b * capacity, (b + 1) * capacity)
        grad_blocks[b, :rows, :] = dot_cols(marks[b], grad_slots[b]).astype(bf16)
        full = jnp.zeros((experts, rows), f32)
        for e in range(2):
            row = jnp.where(masks[e][b], products[e][there, :], 0.0)
            full = jnp.where(expert == ids[e], jnp.sum(row, axis=0, keepdims=True), full)
        high = full.astype(bf16)
        low = (full - high.astype(f32)).astype(bf16)
        parts = [part[i : i + 16, :] for part in (high, low) for i in range(0, experts, 16)]
        tail = jnp.concatenate(parts, axis=1)
        grad_blocks[b, rows:, : tail.shape[1]] = tail
        if tail.shape[1] < grad_blocks.shape[2]:
            rest = grad_blocks[b, rows:, tail.shape[1] :]
            grad_blocks[b, rows:, tail.shape[1] :] = jnp.zeros_like(rest)
        grad_copy(b).start()
    for b in range(SIDE):
        mix_copy(b).wait()
        grad_copy(b).wait()
    for e in range(2):
        for n in range(4):
            save(e, n).wait()


def expert_weights_kernel(e, *refs):
    sources, out = refs[: 4 * SIDE], refs[4 * SIDE]
    *scratch, total, sems = refs[4 * SIDE + 1 :]

    def load(i, n):
        return pltpu.make_async_copy(sources[4 * i + n].at[e], scratch[n].at[i], sems.at[i, n])

    for i in range(SIDE):
        for n in range(4):
            load(i, n).start()
    depth = out.shape[1]
    for i in range(SIDE):
        for n in range(4):
            load(i, n).wait()
        rows_in, grads, active, slopes = (ref[i] for ref in scratch)
        upper, lower = dot_cols(rows_in, slopes), dot_cols(active, grads)
        if i:
            upper, lower = total[:depth, :] + upper, total[depth:, :] + lower
        if i < SIDE - 1:
            total[:depth, :] = upper
            total[depth:, :] = lower
        else:
            out[:depth, :] = upper.astype(bf16)
            out[depth:, :] = lower.astype(bf16)


def fold_kernel(own_lo, own_hi, before_lo, before_hi, after_lo, after_hi, *outs):
    rows = outs[0].shape[0]
    for i, out in enumerate(outs):
        part = slice(i % 2 * rows, (i % 2 + 1) * rows)
        refs = (own_lo, before_lo, after_lo) if i < 2 else (own_hi, before_hi, after_hi)
        out[...] = sum(ref[part, :].astype(f32) for ref in refs).astype(bf16)


def fold_mix_kernel(own, before, after_, *outs):
    rows = outs[0].shape[0]
    for i, out in enumerate(outs):
        part = slice(i * rows, (i + 1) * rows)
        out[...] = sum(ref[part, :].astype(f32) for ref in (own, before, after_)).astype(bf16)


def turn_kernel(
    term_0, term_1, term_2, term_3, shares, router, inputs, hidden_in, gain, cotangent, grad_hidden_out, out,
):
    experts, rows = shares.shape
    total = sum(ref[...].astype(f32) for ref in (term_0, term_1, term_2, term_3))
    tail = [total[rows:, i * rows : (i + 1) * rows] for i in range(experts // 8)]
    count = len(tail) // 2
    grad_share = jnp.concatenate([tail[i] + tail[i + count] for i in range(count)], axis=0)
    share = shares[...]
    grad_logits = share * (grad_share - jnp.sum(share * grad_share, axis=0, keepdims=True))
    grad_logits = grad_logits.astype(bf16)
    out[rows : rows + experts, :] = dot(grad_logits, inputs[...]).astype(bf16)
    grad = total[:rows, :] + dot_cols(grad_logits, router[...])
    hidden = hidden_in[...]
    scale = lax.rsqrt(jnp.mean(hidden * hidden, axis=1, keepdims=True) + eps_norm)
    gain_row = jnp.sum(grad * hidden * scale, axis=0, keepdims=True)
    row = lax.broadcasted_iota(jnp.int32, (16, grad.shape[1]), 0)
    out[rows + experts :, :] = jnp.where(row == 0, gain_row, 0.0).astype(bf16)
    grad = grad * gain[...]
    inner = jnp.mean(grad * hidden, axis=1, keepdims=True)
    grad = cotangent[...].astype(f32) + scale * grad - hidden * (scale * scale * scale * inner)
    grad_hidden_out[...] = grad
    out[:rows, :] = grad.astype(bf16)


def finish_kernel(at, g_0, g_1, g_2, g_3, weights, sib_weights, tokens, gain, grad_hidden, out):
    mine = other = None
    for d, part in enumerate((g_0, g_1, g_2, g_3)):
        owner = (at[3] + d) % SIDE
        terms = dot_rows(part[...], weights[owner]), dot_rows(part[...], sib_weights[owner])
        mine, other = terms if d == 0 else (mine + terms[0], other + terms[1])
    first = at[2] == 0
    grad = jnp.concatenate([jnp.where(first, mine, other), jnp.where(first, other, mine)], axis=1)
    grad = grad * gain[...]
    x = tokens[...].astype(f32)
    scale = lax.rsqrt(jnp.mean(x * x, axis=1, keepdims=True) + eps_norm)
    inner = jnp.mean(grad * x, axis=1, keepdims=True)
    out[...] = grad_hidden[...] + scale * grad - x * (scale * scale * scale * inner)


def pack_kernel(
    at, normed, grads, mixed, part_0, part_1, part_2a, part_2b, part_3, w_own, gain, out, smalls,
):
    count, _, half = out.shape
    rows = mixed.shape[0] // SIDE
    cut = part_2a.shape[0]
    inner = dot_cols(normed[...], grads[...])
    outer = jnp.zeros((mixed.shape[1], normed.shape[1]), f32)
    for d, part in ((0, part_0), (1, part_1), (3, part_3)):
        outer = outer + dot_cols(mixed[place(at, d, rows), :], part[:rows, :])
        smalls[(at[3] + d) % SIDE] = part[rows:, :].astype(f32)
    far = (at[3] + 2) % SIDE * rows
    low = pl.ds(pl.multiple_of(far, 16), cut)
    outer = outer + dot_cols(mixed[low, :], part_2a[...])
    high = pl.ds(pl.multiple_of(far + cut, 16), rows - cut)
    outer = outer + dot_cols(mixed[high, :], part_2b[: rows - cut, :])
    smalls[(at[3] + 2) % SIDE] = part_2b[rows - cut :, :].astype(f32)
    small = smalls[0] + smalls[1] + smalls[2] + smalls[3]
    along = inner * w_own[...].astype(f32)
    along_hi = along.astype(bf16)
    along_lo = (along - along_hi.astype(f32)).astype(bf16)
    ones = jnp.ones((8, along.shape[1]), bf16)
    gain_1 = (dot_rows(ones, along_hi) + dot_rows(ones, along_lo)) / gain[...]
    gain_1, gain_2 = gain_1[0:1, :], small[count : count + 1, :]
    row = lax.broadcasted_iota(jnp.int32, (16, half), 0)
    gains = jnp.zeros((16, half), f32)
    for i, part in enumerate((gain_2[:, :half], gain_2[:, half:], gain_1[:, :half], gain_1[:, half:])):
        gains = jnp.where(row == 2 + i, part, gains)
    inner, outer = inner.astype(bf16), outer.astype(bf16)
    tall, short = inner.shape[0] // count, outer.shape[0] // count
    for c in range(count):
        out[c, :tall, :] = inner[c * tall : (c + 1) * tall, :]
        part = outer[c * short : (c + 1) * short, :].astype(f32)
        part = jnp.concatenate([part[:, :half], part[:, half:]], axis=0)
        out[c, tall : tall + 2 * short, :] = part.astype(bf16)
        last = jnp.where(row == 0, small[c : c + 1, :half], gains)
        last = jnp.where(row == 1, small[c : c + 1, half:], last)
        out[c, tall + 2 * short :, :] = last.astype(bf16)


def share_kernel(parts, out, last):
    total = parts[0].astype(f32)
    for i in range(1, parts.shape[0]):
        total = total + parts[i].astype(f32)
    last[...] = total[-16:, :]
    low = total.astype(bf16)
    for i in range(out.shape[0]):
        out[i] = low


def unpack_kernel(
    at, parts, last_0, last_1, last_2, last_3, query_out, key_out, value_out, output_out, router_out, gain_1_out, gain_2_out, lasts,
):
    count, size, half = parts.shape
    tall = query_out.shape[0] // count
    short = output_out.shape[0] // count
    width = query_out.shape[1]
    rows = []
    for c in range(count):
        here = slice(c * tall, (c + 1) * tall)
        part = parts[c].astype(f32)
        query_out[here, :] = part[:tall, :width]
        key_out[here, :] = part[:tall, width : width + key_out.shape[1]]
        value_out[here, :] = part[:tall, width + key_out.shape[1] :]
        here = slice(c * short, (c + 1) * short)
        output_out[here, :half] = part[tall : tall + short, :]
        output_out[here, half:] = part[tall + short : tall + 2 * short, :]
        last = part[tall + 2 * short :, :]
        rows.append(jnp.concatenate([last[0:1, :], last[1:2, :]], axis=1))
    router_out[...] = jnp.concatenate(rows, axis=0)
    for d, part in enumerate((last_0, last_1, last_2, last_3)):
        lasts[(at[3] + d) % SIDE] = part[...]
    total = lasts[0] + lasts[1] + lasts[2] + lasts[3]
    gain_1_out[:, :half] = total[4:5, :]
    gain_1_out[:, half:] = total[5:6, :]
    gain_2_out[:, :half] = last_0[2:3, :]
    gain_2_out[:, half:] = last_0[3:4, :]


def quarters_kernel(at, own, sib, *refs):
    outs, total = refs[:-1], refs[-1]
    total[...] = (own[...].astype(f32) + sib[...].astype(f32)).astype(bf16)
    rows = outs[0].shape[0]
    for d, out in enumerate(outs):
        out[...] = total[place(at, d, rows), :]


def owned_kernel(own, from_before, from_after, out):
    total = own[...].astype(f32) + from_before[...].astype(f32) + from_after[...].astype(f32)
    out[...] = total.astype(bf16)


def expert_unpack_kernel(at, own, from_after, far_lo, far_hi, from_before, gate_out, up_out, down_out, whole):
    rows = own.shape[0]
    half = far_lo.shape[0]
    whole[place(at, 0, rows), :] = own[...]
    whole[place(at, 1, rows), :] = from_after[...]
    whole[place(at, 3, rows), :] = from_before[...]
    far = (at[3] + 2) % SIDE * rows
    whole[pl.ds(pl.multiple_of(far, half), half), :] = far_lo[...]
    whole[pl.ds(pl.multiple_of(far + half, half), half), :] = far_hi[...]
    depth, width = gate_out.shape[1:]
    gate_out[0] = whole[:depth, :width].astype(f32)
    up_out[0] = whole[:depth, width:].astype(f32)
    down_out[0] = whole[depth:, :].astype(f32)


def body(
    tokens,
    cotangent,
    routes,
    lengths,
    gain_attn,
    w_query,
    w_key,
    w_value,
    w_output,
    gain_mix,
    w_router,
    gate_weight,
    up_weight,
    down_weight,
):
    rows, depth = tokens.shape
    picks = routes.shape[1]
    experts = lax.axis_size(PLANE)
    length = rows * SIDE
    width = w_query.shape[1]
    hidden_units = gate_weight.shape[2]
    capacity = min(rows, 3 * rows * picks // (2 * experts))
    core, y = lax.axis_index("core"), lax.axis_index("head")
    z, x = lax.axis_index("z"), lax.axis_index("x")
    at = jnp.stack([z, x, core, y]).astype(jnp.int32)
    gain_1, gain_2 = gain_attn[None, :], gain_mix[None, :]
    smem = pl.BlockSpec(memory_space=pltpu.SMEM)
    vmem = pl.BlockSpec(memory_space=pltpu.VMEM)
    anywhere = pl.BlockSpec(memory_space=pl.ANY)
    hbm = pl.BlockSpec(memory_space=pltpu.HBM)

    ends = jnp.cumsum(lengths[0], dtype=jnp.int32)
    index = jnp.arange(length, dtype=jnp.int32)
    starts = jnp.max(jnp.where(index[:, None] >= ends[None, :], ends[None, :], 0), axis=1)
    column_starts = starts[:, None]
    lane = jnp.arange(LANES)
    frequency = rope_base ** (-2.0 * (lane % (HEAD_DIM // 2)).astype(f32) / HEAD_DIM)
    angles = (index - starts).astype(f32)[:, None] * frequency[None, :]
    cosine = jnp.cos(angles)
    sine = jnp.sin(angles) * jnp.where(lane % HEAD_DIM < HEAD_DIM // 2, -1.0, 1.0)[None, :]

    half = width // 2
    mine = lax.dynamic_slice_in_dim(w_output, core * half, half, axis=0)
    mine = jnp.broadcast_to(mine[None], (SIDE, half, depth))
    token_parts = ring_gather(tokens, line_shift)
    own_weights = [gate_weight, up_weight, down_weight]
    sib_weights = [swap_core(a) for a in own_weights]
    named = jnp.pad(routes.T.astype(bf16), ((0, 16 - picks), (0, depth - rows)))
    marked = jnp.concatenate([cotangent, named], axis=0)
    grads_u = [shift_u(marked, -1), shift_u(marked, 2), shift_u(marked, 1)]
    grads_before, grads_after = shift_w(marked, 1), shift_w(marked, -1)
    mine, *token_parts[2:4] = together(mine, *token_parts[2:4])
    output_mine = swap_all(mine, "head")
    grads_rest = jnp.concatenate(grads_u, axis=0)
    token_parts[2], grads_rest = together(token_parts[2], grads_rest)
    grads_before_rest, grads_after_rest = shift_w(grads_rest, 1), shift_w(grads_rest, -1)

    normed, query, key, value, mixed, log_total, *mixed_out = call(
        attend_kernel,
        [
            array((length, depth), bf16),
            *[array((length, width), bf16)] * 4,
            array((length, LANES), f32),
            *[array((rows, width), bf16)] * SIDE,
        ],
        [at, *token_parts, gain_1, w_query, w_key, w_value, cosine, sine, column_starts],
        specs=[smem] + [vmem] * 12,
        out_specs=[hbm] * 6 + [vmem] * 4,
        scratch=[
            *[pltpu.VMEM((length, depth), bf16)] * 2,
            *[pltpu.VMEM((length, width), bf16)] * 4,
            pltpu.VMEM((length, LANES), f32),
            pltpu.SemaphoreType.DMA((SIDE, 6)),
        ],
        flops=12 * 10**9,
    )
    mixed_in = direct_swap(mixed_out, line_shift)
    output_mine, mixed_in[0] = together(output_mine, mixed_in[0])
    output_sib = swap_core(output_mine)
    router_rows = w_router.T.astype(bf16)
    router_wide = jnp.pad(w_router, ((0, 0), (0, LANES - experts))).astype(bf16)
    at_join, grads_before_rest, grads_after_rest = together(
        at, grads_before_rest, grads_after_rest
    )
    hidden, inputs = call(
        join_kernel,
        [array((rows, depth), f32), array((rows, depth), bf16)],
        [at_join, *mixed_in, output_mine, output_sib, tokens, gain_2],
        specs=[smem] + [vmem] * 8,
        flops=3 * 10**9,
        vmem=40,
    )

    u_parts = [shift_u(inputs, -1), shift_u(inputs, 2), shift_u(inputs, 1)]
    before_own, after_own = shift_w(inputs, 1), shift_w(inputs, -1)
    u_parts[0], grads_before, grads_after_rest, q_late, k_late, v_late = together(
        u_parts[0], grads_before, grads_after_rest, w_query, w_key, w_value
    )
    grads_far_own = shift_w(grads_before, 1)
    grads_far_rest = shift_w(grads_after_rest, -1)
    w_own = jnp.concatenate([q_late, k_late, v_late], axis=1)
    w_mine = lax.dynamic_slice_in_dim(w_own, core * (depth // 2), depth // 2, axis=0)
    w_mine = all_blocks(w_mine, "head")
    u_rest = jnp.concatenate(u_parts, axis=0)
    before_rest, after_rest = shift_w(u_rest, 1), shift_w(u_rest, -1)
    slots = SIDE * capacity
    half = array((length // 2 + 32, depth), bf16)

    def experts_on(at, x_parts, g_parts):
        outs = [
            half,
            half,
            array((experts, rows), f32),
            array((length, depth), bf16),
            array((2, slots, depth), bf16),
            array((2, slots, depth), bf16),
            array((2, slots, hidden_units), bf16),
            array((2, slots, 2 * hidden_units), bf16),
        ]
        args = [at, *x_parts, *g_parts, router_wide, *own_weights, *sib_weights]
        return list(call(
            functools.partial(expert_kernel, capacity),
            outs,
            args,
            specs=[smem, *[anywhere] * 4, vmem, *[anywhere] * 6],
            out_specs=[hbm, hbm, vmem, *[hbm] * 5],
            scratch=[
                pltpu.VMEM((SIDE, rows, depth), bf16),
                pltpu.VMEM((SIDE, rows + 16, depth), bf16),
                pltpu.VMEM((2, depth, hidden_units), bf16),
                pltpu.VMEM((2, depth, hidden_units), bf16),
                pltpu.VMEM((2, hidden_units, depth), bf16),
                *[pltpu.VMEM((2, slots, depth), bf16)] * 3,
                pltpu.VMEM((2, slots, hidden_units), bf16),
                pltpu.VMEM((2, slots, 2 * hidden_units), bf16),
                pltpu.VMEM((SIDE, 2 * capacity, rows), bf16),
                pltpu.VMEM((SIDE, 2 * capacity, depth), bf16),
                pltpu.VMEM((SIDE, 2 * capacity, depth), bf16),
                pltpu.VMEM((SIDE, rows + 16, depth), bf16),
                pltpu.VMEM((SIDE, rows, depth), bf16),
                pltpu.SemaphoreType.DMA((SIDE,)),
                pltpu.SemaphoreType.DMA((SIDE,)),
                pltpu.SemaphoreType.DMA((2, 3)),
                pltpu.SemaphoreType.DMA((SIDE,)),
                pltpu.SemaphoreType.DMA((SIDE,)),
                pltpu.SemaphoreType.DMA((2, 4)),
            ],
            flops=14 * 10**9,
        ))

    column = experts_on(at, [inputs, u_rest], [marked, grads_rest])
    before_own, after_rest, before_rest, column[0] = together(
        before_own, after_rest, before_rest, column[0]
    )
    far_own, far_rest = shift_w(before_own, 1), shift_w(after_rest, -1)
    at_next, column[0], grads_far_own, grads_far_rest = together(
        at, column[0], grads_far_own, grads_far_rest
    )
    right = experts_on(at_next, [after_own, after_rest], [grads_after, grads_after_rest])
    at_next, right[0], w_mine = together(at, right[0], w_mine)
    w_sib = swap_core(w_mine)
    far = experts_on(at_next, [far_own, far_rest], [grads_far_own, grads_far_rest])
    at_next, far[0] = together(at, far[0])
    left = experts_on(at_next, [before_own, before_rest], [grads_before, grads_before_rest])
    results = [column, right, far, left]

    weight_rows = depth + hidden_units
    flat = [a for r in results for a in r[4:]]

    def expert_weights(e):
        return call(
            functools.partial(expert_weights_kernel, e),
            [array((weight_rows, depth), bf16)],
            flat,
            specs=[anywhere] * len(flat),
            scratch=[
                *[pltpu.VMEM((SIDE, *a.shape[1:]), bf16) for a in flat[:4]],
                pltpu.VMEM((weight_rows, depth), f32),
                pltpu.SemaphoreType.DMA((SIDE, 4)),
            ],
            flops=10 * 10**9,
        )[0]

    from_before, from_after, _ = ring_sum([(r[0], r[1]) for r in results], shift_w)
    folded = list(call(
        fold_kernel,
        [array((rows + 16, depth), bf16)] * SIDE,
        [column[0], column[1], *from_before, *from_after],
        flops=2 * 10**9,
    ))
    flat[0], folded[0] = together(flat[0], folded[0])
    own_grads = expert_weights(0)
    grad_terms = direct_swap(folded, shift_u)
    grad_terms[0], own_grads = together(grad_terms[0], own_grads)

    grad_hidden, grad_low = call(
        turn_kernel,
        [array((rows, depth), f32), array((rows + experts + 16, depth), bf16)],
        [*grad_terms, column[2], router_rows, inputs, hidden, gain_2, cotangent],
        flops=4 * 10**9,
        vmem=40,
    )
    flat[0], grad_low = together(flat[0], grad_low)
    sib_grads = expert_weights(1)
    grad_parts, (sib_grads,) = ring_gather(grad_low, line_shift, sib_grads)
    sib_sums = swap_core(sib_grads)
    quarters = list(call(
        quarters_kernel,
        [array((weight_rows // SIDE, depth), bf16)] * SIDE,
        [at, own_grads, sib_sums],
        specs=[smem] + [vmem] * 2,
        scratch=[pltpu.VMEM((weight_rows, depth), bf16)],
        flops=3 * 10**9,
    ))
    quarter_far, quarter_after = line_shift(quarters[2], 1), line_shift(quarters[3], -1)
    at_back, quarters[0] = together(at, quarters[0])
    *mixes, grad_hidden = together(*[r[3] for r in results], grad_hidden)
    mix_far, mix_after = shift_w(mixes[2], 1), shift_w(mixes[3], -1)
    grads, *grads_out = call(
        attend_back_kernel,
        [array((length, 2 * width), bf16), *[array((rows, 2 * width), bf16)] * SIDE],
        [
            at_back,
            *grad_parts,
            w_output,
            query,
            key,
            value,
            mixed,
            log_total,
            starts[None, :],
            cosine,
            sine,
        ],
        specs=[smem] + [vmem] * 14,
        scratch=[pltpu.VMEM((length, width), bf16), pltpu.VMEM((length, width), f32)],
        flops=12 * 10**9,
    )
    grads_in = direct_swap(grads_out, line_shift)
    tall, short = depth // experts, width // experts
    size = tall + 2 * short + 16
    quarter_up = (quarters[1].astype(f32) + quarter_far.astype(f32)).astype(bf16)
    at_pack, quarter_up, quarter_after, mix_after = together(
        at, quarter_up, quarter_after, mix_after
    )
    quarter_before = line_shift(quarter_up, 1)
    mix_far, grads = together(mix_far, grads)
    mix_up = (mixes[1].astype(f32) + mix_far.astype(f32)).astype(bf16)
    at_pack, mix_up = together(at_pack, mix_up)
    mix_before = shift_w(mix_up, 1)
    packed = call(
        pack_kernel,
        [array((experts, size, depth // 2), bf16)],
        [at_pack, normed, grads, mixed, *grad_parts, w_own, gain_1],
        specs=[smem] + [vmem] * 10,
        scratch=[pltpu.VMEM((SIDE, experts + 16, depth), f32)],
        flops=6 * 10**9,
    )[0]
    packed, *grads_in = together(packed, *grads_in)
    arrived = swap_all(packed, PLANE)
    at_finish, packed, mix_before = together(at, packed, mix_before)
    grad_tokens = call(
        finish_kernel,
        [array((rows, depth), f32)],
        [at_finish, *grads_in, w_mine, w_sib, tokens, gain_1, grad_hidden],
        specs=[smem] + [vmem] * 9,
        flops=4 * 10**9,
    )[0]
    mixes[0], grad_tokens = together(mixes[0], grad_tokens)
    mix_folded = list(call(
        fold_mix_kernel,
        [array((rows, depth), bf16)] * SIDE,
        [mixes[0], mix_before, mix_after],
        flops=2 * 10**9,
    ))
    mix_terms = direct_swap(mix_folded, shift_u)
    arrived, mix_folded[0] = together(arrived, mix_folded[0])
    shared, last = call(
        share_kernel,
        [array(packed.shape, bf16), array((16, depth // 2), f32)],
        [arrived],
        flops=2 * 10**9,
    )
    quarters[0], last = together(quarters[0], last)
    expert_owned = call(
        owned_kernel,
        [array((weight_rows // SIDE, depth), bf16)],
        [quarters[0], quarter_before, quarter_after],
        flops=10**9,
    )[0]
    expert_parts = ring_gather(expert_owned, line_shift)
    lasts = [last, line_shift(last, -1), line_shift(last, 2), line_shift(last, 1)]
    output = (hidden + sum(term.astype(f32) for term in mix_terms)).astype(bf16)
    mix_terms[1], mix_terms[2], mix_terms[3], expert_parts[2] = together(
        mix_terms[1], mix_terms[2], mix_terms[3], expert_parts[2]
    )
    expert_totals = call(
        expert_unpack_kernel,
        [
            array((1, depth, hidden_units), f32),
            array((1, depth, hidden_units), f32),
            array((1, hidden_units, depth), f32),
        ],
        [at, *expert_parts],
        specs=[smem] + [vmem] * 5,
        scratch=[pltpu.VMEM((weight_rows, depth), bf16)],
        flops=4 * 10**9,
    )
    gathered, output, *expert_totals = together(swap_all(shared, PLANE), output, *expert_totals)
    grad_query, grad_key, grad_value, grad_output, grad_router, grad_gain_1, grad_gain_2 = call(
        unpack_kernel,
        [
            array((depth, width), f32),
            array((depth, LANES), f32),
            array((depth, LANES), f32),
            array((width, depth), f32),
            array((experts, depth), f32),
            array((1, depth), f32),
            array((1, depth), f32),
        ],
        [at, gathered, *lasts],
        specs=[smem] + [vmem] * 5,
        scratch=[pltpu.VMEM((SIDE, 16, depth // 2), f32)],
        flops=4 * 10**9,
    )

    return (
        output,
        grad_tokens,
        grad_gain_1[0],
        grad_query,
        grad_key,
        grad_value,
        grad_output,
        grad_gain_2[0],
        grad_router.T,
        *expert_totals,
    )


def solution(mesh):
    axes = (*PLANE, "head")
    mesh = jax.sharding.Mesh(mesh.devices.reshape(SIDE, SIDE, 2, SIDE), axes)
    rows = P(axes, None)
    per_expert = P(PLANE, None, None)
    columns = P(None, "head")
    in_specs = (
        rows,
        rows,
        rows,
        P(PLANE, None),
        P(),
        columns,
        columns,
        columns,
        P("head", None),
        P(),
        P(),
        per_expert,
        per_expert,
        per_expert,
    )
    out_specs = (
        rows,
        rows,
        P(),
        columns,
        columns,
        columns,
        P("head", None),
        P(),
        P(),
        per_expert,
        per_expert,
        per_expert,
    )
    return jax.shard_map(body, mesh=mesh, in_specs=in_specs, out_specs=out_specs, check_vma=False)
```

```python
import functools

import jax
import jax.numpy as jnp
from jax import lax
from jax.experimental import pallas as pl
from jax.experimental.pallas import tpu as pltpu
from jax.sharding import PartitionSpec as P

HEAD_DIM = 64
SIDE = 4
LANES = 128
MIB = 1024 * 1024

eps_norm = 1e-06
rope_base = 10000.0
mask_fill = -1000000000.0

bf16 = jnp.bfloat16
f32 = jnp.float32


def dot(left, right):
    return lax.dot_general(left, right, (((1,), (0,)), ((), ())), preferred_element_type=f32)


def dot_rows(left, right):
    return lax.dot_general(left, right, (((1,), (1,)), ((), ())), preferred_element_type=f32)


def dot_cols(left, right):
    return lax.dot_general(left, right, (((0,), (0,)), ((), ())), preferred_element_type=f32)


def call(kernel, out_shapes, args, specs=None, out_specs=None, scratch=(), flops=0, vmem=60):
    moved = sum(a.size * a.dtype.itemsize for a in args)
    moved += sum(s.size * s.dtype.itemsize for s in out_shapes)
    whole = pl.BlockSpec(memory_space=pltpu.VMEM)
    return pl.pallas_call(
        kernel,
        out_shape=out_shapes,
        in_specs=specs or [whole] * len(args),
        out_specs=out_specs or [whole] * len(out_shapes),
        scratch_shapes=list(scratch),
        compiler_params=pltpu.CompilerParams(vmem_limit_bytes=vmem * MIB),
        cost_estimate=pl.CostEstimate(flops=flops, bytes_accessed=moved, transcendentals=0),
    )(*args)


def array(shape, dtype):
    return jax.ShapeDtypeStruct(shape, dtype)


CHIPS = ("z", "x")
PLANE = ("z", "x", "core")


def line_shift(values, step):
    pairs = [(i, (i + step) % SIDE) for i in range(SIDE)]
    return lax.ppermute(values, "head", pairs)


def plane_shift(first, values, step):
    pairs = []
    for i in range(2 * SIDE * SIDE):
        z, x, core = i // (2 * SIDE), i // 2 % SIDE, i % 2
        if (core == 0) == first:
            z = (z + step) % SIDE
        else:
            x = (x + step) % SIDE
        pairs.append((i, (z * SIDE + x) * 2 + core))
    return lax.ppermute(values, PLANE, pairs)


shift_u = functools.partial(plane_shift, True)
shift_w = functools.partial(plane_shift, False)


def swap_core(values):
    return lax.ppermute(values, "core", [(0, 1), (1, 0)])


def together(*values):
    return lax.optimization_barrier(values)


def ring_gather(block, shift, *between):
    half = block.shape[0] // 32 * 16
    from_before, from_after = shift(block, 1), shift(block, -1)
    from_before, from_after, *between = together(from_before, from_after, *between)
    far_lo, far_hi = shift(from_before[:half], 1), shift(from_after[half:], -1)
    parts = [block, from_after, far_lo, far_hi, from_before]
    return (parts, between) if between else parts


def direct_swap(parts, shift):
    return [parts[0], shift(parts[3], -1), shift(parts[2], 2), shift(parts[1], 1)]


def ring_sum(parts, shift):
    before_high, after_low = shift(parts[1][1], 1), shift(parts[3][0], -1)
    low_in, high_in = shift(parts[2][0], 1), shift(parts[2][1], -1)
    up = (parts[1][0].astype(f32) + low_in.astype(f32)).astype(bf16)
    down = (parts[3][1].astype(f32) + high_in.astype(f32)).astype(bf16)
    before_low, after_high = shift(up, 1), shift(down, -1)
    return (before_low, before_high), (after_low, after_high), (up, down)


def swap_all(values, axes):
    return lax.all_to_all(values, axes, 0, 0, tiled=True)


def all_blocks(block, axes):
    count = lax.axis_size(axes)
    return swap_all(jnp.broadcast_to(block[None], (count, *block.shape)), axes)


def rope(values, cosine, sine_signed):
    lane = lax.broadcasted_iota(jnp.int32, cosine.shape, 1)
    front = lane % HEAD_DIM < HEAD_DIM // 2
    out = []
    for at in range(0, values.shape[1], LANES):
        part = values[:, at : at + LANES]
        partner = jnp.where(
            front,
            pltpu.roll(part, LANES - HEAD_DIM // 2, 1),
            pltpu.roll(part, HEAD_DIM // 2, 1),
        )
        out.append(part * cosine + partner * sine_signed)
    return jnp.concatenate(out, axis=1)


def twice(values):
    lane = lax.broadcasted_iota(jnp.int32, values.shape, 1)
    swapped = pltpu.roll(values, HEAD_DIM, 1)
    first = lane < HEAD_DIM
    return jnp.concatenate(
        [jnp.where(first, values, swapped), jnp.where(first, swapped, values)], axis=1
    )


def place(at, distance, rows):
    return pl.ds(pl.multiple_of((at[3] + distance) % SIDE * rows, rows), rows)


def attend_kernel(
    at, own, from_after, far_lo, far_hi, from_before, gain, w_query, w_key, w_value, cosine, sine, starts,
    normed_out, query_out, key_out, value_out, mixed_out, log_out, mixed_0, mixed_1, mixed_2, mixed_3,
    rows_in, normed, query, key, value, mixed, log_total, sems,
):
    rows = own.shape[0]
    width = query.shape[1]
    kept = (normed, query, key, value, mixed, log_total)
    outs = (normed_out, query_out, key_out, value_out, mixed_out, log_out)

    def keep(i, n):
        here = pl.ds(i * rows, rows)
        return pltpu.make_async_copy(kept[n].at[here, :], outs[n].at[here, :], sems.at[i, n])

    rows_in[place(at, 0, rows), :] = own[...]
    rows_in[place(at, 1, rows), :] = from_after[...]
    rows_in[place(at, 3, rows), :] = from_before[...]
    half = rows // 2
    far = (at[3] + 2) % SIDE * rows
    rows_in[pl.ds(pl.multiple_of(far, half), half), :] = far_lo[...]
    rows_in[pl.ds(pl.multiple_of(far + half, half), half), :] = far_hi[...]
    head_of = lax.broadcasted_iota(jnp.int32, (rows, width), 1) // HEAD_DIM
    lane = lax.broadcasted_iota(jnp.int32, (rows, LANES), 1)
    for i in range(SIDE):
        here = slice(i * rows, (i + 1) * rows)
        extent = (i + 1) * rows
        x = rows_in[here, :].astype(f32)
        scale = lax.rsqrt(jnp.mean(x * x, axis=1, keepdims=True) + eps_norm)
        low = (x * scale * gain[...]).astype(bf16)
        normed[here, :] = low
        q = rope(dot(low, w_query[...]), cosine[here, :], sine[here, :]).astype(bf16)
        q = q * jnp.asarray(HEAD_DIM**-0.5, bf16)
        query[here, :] = q
        raw = rope(dot(low, w_key[...]), cosine[here, :], sine[here, :])
        key[here, :] = twice(raw).astype(bf16)
        value[here, :] = twice(dot(low, w_value[...])).astype(bf16)
        column = lax.broadcasted_iota(jnp.int32, (rows, extent), 1)
        row = i * rows + lax.broadcasted_iota(jnp.int32, (rows, extent), 0)
        bias = jnp.where((column >= starts[here, :]) & (column <= row), 0.0, mask_fill)
        total = jnp.zeros((rows, width), f32)
        logs = jnp.zeros((rows, LANES), f32)
        for h in range(width // HEAD_DIM):
            q_h = jnp.where(head_of == h, q, jnp.zeros_like(q))
            scores = dot_rows(q_h, key[:extent, :]) + bias
            peak = jnp.max(scores, axis=1, keepdims=True)
            lifted = jnp.exp(scores - peak)
            summed = jnp.sum(lifted, axis=1, keepdims=True)
            probs = (lifted * (1.0 / summed)).astype(bf16)
            total = jnp.where(head_of == h, dot(probs, value[:extent, :]), total)
            logs = jnp.where(lane == h, peak + jnp.log(summed), logs)
        mixed[here, :] = total.astype(bf16)
        log_total[here, :] = logs
        for n in range(len(kept)):
            keep(i, n).start()
    for d, out in enumerate((mixed_0, mixed_1, mixed_2, mixed_3)):
        out[...] = mixed[place(at, d, rows), :]
    for i in range(SIDE):
        for n in range(len(kept)):
            keep(i, n).wait()


def attend_back_kernel(
    at, part_0, part_1, part_2a, part_2b, part_3, w_output, query, key, value, mixed, log_total, starts, cosine, sine,
    grads, out_0, out_1, out_2, out_3, grad_in, grad_query,
):
    rows, width = out_0.shape[0], query.shape[1]
    length = rows * SIDE
    heads = width // HEAD_DIM
    for d, part in ((0, part_0), (1, part_1), (3, part_3)):
        grad_in[place(at, d, rows), :] = dot_rows(part[:rows, :], w_output[...]).astype(bf16)
    cut = part_2a.shape[0]
    far = (at[3] + 2) % SIDE * rows
    low = pl.ds(pl.multiple_of(far, 16), cut)
    grad_in[low, :] = dot_rows(part_2a[...], w_output[...]).astype(bf16)
    high = pl.ds(pl.multiple_of(far + cut, 16), rows - cut)
    grad_in[high, :] = dot_rows(part_2b[: rows - cut, :], w_output[...]).astype(bf16)
    both = grad_in[...].astype(f32) * mixed[...].astype(f32)
    both_hi = both.astype(bf16)
    both_lo = (both - both_hi.astype(f32)).astype(bf16)
    marks = lax.broadcasted_iota(jnp.int32, (8, width), 1) // HEAD_DIM
    marks = (marks == lax.broadcasted_iota(jnp.int32, (8, width), 0)).astype(bf16)
    inner = dot_rows(marks, both_hi) + dot_rows(marks, both_lo)
    logs = jnp.transpose(log_total[...])
    head_of = lax.broadcasted_iota(jnp.int32, (rows, width), 1) // HEAD_DIM
    lane = lax.broadcasted_iota(jnp.int32, (rows, LANES), 1)
    for j in range(SIDE):
        here = slice(j * rows, (j + 1) * rows)
        first = j * rows
        extent = length - first
        key_at = first + lax.broadcasted_iota(jnp.int32, (rows, extent), 0)
        query_at = first + lax.broadcasted_iota(jnp.int32, (rows, extent), 1)
        allowed = (key_at >= starts[:, first:]) & (key_at <= query_at)
        bias = jnp.where(allowed, 0.0, mask_fill)
        k_here, v_here = key[here, :], value[here, :]
        q_there, g_there = query[first:, :], grad_in[first:, :]
        grad_k = jnp.zeros((rows, width), f32)
        grad_v = jnp.zeros((rows, width), f32)
        grad_q = None
        for h in range(heads):
            mine = head_of == h
            k_h = jnp.where(mine, k_here, jnp.zeros_like(k_here))
            v_h = jnp.where(mine, v_here, jnp.zeros_like(v_here))
            probs = jnp.exp(dot_rows(k_h, q_there) + bias - logs[h : h + 1, first:])
            slopes = probs * (dot_rows(v_h, g_there) - inner[h : h + 1, first:])
            probs_low, slopes_low = probs.astype(bf16), slopes.astype(bf16)
            grad_v = jnp.where(mine, dot(probs_low, g_there), grad_v)
            grad_k = jnp.where(mine, dot(slopes_low, q_there), grad_k)
            term = dot_cols(slopes_low, k_h)
            grad_q = term if grad_q is None else grad_q + term
        if j == 0:
            grad_query[...] = grad_q
        else:
            grad_query[first:, :] = grad_query[first:, :] + grad_q
        compact = []
        for values, turn in ((grad_k, True), (grad_v, False)):
            halves = []
            for lane_at in (0, LANES):
                part = values[:, lane_at : lane_at + LANES]
                part = part + pltpu.roll(part, HEAD_DIM, 1)
                halves.append(rope(part, cosine[here, :], -sine[here, :]) if turn else part)
            compact.append(jnp.where(lane < HEAD_DIM, halves[0], halves[1]).astype(bf16))
        grads[here, width : width + LANES] = compact[0]
        grads[here, width + LANES :] = compact[1]
        turned_q = rope(grad_query[here, :], cosine[here, :], -sine[here, :])
        grads[here, :width] = (turned_q * HEAD_DIM**-0.5).astype(bf16)
    for d, out in enumerate((out_0, out_1, out_2, out_3)):
        out[...] = grads[place(at, d, rows), :]


def join_kernel(
    at, mixed_0, mixed_1, mixed_2, mixed_3, weights, sib_weights, tokens, gain, hidden_out, inputs_out,
):
    half = weights.shape[1]
    mine = pl.ds(pl.multiple_of(at[2] * half, half), half)
    other = pl.ds(pl.multiple_of((1 - at[2]) * half, half), half)
    hidden = tokens[...].astype(f32)
    for d, part in enumerate((mixed_0, mixed_1, mixed_2, mixed_3)):
        owner = (at[3] + d) % SIDE
        hidden = hidden + dot(part[:, mine], weights[owner])
        hidden = hidden + dot(part[:, other], sib_weights[owner])
    scale = lax.rsqrt(jnp.mean(hidden * hidden, axis=1, keepdims=True) + eps_norm)
    hidden_out[...] = hidden
    inputs_out[...] = (hidden * scale * gain[...]).astype(bf16)


def expert_kernel(capacity, at, x_a, x_b, g_a, g_b, router, *refs):
    own, sib = refs[:3], refs[3:6]
    (grad_lo, grad_hi, share_out, mix_out, rows_out, grads_out, active_out, slopes_out,
     x_blocks, g_blocks, w_gate, w_up, w_down, taken_x, taken_g, grads, active, slopes, marks, grad_slots, mix_slots,
     grad_blocks, mix_blocks, x_sem, g_sem, w_sem, mix_sem, grad_sem, save_sem) = refs[6:]
    rows = x_a.shape[0]
    picks = 8
    experts = share_out.shape[0]
    taken = g_blocks.shape[1]
    z, x, core = at[0], at[1], at[2]
    me = (z * SIDE + x) * 2 + core
    ids = (me, me + 1 - 2 * core)
    x_from = (x_a, *[x_b.at[pl.ds(b * rows, rows), :] for b in range(SIDE - 1)])
    g_from = (g_a, *[g_b.at[pl.ds(b * taken, taken), :] for b in range(SIDE - 1)])
    saved = ((taken_x, rows_out), (grads, grads_out), (active, active_out), (slopes, slopes_out))

    def x_copy(b):
        return pltpu.make_async_copy(x_from[b], x_blocks.at[b], x_sem.at[b])

    def g_copy(b):
        return pltpu.make_async_copy(g_from[b], g_blocks.at[b], g_sem.at[b])

    def w_copy(e, n):
        there = (w_gate, w_up, w_down)[n].at[e]
        return pltpu.make_async_copy((own, sib)[e][n].at[0], there, w_sem.at[e, n])

    def mix_copy(b):
        there = mix_out.at[pl.ds(b * rows, rows), :]
        return pltpu.make_async_copy(mix_blocks.at[b], there, mix_sem.at[b])

    def grad_copy(b):
        out = grad_lo if b < SIDE // 2 else grad_hi
        there = pl.ds(b % (SIDE // 2) * taken, taken)
        return pltpu.make_async_copy(grad_blocks.at[b], out.at[there, :], grad_sem.at[b])

    def save(e, n):
        return pltpu.make_async_copy(saved[n][0].at[e], saved[n][1].at[e], save_sem.at[e, n])

    for b in range(SIDE):
        g_copy(b).start()
        x_copy(b).start()
    for e in range(2):
        for n in range(3):
            w_copy(e, n).start()

    expert = lax.broadcasted_iota(jnp.int32, (experts, rows), 0)
    token = lax.broadcasted_iota(jnp.int32, (rows, rows), 0)
    earlier = token < lax.broadcasted_iota(jnp.int32, (rows, rows), 1)
    earlier = earlier.astype(f32).astype(bf16)
    slot = lax.broadcasted_iota(jnp.int32, (capacity, rows), 0).astype(f32)
    gates, masks = ([], []), ([], [])
    for b in range(SIDE):
        there = slice(b * capacity, (b + 1) * capacity)
        g_copy(b).wait()
        named = g_blocks[b, rows : rows + picks, :rows].astype(f32).astype(jnp.int32)
        used = jnp.zeros((experts, rows), f32)
        for p in range(picks):
            used = jnp.where(named[p : p + 1, :] == expert, 1.0, used)
        rank = jnp.where(used > 0, dot(used.astype(bf16), earlier), -1.0)
        x_copy(b).wait()
        logits = jnp.transpose(dot(x_blocks[b], router[...]))[:experts, :]
        peak = jnp.max(jnp.where(used > 0, logits, mask_fill), axis=0, keepdims=True)
        raised = jnp.where(used > 0, jnp.exp(jnp.minimum(logits - peak, 0.0)), 0.0)
        ratio = raised / jnp.sum(raised, axis=0, keepdims=True)
        if b == 0:
            share_out[...] = ratio
        for e in range(2):
            mine = expert == ids[e]
            place_row = jnp.sum(jnp.where(mine, rank, 0.0), axis=0, keepdims=True)
            share_row = jnp.sum(jnp.where(mine, ratio, 0.0), axis=0, keepdims=True)
            mask = slot == place_row
            masks[e].append(mask)
            marks[b, e * capacity : (e + 1) * capacity, :] = mask.astype(f32).astype(bf16)
            gates[e].append(jnp.sum(jnp.where(mask, share_row, 0.0), axis=1, keepdims=True))
        both = dot(marks[b], x_blocks[b]).astype(bf16)
        taken_x[0, there, :], taken_x[1, there, :] = both[:capacity, :], both[capacity:, :]
        both = dot(marks[b], g_blocks[b, :rows, :]).astype(bf16)
        taken_g[0, there, :], taken_g[1, there, :] = both[:capacity, :], both[capacity:, :]
    products = []
    for e in range(2):
        save(e, 0).start()
        gate = jnp.concatenate(gates[e], axis=0)
        here = slice(e * capacity, (e + 1) * capacity)
        w_copy(e, 0).wait()
        w_copy(e, 1).wait()
        gate_pre = dot(taken_x[e], w_gate[e])
        up_pre = dot(taken_x[e], w_up[e])
        sigmoid = 1.0 / (1.0 + jnp.exp(-gate_pre))
        silu = gate_pre * sigmoid
        active[e] = (silu * up_pre).astype(bf16)
        save(e, 2).start()
        w_copy(e, 2).wait()
        produced = dot(active[e], w_down[e]).astype(bf16).astype(f32)
        wide_g = taken_g[e].astype(f32)
        products.append(jnp.sum(wide_g * produced, axis=1, keepdims=True))
        grads[e] = (gate * wide_g).astype(bf16)
        save(e, 1).start()
        mix = (gate * produced).astype(bf16)
        for b in range(SIDE):
            mix_slots[b, here, :] = mix[b * capacity : (b + 1) * capacity, :]
            if e == 1:
                mix_blocks[b] = dot_cols(marks[b], mix_slots[b]).astype(bf16)
                mix_copy(b).start()
        grad_active = dot_rows(grads[e], w_down[e])
        grad_up = (grad_active * silu).astype(bf16)
        slope = sigmoid * (1.0 + gate_pre * (1.0 - sigmoid))
        grad_gate = (grad_active * up_pre * slope).astype(bf16)
        width = grad_gate.shape[1]
        slopes[e, :, :width] = grad_gate
        slopes[e, :, width:] = grad_up
        save(e, 3).start()
        grad_x = (dot_rows(grad_gate, w_gate[e]) + dot_rows(grad_up, w_up[e])).astype(bf16)
        for b in range(SIDE):
            grad_slots[b, here, :] = grad_x[b * capacity : (b + 1) * capacity, :]
    for b in range(SIDE):
        there = slice(b * capacity, (b + 1) * capacity)
        grad_blocks[b, :rows, :] = dot_cols(marks[b], grad_slots[b]).astype(bf16)
        full = jnp.zeros((experts, rows), f32)
        for e in range(2):
            row = jnp.where(masks[e][b], products[e][there, :], 0.0)
            full = jnp.where(expert == ids[e], jnp.sum(row, axis=0, keepdims=True), full)
        high = full.astype(bf16)
        low = (full - high.astype(f32)).astype(bf16)
        parts = [part[i : i + 16, :] for part in (high, low) for i in range(0, experts, 16)]
        tail = jnp.concatenate(parts, axis=1)
        grad_blocks[b, rows:, : tail.shape[1]] = tail
        if tail.shape[1] < grad_blocks.shape[2]:
            rest = grad_blocks[b, rows:, tail.shape[1] :]
            grad_blocks[b, rows:, tail.shape[1] :] = jnp.zeros_like(rest)
        grad_copy(b).start()
    for b in range(SIDE):
        mix_copy(b).wait()
        grad_copy(b).wait()
    for e in range(2):
        for n in range(4):
            save(e, n).wait()


def expert_weights_kernel(e, *refs):
    sources, out = refs[: 4 * SIDE], refs[4 * SIDE]
    *scratch, total, sems = refs[4 * SIDE + 1 :]

    def load(i, n):
        return pltpu.make_async_copy(sources[4 * i + n].at[e], scratch[n].at[i], sems.at[i, n])

    for i in range(SIDE):
        for n in range(4):
            load(i, n).start()
    depth = out.shape[1]
    for i in range(SIDE):
        for n in range(4):
            load(i, n).wait()
        rows_in, grads, active, slopes = (ref[i] for ref in scratch)
        upper, lower = dot_cols(rows_in, slopes), dot_cols(active, grads)
        if i:
            upper, lower = total[:depth, :] + upper, total[depth:, :] + lower
        if i < SIDE - 1:
            total[:depth, :] = upper
            total[depth:, :] = lower
        else:
            out[:depth, :] = upper.astype(bf16)
            out[depth:, :] = lower.astype(bf16)


def fold_kernel(own_lo, own_hi, before_lo, before_hi, after_lo, after_hi, *outs):
    rows = outs[0].shape[0]
    for i, out in enumerate(outs):
        part = slice(i % 2 * rows, (i % 2 + 1) * rows)
        refs = (own_lo, before_lo, after_lo) if i < 2 else (own_hi, before_hi, after_hi)
        out[...] = sum(ref[part, :].astype(f32) for ref in refs).astype(bf16)


def fold_mix_kernel(own, before, after_, *outs):
    rows = outs[0].shape[0]
    for i, out in enumerate(outs):
        part = slice(i * rows, (i + 1) * rows)
        out[...] = sum(ref[part, :].astype(f32) for ref in (own, before, after_)).astype(bf16)


def turn_kernel(
    term_0, term_1, term_2, term_3, shares, router, inputs, hidden_in, gain, cotangent, grad_hidden_out, out,
):
    experts, rows = shares.shape
    total = sum(ref[...].astype(f32) for ref in (term_0, term_1, term_2, term_3))
    tail = [total[rows:, i * rows : (i + 1) * rows] for i in range(experts // 8)]
    count = len(tail) // 2
    grad_share = jnp.concatenate([tail[i] + tail[i + count] for i in range(count)], axis=0)
    share = shares[...]
    grad_logits = share * (grad_share - jnp.sum(share * grad_share, axis=0, keepdims=True))
    grad_logits = grad_logits.astype(bf16)
    out[rows : rows + experts, :] = dot(grad_logits, inputs[...]).astype(bf16)
    grad = total[:rows, :] + dot_cols(grad_logits, router[...])
    hidden = hidden_in[...]
    scale = lax.rsqrt(jnp.mean(hidden * hidden, axis=1, keepdims=True) + eps_norm)
    gain_row = jnp.sum(grad * hidden * scale, axis=0, keepdims=True)
    row = lax.broadcasted_iota(jnp.int32, (16, grad.shape[1]), 0)
    out[rows + experts :, :] = jnp.where(row == 0, gain_row, 0.0).astype(bf16)
    grad = grad * gain[...]
    inner = jnp.mean(grad * hidden, axis=1, keepdims=True)
    grad = cotangent[...].astype(f32) + scale * grad - hidden * (scale * scale * scale * inner)
    grad_hidden_out[...] = grad
    out[:rows, :] = grad.astype(bf16)


def finish_kernel(at, g_0, g_1, g_2, g_3, weights, sib_weights, tokens, gain, grad_hidden, out):
    mine = other = None
    for d, part in enumerate((g_0, g_1, g_2, g_3)):
        owner = (at[3] + d) % SIDE
        terms = dot_rows(part[...], weights[owner]), dot_rows(part[...], sib_weights[owner])
        mine, other = terms if d == 0 else (mine + terms[0], other + terms[1])
    first = at[2] == 0
    grad = jnp.concatenate([jnp.where(first, mine, other), jnp.where(first, other, mine)], axis=1)
    grad = grad * gain[...]
    x = tokens[...].astype(f32)
    scale = lax.rsqrt(jnp.mean(x * x, axis=1, keepdims=True) + eps_norm)
    inner = jnp.mean(grad * x, axis=1, keepdims=True)
    out[...] = grad_hidden[...] + scale * grad - x * (scale * scale * scale * inner)


def pack_kernel(
    at, normed, grads, mixed, part_0, part_1, part_2a, part_2b, part_3, w_own, gain, out, smalls,
):
    count, _, half = out.shape
    rows = mixed.shape[0] // SIDE
    cut = part_2a.shape[0]
    inner = dot_cols(normed[...], grads[...])
    outer = jnp.zeros((mixed.shape[1], normed.shape[1]), f32)
    for d, part in ((0, part_0), (1, part_1), (3, part_3)):
        outer = outer + dot_cols(mixed[place(at, d, rows), :], part[:rows, :])
        smalls[(at[3] + d) % SIDE] = part[rows:, :].astype(f32)
    far = (at[3] + 2) % SIDE * rows
    low = pl.ds(pl.multiple_of(far, 16), cut)
    outer = outer + dot_cols(mixed[low, :], part_2a[...])
    high = pl.ds(pl.multiple_of(far + cut, 16), rows - cut)
    outer = outer + dot_cols(mixed[high, :], part_2b[: rows - cut, :])
    smalls[(at[3] + 2) % SIDE] = part_2b[rows - cut :, :].astype(f32)
    small = smalls[0] + smalls[1] + smalls[2] + smalls[3]
    along = inner * w_own[...].astype(f32)
    along_hi = along.astype(bf16)
    along_lo = (along - along_hi.astype(f32)).astype(bf16)
    ones = jnp.ones((8, along.shape[1]), bf16)
    gain_1 = (dot_rows(ones, along_hi) + dot_rows(ones, along_lo)) / gain[...]
    gain_1, gain_2 = gain_1[0:1, :], small[count : count + 1, :]
    row = lax.broadcasted_iota(jnp.int32, (16, half), 0)
    gains = jnp.zeros((16, half), f32)
    for i, part in enumerate((gain_2[:, :half], gain_2[:, half:], gain_1[:, :half], gain_1[:, half:])):
        gains = jnp.where(row == 2 + i, part, gains)
    inner, outer = inner.astype(bf16), outer.astype(bf16)
    tall, short = inner.shape[0] // count, outer.shape[0] // count
    for c in range(count):
        out[c, :tall, :] = inner[c * tall : (c + 1) * tall, :]
        part = outer[c * short : (c + 1) * short, :].astype(f32)
        part = jnp.concatenate([part[:, :half], part[:, half:]], axis=0)
        out[c, tall : tall + 2 * short, :] = part.astype(bf16)
        last = jnp.where(row == 0, small[c : c + 1, :half], gains)
        last = jnp.where(row == 1, small[c : c + 1, half:], last)
        out[c, tall + 2 * short :, :] = last.astype(bf16)


def share_kernel(parts, out, last):
    total = parts[0].astype(f32)
    for i in range(1, parts.shape[0]):
        total = total + parts[i].astype(f32)
    last[...] = total[-16:, :]
    low = total.astype(bf16)
    for i in range(out.shape[0]):
        out[i] = low


def unpack_kernel(
    at, parts, last_0, last_1, last_2, last_3, query_out, key_out, value_out, output_out, router_out, gain_1_out, gain_2_out, lasts,
):
    count, size, half = parts.shape
    tall = query_out.shape[0] // count
    short = output_out.shape[0] // count
    width = query_out.shape[1]
    rows = []
    for c in range(count):
        here = slice(c * tall, (c + 1) * tall)
        part = parts[c].astype(f32)
        query_out[here, :] = part[:tall, :width]
        key_out[here, :] = part[:tall, width : width + key_out.shape[1]]
        value_out[here, :] = part[:tall, width + key_out.shape[1] :]
        here = slice(c * short, (c + 1) * short)
        output_out[here, :half] = part[tall : tall + short, :]
        output_out[here, half:] = part[tall + short : tall + 2 * short, :]
        last = part[tall + 2 * short :, :]
        rows.append(jnp.concatenate([last[0:1, :], last[1:2, :]], axis=1))
    router_out[...] = jnp.concatenate(rows, axis=0)
    for d, part in enumerate((last_0, last_1, last_2, last_3)):
        lasts[(at[3] + d) % SIDE] = part[...]
    total = lasts[0] + lasts[1] + lasts[2] + lasts[3]
    gain_1_out[:, :half] = total[4:5, :]
    gain_1_out[:, half:] = total[5:6, :]
    gain_2_out[:, :half] = last_0[2:3, :]
    gain_2_out[:, half:] = last_0[3:4, :]


def quarters_kernel(at, own, sib, *refs):
    outs, total = refs[:-1], refs[-1]
    total[...] = (own[...].astype(f32) + sib[...].astype(f32)).astype(bf16)
    rows = outs[0].shape[0]
    for d, out in enumerate(outs):
        out[...] = total[place(at, d, rows), :]


def owned_kernel(own, from_before, from_after, out):
    total = own[...].astype(f32) + from_before[...].astype(f32) + from_after[...].astype(f32)
    out[...] = total.astype(bf16)


def expert_unpack_kernel(at, own, from_after, far_lo, far_hi, from_before, gate_out, up_out, down_out, whole):
    rows = own.shape[0]
    half = far_lo.shape[0]
    whole[place(at, 0, rows), :] = own[...]
    whole[place(at, 1, rows), :] = from_after[...]
    whole[place(at, 3, rows), :] = from_before[...]
    far = (at[3] + 2) % SIDE * rows
    whole[pl.ds(pl.multiple_of(far, half), half), :] = far_lo[...]
    whole[pl.ds(pl.multiple_of(far + half, half), half), :] = far_hi[...]
    depth, width = gate_out.shape[1:]
    gate_out[0] = whole[:depth, :width].astype(f32)
    up_out[0] = whole[:depth, width:].astype(f32)
    down_out[0] = whole[depth:, :].astype(f32)


def body(
    tokens,
    cotangent,
    routes,
    lengths,
    gain_attn,
    w_query,
    w_key,
    w_value,
    w_output,
    gain_mix,
    w_router,
    gate_weight,
    up_weight,
    down_weight,
):
    rows, depth = tokens.shape
    picks = routes.shape[1]
    experts = lax.axis_size(PLANE)
    length = rows * SIDE
    width = w_query.shape[1]
    hidden_units = gate_weight.shape[2]
    capacity = min(rows, 3 * rows * picks // (2 * experts))
    core, y = lax.axis_index("core"), lax.axis_index("head")
    z, x = lax.axis_index("z"), lax.axis_index("x")
    at = jnp.stack([z, x, core, y]).astype(jnp.int32)
    gain_1, gain_2 = gain_attn[None, :], gain_mix[None, :]
    smem = pl.BlockSpec(memory_space=pltpu.SMEM)
    vmem = pl.BlockSpec(memory_space=pltpu.VMEM)
    anywhere = pl.BlockSpec(memory_space=pl.ANY)
    hbm = pl.BlockSpec(memory_space=pltpu.HBM)

    ends = jnp.cumsum(lengths[0], dtype=jnp.int32)
    index = jnp.arange(length, dtype=jnp.int32)
    starts = jnp.max(jnp.where(index[:, None] >= ends[None, :], ends[None, :], 0), axis=1)
    column_starts = starts[:, None]
    lane = jnp.arange(LANES)
    frequency = rope_base ** (-2.0 * (lane % (HEAD_DIM // 2)).astype(f32) / HEAD_DIM)
    angles = (index - starts).astype(f32)[:, None] * frequency[None, :]
    cosine = jnp.cos(angles)
    sine = jnp.sin(angles) * jnp.where(lane % HEAD_DIM < HEAD_DIM // 2, -1.0, 1.0)[None, :]

    half = width // 2
    mine = lax.dynamic_slice_in_dim(w_output, core * half, half, axis=0)
    mine = jnp.broadcast_to(mine[None], (SIDE, half, depth))
    token_parts = ring_gather(tokens, line_shift)
    own_weights = [gate_weight, up_weight, down_weight]
    sib_weights = [swap_core(a) for a in own_weights]
    named = jnp.pad(routes.T.astype(bf16), ((0, 16 - picks), (0, depth - rows)))
    marked = jnp.concatenate([cotangent, named], axis=0)
    grads_u = [shift_u(marked, -1), shift_u(marked, 2), shift_u(marked, 1)]
    grads_before, grads_after = shift_w(marked, 1), shift_w(marked, -1)
    mine, *token_parts[2:4] = together(mine, *token_parts[2:4])
    output_mine = swap_all(mine, "head")
    grads_rest = jnp.concatenate(grads_u, axis=0)
    token_parts[2], grads_rest = together(token_parts[2], grads_rest)
    grads_before_rest, grads_after_rest = shift_w(grads_rest, 1), shift_w(grads_rest, -1)

    normed, query, key, value, mixed, log_total, *mixed_out = call(
        attend_kernel,
        [
            array((length, depth), bf16),
            *[array((length, width), bf16)] * 4,
            array((length, LANES), f32),
            *[array((rows, width), bf16)] * SIDE,
        ],
        [at, *token_parts, gain_1, w_query, w_key, w_value, cosine, sine, column_starts],
        specs=[smem] + [vmem] * 12,
        out_specs=[hbm] * 6 + [vmem] * 4,
        scratch=[
            *[pltpu.VMEM((length, depth), bf16)] * 2,
            *[pltpu.VMEM((length, width), bf16)] * 4,
            pltpu.VMEM((length, LANES), f32),
            pltpu.SemaphoreType.DMA((SIDE, 6)),
        ],
        flops=12 * 10**9,
    )
    mixed_in = direct_swap(mixed_out, line_shift)
    output_mine, mixed_in[0] = together(output_mine, mixed_in[0])
    output_sib = swap_core(output_mine)
    router_rows = w_router.T.astype(bf16)
    router_wide = jnp.pad(w_router, ((0, 0), (0, LANES - experts))).astype(bf16)
    at_join, grads_before_rest, grads_after_rest = together(
        at, grads_before_rest, grads_after_rest
    )
    hidden, inputs = call(
        join_kernel,
        [array((rows, depth), f32), array((rows, depth), bf16)],
        [at_join, *mixed_in, output_mine, output_sib, tokens, gain_2],
        specs=[smem] + [vmem] * 8,
        flops=3 * 10**9,
        vmem=40,
    )

    u_parts = [shift_u(inputs, -1), shift_u(inputs, 2), shift_u(inputs, 1)]
    before_own, after_own = shift_w(inputs, 1), shift_w(inputs, -1)
    u_parts[0], grads_before, grads_after_rest, q_late, k_late, v_late = together(
        u_parts[0], grads_before, grads_after_rest, w_query, w_key, w_value
    )
    grads_far_own = shift_w(grads_before, 1)
    grads_far_rest = shift_w(grads_after_rest, -1)
    w_own = jnp.concatenate([q_late, k_late, v_late], axis=1)
    w_mine = lax.dynamic_slice_in_dim(w_own, core * (depth // 2), depth // 2, axis=0)
    w_mine = all_blocks(w_mine, "head")
    u_rest = jnp.concatenate(u_parts, axis=0)
    before_rest, after_rest = shift_w(u_rest, 1), shift_w(u_rest, -1)
    slots = SIDE * capacity
    half = array((length // 2 + 32, depth), bf16)

    def experts_on(at, x_parts, g_parts):
        outs = [
            half,
            half,
            array((experts, rows), f32),
            array((length, depth), bf16),
            array((2, slots, depth), bf16),
            array((2, slots, depth), bf16),
            array((2, slots, hidden_units), bf16),
            array((2, slots, 2 * hidden_units), bf16),
        ]
        args = [at, *x_parts, *g_parts, router_wide, *own_weights, *sib_weights]
        return list(call(
            functools.partial(expert_kernel, capacity),
            outs,
            args,
            specs=[smem, *[anywhere] * 4, vmem, *[anywhere] * 6],
            out_specs=[hbm, hbm, vmem, *[hbm] * 5],
            scratch=[
                pltpu.VMEM((SIDE, rows, depth), bf16),
                pltpu.VMEM((SIDE, rows + 16, depth), bf16),
                pltpu.VMEM((2, depth, hidden_units), bf16),
                pltpu.VMEM((2, depth, hidden_units), bf16),
                pltpu.VMEM((2, hidden_units, depth), bf16),
                *[pltpu.VMEM((2, slots, depth), bf16)] * 3,
                pltpu.VMEM((2, slots, hidden_units), bf16),
                pltpu.VMEM((2, slots, 2 * hidden_units), bf16),
                pltpu.VMEM((SIDE, 2 * capacity, rows), bf16),
                pltpu.VMEM((SIDE, 2 * capacity, depth), bf16),
                pltpu.VMEM((SIDE, 2 * capacity, depth), bf16),
                pltpu.VMEM((SIDE, rows + 16, depth), bf16),
                pltpu.VMEM((SIDE, rows, depth), bf16),
                pltpu.SemaphoreType.DMA((SIDE,)),
                pltpu.SemaphoreType.DMA((SIDE,)),
                pltpu.SemaphoreType.DMA((2, 3)),
                pltpu.SemaphoreType.DMA((SIDE,)),
                pltpu.SemaphoreType.DMA((SIDE,)),
                pltpu.SemaphoreType.DMA((2, 4)),
            ],
            flops=14 * 10**9,
        ))

    column = experts_on(at, [inputs, u_rest], [marked, grads_rest])
    before_own, after_rest, before_rest, column[0] = together(
        before_own, after_rest, before_rest, column[0]
    )
    far_own, far_rest = shift_w(before_own, 1), shift_w(after_rest, -1)
    at_next, column[0], grads_far_own, grads_far_rest = together(
        at, column[0], grads_far_own, grads_far_rest
    )
    right = experts_on(at_next, [after_own, after_rest], [grads_after, grads_after_rest])
    at_next, right[0], w_mine = together(at, right[0], w_mine)
    w_sib = swap_core(w_mine)
    far = experts_on(at_next, [far_own, far_rest], [grads_far_own, grads_far_rest])
    at_next, far[0] = together(at, far[0])
    left = experts_on(at_next, [before_own, before_rest], [grads_before, grads_before_rest])
    results = [column, right, far, left]

    weight_rows = depth + hidden_units
    flat = [a for r in results for a in r[4:]]

    def expert_weights(e):
        return call(
            functools.partial(expert_weights_kernel, e),
            [array((weight_rows, depth), bf16)],
            flat,
            specs=[anywhere] * len(flat),
            scratch=[
                *[pltpu.VMEM((SIDE, *a.shape[1:]), bf16) for a in flat[:4]],
                pltpu.VMEM((weight_rows, depth), f32),
                pltpu.SemaphoreType.DMA((SIDE, 4)),
            ],
            flops=10 * 10**9,
        )[0]

    from_before, from_after, _ = ring_sum([(r[0], r[1]) for r in results], shift_w)
    folded = list(call(
        fold_kernel,
        [array((rows + 16, depth), bf16)] * SIDE,
        [column[0], column[1], *from_before, *from_after],
        flops=2 * 10**9,
    ))
    flat[0], folded[0] = together(flat[0], folded[0])
    own_grads = expert_weights(0)
    grad_terms = direct_swap(folded, shift_u)
    grad_terms[0], own_grads = together(grad_terms[0], own_grads)

    grad_hidden, grad_low = call(
        turn_kernel,
        [array((rows, depth), f32), array((rows + experts + 16, depth), bf16)],
        [*grad_terms, column[2], router_rows, inputs, hidden, gain_2, cotangent],
        flops=4 * 10**9,
        vmem=40,
    )
    flat[0], grad_low = together(flat[0], grad_low)
    sib_grads = expert_weights(1)
    grad_parts, (sib_grads,) = ring_gather(grad_low, line_shift, sib_grads)
    sib_sums = swap_core(sib_grads)
    quarters = list(call(
        quarters_kernel,
        [array((weight_rows // SIDE, depth), bf16)] * SIDE,
        [at, own_grads, sib_sums],
        specs=[smem] + [vmem] * 2,
        scratch=[pltpu.VMEM((weight_rows, depth), bf16)],
        flops=3 * 10**9,
    ))
    quarter_far, quarter_after = line_shift(quarters[2], 1), line_shift(quarters[3], -1)
    at_back, quarters[0] = together(at, quarters[0])
    *mixes, grad_hidden = together(*[r[3] for r in results], grad_hidden)
    mix_far, mix_after = shift_w(mixes[2], 1), shift_w(mixes[3], -1)
    grads, *grads_out = call(
        attend_back_kernel,
        [array((length, 2 * width), bf16), *[array((rows, 2 * width), bf16)] * SIDE],
        [
            at_back,
            *grad_parts,
            w_output,
            query,
            key,
            value,
            mixed,
            log_total,
            starts[None, :],
            cosine,
            sine,
        ],
        specs=[smem] + [vmem] * 14,
        scratch=[pltpu.VMEM((length, width), bf16), pltpu.VMEM((length, width), f32)],
        flops=12 * 10**9,
    )
    grads_in = direct_swap(grads_out, line_shift)
    tall, short = depth // experts, width // experts
    size = tall + 2 * short + 16
    quarter_up = (quarters[1].astype(f32) + quarter_far.astype(f32)).astype(bf16)
    at_pack, quarter_up, quarter_after, mix_after = together(
        at, quarter_up, quarter_after, mix_after
    )
    quarter_before = line_shift(quarter_up, 1)
    mix_far, grads = together(mix_far, grads)
    mix_up = (mixes[1].astype(f32) + mix_far.astype(f32)).astype(bf16)
    at_pack, mix_up = together(at_pack, mix_up)
    mix_before = shift_w(mix_up, 1)
    packed = call(
        pack_kernel,
        [array((experts, size, depth // 2), bf16)],
        [at_pack, normed, grads, mixed, *grad_parts, w_own, gain_1],
        specs=[smem] + [vmem] * 10,
        scratch=[pltpu.VMEM((SIDE, experts + 16, depth), f32)],
        flops=6 * 10**9,
    )[0]
    packed, *grads_in = together(packed, *grads_in)
    arrived = swap_all(packed, PLANE)
    at_finish, packed, mix_before = together(at, packed, mix_before)
    grad_tokens = call(
        finish_kernel,
        [array((rows, depth), f32)],
        [at_finish, *grads_in, w_mine, w_sib, tokens, gain_1, grad_hidden],
        specs=[smem] + [vmem] * 9,
        flops=4 * 10**9,
    )[0]
    mixes[0], grad_tokens = together(mixes[0], grad_tokens)
    mix_folded = list(call(
        fold_mix_kernel,
        [array((rows, depth), bf16)] * SIDE,
        [mixes[0], mix_before, mix_after],
        flops=2 * 10**9,
    ))
    mix_terms = direct_swap(mix_folded, shift_u)
    arrived, mix_folded[0], mix_terms[1], mix_terms[3] = together(
        arrived, mix_folded[0], mix_terms[1], mix_terms[3]
    )
    shared, last = call(
        share_kernel,
        [array(packed.shape, bf16), array((16, depth // 2), f32)],
        [arrived],
        flops=2 * 10**9,
    )
    quarters[0], last = together(quarters[0], last)
    expert_owned = call(
        owned_kernel,
        [array((weight_rows // SIDE, depth), bf16)],
        [quarters[0], quarter_before, quarter_after],
        flops=10**9,
    )[0]
    expert_parts = ring_gather(expert_owned, line_shift)
    lasts = [last, line_shift(last, -1), line_shift(last, 2), line_shift(last, 1)]
    output = (hidden + sum(term.astype(f32) for term in mix_terms)).astype(bf16)
    mix_terms[1], mix_terms[2], mix_terms[3], expert_parts[2] = together(
        mix_terms[1], mix_terms[2], mix_terms[3], expert_parts[2]
    )
    expert_totals = call(
        expert_unpack_kernel,
        [
            array((1, depth, hidden_units), f32),
            array((1, depth, hidden_units), f32),
            array((1, hidden_units, depth), f32),
        ],
        [at, *expert_parts],
        specs=[smem] + [vmem] * 5,
        scratch=[pltpu.VMEM((weight_rows, depth), bf16)],
        flops=4 * 10**9,
    )
    gathered, output, *expert_totals = together(swap_all(shared, PLANE), output, *expert_totals)
    grad_query, grad_key, grad_value, grad_output, grad_router, grad_gain_1, grad_gain_2 = call(
        unpack_kernel,
        [
            array((depth, width), f32),
            array((depth, LANES), f32),
            array((depth, LANES), f32),
            array((width, depth), f32),
            array((experts, depth), f32),
            array((1, depth), f32),
            array((1, depth), f32),
        ],
        [at, gathered, *lasts],
        specs=[smem] + [vmem] * 5,
        scratch=[pltpu.VMEM((SIDE, 16, depth // 2), f32)],
        flops=4 * 10**9,
    )

    return (
        output,
        grad_tokens,
        grad_gain_1[0],
        grad_query,
        grad_key,
        grad_value,
        grad_output,
        grad_gain_2[0],
        grad_router.T,
        *expert_totals,
    )


def solution(mesh):
    axes = (*PLANE, "head")
    mesh = jax.sharding.Mesh(mesh.devices.reshape(SIDE, SIDE, 2, SIDE), axes)
    rows = P(axes, None)
    per_expert = P(PLANE, None, None)
    columns = P(None, "head")
    in_specs = (
        rows,
        rows,
        rows,
        P(PLANE, None),
        P(),
        columns,
        columns,
        columns,
        P("head", None),
        P(),
        P(),
        per_expert,
        per_expert,
        per_expert,
    )
    out_specs = (
        rows,
        rows,
        P(),
        columns,
        columns,
        columns,
        P("head", None),
        P(),
        P(),
        per_expert,
        per_expert,
        per_expert,
    )
    return jax.shard_map(body, mesh=mesh, in_specs=in_specs, out_specs=out_specs, check_vma=False)
```

```python
import functools

import jax
import jax.numpy as jnp
from jax import lax
from jax.experimental import pallas as pl
from jax.experimental.pallas import tpu as pltpu
from jax.sharding import PartitionSpec as P

HEAD_DIM = 64
SIDE = 4
LANES = 128
MIB = 1024 * 1024

eps_norm = 1e-06
rope_base = 10000.0
mask_fill = -1000000000.0

bf16 = jnp.bfloat16
f32 = jnp.float32


def dot(left, right):
    return lax.dot_general(left, right, (((1,), (0,)), ((), ())), preferred_element_type=f32)


def dot_rows(left, right):
    return lax.dot_general(left, right, (((1,), (1,)), ((), ())), preferred_element_type=f32)


def dot_cols(left, right):
    return lax.dot_general(left, right, (((0,), (0,)), ((), ())), preferred_element_type=f32)


def call(kernel, out_shapes, args, specs=None, out_specs=None, scratch=(), flops=0, vmem=60):
    moved = sum(a.size * a.dtype.itemsize for a in args)
    moved += sum(s.size * s.dtype.itemsize for s in out_shapes)
    whole = pl.BlockSpec(memory_space=pltpu.VMEM)
    return pl.pallas_call(
        kernel,
        out_shape=out_shapes,
        in_specs=specs or [whole] * len(args),
        out_specs=out_specs or [whole] * len(out_shapes),
        scratch_shapes=list(scratch),
        compiler_params=pltpu.CompilerParams(vmem_limit_bytes=vmem * MIB),
        cost_estimate=pl.CostEstimate(flops=flops, bytes_accessed=moved, transcendentals=0),
    )(*args)


def array(shape, dtype):
    return jax.ShapeDtypeStruct(shape, dtype)


CHIPS = ("z", "x")
PLANE = ("z", "x", "core")


def line_shift(values, step):
    pairs = [(i, (i + step) % SIDE) for i in range(SIDE)]
    return lax.ppermute(values, "head", pairs)


def plane_shift(first, values, step):
    pairs = []
    for i in range(2 * SIDE * SIDE):
        z, x, core = i // (2 * SIDE), i // 2 % SIDE, i % 2
        if (core == 0) == first:
            z = (z + step) % SIDE
        else:
            x = (x + step) % SIDE
        pairs.append((i, (z * SIDE + x) * 2 + core))
    return lax.ppermute(values, PLANE, pairs)


shift_u = functools.partial(plane_shift, True)
shift_w = functools.partial(plane_shift, False)


def swap_core(values):
    return lax.ppermute(values, "core", [(0, 1), (1, 0)])


def together(*values):
    return lax.optimization_barrier(values)


def ring_gather(block, shift, *between):
    half = block.shape[0] // 32 * 16
    from_before, from_after = shift(block, 1), shift(block, -1)
    from_before, from_after, *between = together(from_before, from_after, *between)
    far_lo, far_hi = shift(from_before[:half], 1), shift(from_after[half:], -1)
    parts = [block, from_after, far_lo, far_hi, from_before]
    return (parts, between) if between else parts


def direct_swap(parts, shift):
    return [parts[0], shift(parts[3], -1), shift(parts[2], 2), shift(parts[1], 1)]


def ring_sum(parts, shift):
    before_high, after_low = shift(parts[1][1], 1), shift(parts[3][0], -1)
    low_in, high_in = shift(parts[2][0], 1), shift(parts[2][1], -1)
    up = (parts[1][0].astype(f32) + low_in.astype(f32)).astype(bf16)
    down = (parts[3][1].astype(f32) + high_in.astype(f32)).astype(bf16)
    before_low, after_high = shift(up, 1), shift(down, -1)
    return (before_low, before_high), (after_low, after_high), (up, down)


def swap_all(values, axes):
    return lax.all_to_all(values, axes, 0, 0, tiled=True)


def all_blocks(block, axes):
    count = lax.axis_size(axes)
    return swap_all(jnp.broadcast_to(block[None], (count, *block.shape)), axes)


def rope(values, cosine, sine_signed):
    lane = lax.broadcasted_iota(jnp.int32, cosine.shape, 1)
    front = lane % HEAD_DIM < HEAD_DIM // 2
    out = []
    for at in range(0, values.shape[1], LANES):
        part = values[:, at : at + LANES]
        partner = jnp.where(
            front,
            pltpu.roll(part, LANES - HEAD_DIM // 2, 1),
            pltpu.roll(part, HEAD_DIM // 2, 1),
        )
        out.append(part * cosine + partner * sine_signed)
    return jnp.concatenate(out, axis=1)


def twice(values):
    lane = lax.broadcasted_iota(jnp.int32, values.shape, 1)
    swapped = pltpu.roll(values, HEAD_DIM, 1)
    first = lane < HEAD_DIM
    return jnp.concatenate(
        [jnp.where(first, values, swapped), jnp.where(first, swapped, values)], axis=1
    )


def place(at, distance, rows):
    return pl.ds(pl.multiple_of((at[3] + distance) % SIDE * rows, rows), rows)


def attend_kernel(
    at, own, from_after, far_lo, far_hi, from_before, gain, w_query, w_key, w_value, cosine, sine, starts,
    normed_out, query_out, key_out, value_out, mixed_out, log_out, mixed_0, mixed_1, mixed_2, mixed_3,
    rows_in, normed, query, key, value, mixed, log_total, sems,
):
    rows = own.shape[0]
    width = query.shape[1]
    kept = (normed, query, key, value, mixed, log_total)
    outs = (normed_out, query_out, key_out, value_out, mixed_out, log_out)

    def keep(i, n):
        here = pl.ds(i * rows, rows)
        return pltpu.make_async_copy(kept[n].at[here, :], outs[n].at[here, :], sems.at[i, n])

    rows_in[place(at, 0, rows), :] = own[...]
    rows_in[place(at, 1, rows), :] = from_after[...]
    rows_in[place(at, 3, rows), :] = from_before[...]
    half = rows // 2
    far = (at[3] + 2) % SIDE * rows
    rows_in[pl.ds(pl.multiple_of(far, half), half), :] = far_lo[...]
    rows_in[pl.ds(pl.multiple_of(far + half, half), half), :] = far_hi[...]
    head_of = lax.broadcasted_iota(jnp.int32, (rows, width), 1) // HEAD_DIM
    lane = lax.broadcasted_iota(jnp.int32, (rows, LANES), 1)
    for i in range(SIDE):
        here = slice(i * rows, (i + 1) * rows)
        extent = (i + 1) * rows
        x = rows_in[here, :].astype(f32)
        scale = lax.rsqrt(jnp.mean(x * x, axis=1, keepdims=True) + eps_norm)
        low = (x * scale * gain[...]).astype(bf16)
        normed[here, :] = low
        q = rope(dot(low, w_query[...]), cosine[here, :], sine[here, :]).astype(bf16)
        q = q * jnp.asarray(HEAD_DIM**-0.5, bf16)
        query[here, :] = q
        raw = rope(dot(low, w_key[...]), cosine[here, :], sine[here, :])
        key[here, :] = twice(raw).astype(bf16)
        value[here, :] = twice(dot(low, w_value[...])).astype(bf16)
        column = lax.broadcasted_iota(jnp.int32, (rows, extent), 1)
        row = i * rows + lax.broadcasted_iota(jnp.int32, (rows, extent), 0)
        bias = jnp.where((column >= starts[here, :]) & (column <= row), 0.0, mask_fill)
        total = jnp.zeros((rows, width), f32)
        logs = jnp.zeros((rows, LANES), f32)
        for h in range(width // HEAD_DIM):
            q_h = jnp.where(head_of == h, q, jnp.zeros_like(q))
            scores = dot_rows(q_h, key[:extent, :]) + bias
            peak = jnp.max(scores, axis=1, keepdims=True)
            lifted = jnp.exp(scores - peak)
            summed = jnp.sum(lifted, axis=1, keepdims=True)
            probs = (lifted * (1.0 / summed)).astype(bf16)
            total = jnp.where(head_of == h, dot(probs, value[:extent, :]), total)
            logs = jnp.where(lane == h, peak + jnp.log(summed), logs)
        mixed[here, :] = total.astype(bf16)
        log_total[here, :] = logs
        for n in range(len(kept)):
            keep(i, n).start()
    for d, out in enumerate((mixed_0, mixed_1, mixed_2, mixed_3)):
        out[...] = mixed[place(at, d, rows), :]
    for i in range(SIDE):
        for n in range(len(kept)):
            keep(i, n).wait()


def attend_back_kernel(
    at, part_0, part_1, part_2a, part_2b, part_3, w_output, query_in, key_in, value_in, mixed_in, logs_in, starts,
    cosine_in, sine_in, grads, out_0, out_1, out_2, out_3, grad_in, grad_query,
    query, key, value, mixed, log_total, cosine, sine, sems,
):
    sources = (mixed_in, logs_in, key_in, query_in, value_in, cosine_in, sine_in)
    kept = (mixed, log_total, key, query, value, cosine, sine)
    loads = [pltpu.make_async_copy(a, b, sems.at[n]) for n, (a, b) in enumerate(zip(sources, kept))]
    for load in loads:
        load.start()
    rows, width = out_0.shape[0], query.shape[1]
    length = rows * SIDE
    heads = width // HEAD_DIM
    for d, part in ((0, part_0), (1, part_1), (3, part_3)):
        grad_in[place(at, d, rows), :] = dot_rows(part[:rows, :], w_output[...]).astype(bf16)
    cut = part_2a.shape[0]
    far = (at[3] + 2) % SIDE * rows
    low = pl.ds(pl.multiple_of(far, 16), cut)
    grad_in[low, :] = dot_rows(part_2a[...], w_output[...]).astype(bf16)
    high = pl.ds(pl.multiple_of(far + cut, 16), rows - cut)
    grad_in[high, :] = dot_rows(part_2b[: rows - cut, :], w_output[...]).astype(bf16)
    loads[0].wait()
    both = grad_in[...].astype(f32) * mixed[...].astype(f32)
    both_hi = both.astype(bf16)
    both_lo = (both - both_hi.astype(f32)).astype(bf16)
    marks = lax.broadcasted_iota(jnp.int32, (8, width), 1) // HEAD_DIM
    marks = (marks == lax.broadcasted_iota(jnp.int32, (8, width), 0)).astype(bf16)
    inner = dot_rows(marks, both_hi) + dot_rows(marks, both_lo)
    loads[1].wait()
    logs = jnp.transpose(log_total[...])
    for load in loads[2:]:
        load.wait()
    head_of = lax.broadcasted_iota(jnp.int32, (rows, width), 1) // HEAD_DIM
    lane = lax.broadcasted_iota(jnp.int32, (rows, LANES), 1)
    for j in range(SIDE):
        here = slice(j * rows, (j + 1) * rows)
        first = j * rows
        extent = length - first
        key_at = first + lax.broadcasted_iota(jnp.int32, (rows, extent), 0)
        query_at = first + lax.broadcasted_iota(jnp.int32, (rows, extent), 1)
        allowed = (key_at >= starts[:, first:]) & (key_at <= query_at)
        bias = jnp.where(allowed, 0.0, mask_fill)
        k_here, v_here = key[here, :], value[here, :]
        q_there, g_there = query[first:, :], grad_in[first:, :]
        grad_k = jnp.zeros((rows, width), f32)
        grad_v = jnp.zeros((rows, width), f32)
        grad_q = None
        for h in range(heads):
            mine = head_of == h
            k_h = jnp.where(mine, k_here, jnp.zeros_like(k_here))
            v_h = jnp.where(mine, v_here, jnp.zeros_like(v_here))
            probs = jnp.exp(dot_rows(k_h, q_there) + bias - logs[h : h + 1, first:])
            slopes = probs * (dot_rows(v_h, g_there) - inner[h : h + 1, first:])
            probs_low, slopes_low = probs.astype(bf16), slopes.astype(bf16)
            grad_v = jnp.where(mine, dot(probs_low, g_there), grad_v)
            grad_k = jnp.where(mine, dot(slopes_low, q_there), grad_k)
            term = dot_cols(slopes_low, k_h)
            grad_q = term if grad_q is None else grad_q + term
        if j == 0:
            grad_query[...] = grad_q
        else:
            grad_query[first:, :] = grad_query[first:, :] + grad_q
        compact = []
        for values, turn in ((grad_k, True), (grad_v, False)):
            halves = []
            for lane_at in (0, LANES):
                part = values[:, lane_at : lane_at + LANES]
                part = part + pltpu.roll(part, HEAD_DIM, 1)
                halves.append(rope(part, cosine[here, :], -sine[here, :]) if turn else part)
            compact.append(jnp.where(lane < HEAD_DIM, halves[0], halves[1]).astype(bf16))
        grads[here, width : width + LANES] = compact[0]
        grads[here, width + LANES :] = compact[1]
        turned_q = rope(grad_query[here, :], cosine[here, :], -sine[here, :])
        grads[here, :width] = (turned_q * HEAD_DIM**-0.5).astype(bf16)
    for d, out in enumerate((out_0, out_1, out_2, out_3)):
        out[...] = grads[place(at, d, rows), :]


def join_kernel(
    at, mixed_0, mixed_1, mixed_2, mixed_3, weights, sib_weights, tokens, gain, hidden_out, inputs_out,
):
    half = weights.shape[1]
    mine = pl.ds(pl.multiple_of(at[2] * half, half), half)
    other = pl.ds(pl.multiple_of((1 - at[2]) * half, half), half)
    hidden = tokens[...].astype(f32)
    for d, part in enumerate((mixed_0, mixed_1, mixed_2, mixed_3)):
        owner = (at[3] + d) % SIDE
        hidden = hidden + dot(part[:, mine], weights[owner])
        hidden = hidden + dot(part[:, other], sib_weights[owner])
    scale = lax.rsqrt(jnp.mean(hidden * hidden, axis=1, keepdims=True) + eps_norm)
    hidden_out[...] = hidden
    inputs_out[...] = (hidden * scale * gain[...]).astype(bf16)


def expert_kernel(capacity, at, x_a, x_b, g_a, g_b, router, *refs):
    own, sib = refs[:3], refs[3:6]
    (grad_lo, grad_hi, share_out, mix_out, rows_out, grads_out, active_out, slopes_out,
     x_blocks, g_blocks, w_gate, w_up, w_down, taken_x, taken_g, grads, active, slopes, marks, grad_slots, mix_slots,
     grad_blocks, mix_blocks, x_sem, g_sem, w_sem, mix_sem, grad_sem, save_sem) = refs[6:]
    rows = x_a.shape[0]
    picks = 8
    experts = share_out.shape[0]
    taken = g_blocks.shape[1]
    z, x, core = at[0], at[1], at[2]
    me = (z * SIDE + x) * 2 + core
    ids = (me, me + 1 - 2 * core)
    x_from = (x_a, *[x_b.at[pl.ds(b * rows, rows), :] for b in range(SIDE - 1)])
    g_from = (g_a, *[g_b.at[pl.ds(b * taken, taken), :] for b in range(SIDE - 1)])
    saved = ((taken_x, rows_out), (grads, grads_out), (active, active_out), (slopes, slopes_out))

    def x_copy(b):
        return pltpu.make_async_copy(x_from[b], x_blocks.at[b], x_sem.at[b])

    def g_copy(b):
        return pltpu.make_async_copy(g_from[b], g_blocks.at[b], g_sem.at[b])

    def w_copy(e, n):
        there = (w_gate, w_up, w_down)[n].at[e]
        return pltpu.make_async_copy((own, sib)[e][n].at[0], there, w_sem.at[e, n])

    def mix_copy(b):
        there = mix_out.at[pl.ds(b * rows, rows), :]
        return pltpu.make_async_copy(mix_blocks.at[b], there, mix_sem.at[b])

    def grad_copy(b):
        out = grad_lo if b < SIDE // 2 else grad_hi
        there = pl.ds(b % (SIDE // 2) * taken, taken)
        return pltpu.make_async_copy(grad_blocks.at[b], out.at[there, :], grad_sem.at[b])

    def save(e, n):
        return pltpu.make_async_copy(saved[n][0].at[e], saved[n][1].at[e], save_sem.at[e, n])

    for b in range(SIDE):
        g_copy(b).start()
        x_copy(b).start()
    for e in range(2):
        for n in range(3):
            w_copy(e, n).start()

    expert = lax.broadcasted_iota(jnp.int32, (experts, rows), 0)
    token = lax.broadcasted_iota(jnp.int32, (rows, rows), 0)
    earlier = token < lax.broadcasted_iota(jnp.int32, (rows, rows), 1)
    earlier = earlier.astype(f32).astype(bf16)
    slot = lax.broadcasted_iota(jnp.int32, (capacity, rows), 0).astype(f32)
    gates, masks = ([], []), ([], [])
    for b in range(SIDE):
        there = slice(b * capacity, (b + 1) * capacity)
        g_copy(b).wait()
        named = g_blocks[b, rows : rows + picks, :rows].astype(f32).astype(jnp.int32)
        used = jnp.zeros((experts, rows), f32)
        for p in range(picks):
            used = jnp.where(named[p : p + 1, :] == expert, 1.0, used)
        rank = jnp.where(used > 0, dot(used.astype(bf16), earlier), -1.0)
        x_copy(b).wait()
        logits = jnp.transpose(dot(x_blocks[b], router[...]))[:experts, :]
        peak = jnp.max(jnp.where(used > 0, logits, mask_fill), axis=0, keepdims=True)
        raised = jnp.where(used > 0, jnp.exp(jnp.minimum(logits - peak, 0.0)), 0.0)
        ratio = raised / jnp.sum(raised, axis=0, keepdims=True)
        if b == 0:
            share_out[...] = ratio
        for e in range(2):
            mine = expert == ids[e]
            place_row = jnp.sum(jnp.where(mine, rank, 0.0), axis=0, keepdims=True)
            share_row = jnp.sum(jnp.where(mine, ratio, 0.0), axis=0, keepdims=True)
            mask = slot == place_row
            masks[e].append(mask)
            marks[b, e * capacity : (e + 1) * capacity, :] = mask.astype(f32).astype(bf16)
            gates[e].append(jnp.sum(jnp.where(mask, share_row, 0.0), axis=1, keepdims=True))
        both = dot(marks[b], x_blocks[b]).astype(bf16)
        taken_x[0, there, :], taken_x[1, there, :] = both[:capacity, :], both[capacity:, :]
        both = dot(marks[b], g_blocks[b, :rows, :]).astype(bf16)
        taken_g[0, there, :], taken_g[1, there, :] = both[:capacity, :], both[capacity:, :]
    products = []
    for e in range(2):
        save(e, 0).start()
        gate = jnp.concatenate(gates[e], axis=0)
        here = slice(e * capacity, (e + 1) * capacity)
        w_copy(e, 0).wait()
        w_copy(e, 1).wait()
        gate_pre = dot(taken_x[e], w_gate[e])
        up_pre = dot(taken_x[e], w_up[e])
        sigmoid = 1.0 / (1.0 + jnp.exp(-gate_pre))
        silu = gate_pre * sigmoid
        active[e] = (silu * up_pre).astype(bf16)
        save(e, 2).start()
        w_copy(e, 2).wait()
        produced = dot(active[e], w_down[e]).astype(bf16).astype(f32)
        wide_g = taken_g[e].astype(f32)
        products.append(jnp.sum(wide_g * produced, axis=1, keepdims=True))
        grads[e] = (gate * wide_g).astype(bf16)
        save(e, 1).start()
        mix = (gate * produced).astype(bf16)
        for b in range(SIDE):
            mix_slots[b, here, :] = mix[b * capacity : (b + 1) * capacity, :]
            if e == 1:
                mix_blocks[b] = dot_cols(marks[b], mix_slots[b]).astype(bf16)
                mix_copy(b).start()
        grad_active = dot_rows(grads[e], w_down[e])
        grad_up = (grad_active * silu).astype(bf16)
        slope = sigmoid * (1.0 + gate_pre * (1.0 - sigmoid))
        grad_gate = (grad_active * up_pre * slope).astype(bf16)
        width = grad_gate.shape[1]
        slopes[e, :, :width] = grad_gate
        slopes[e, :, width:] = grad_up
        save(e, 3).start()
        grad_x = (dot_rows(grad_gate, w_gate[e]) + dot_rows(grad_up, w_up[e])).astype(bf16)
        for b in range(SIDE):
            grad_slots[b, here, :] = grad_x[b * capacity : (b + 1) * capacity, :]
    for b in range(SIDE):
        there = slice(b * capacity, (b + 1) * capacity)
        grad_blocks[b, :rows, :] = dot_cols(marks[b], grad_slots[b]).astype(bf16)
        full = jnp.zeros((experts, rows), f32)
        for e in range(2):
            row = jnp.where(masks[e][b], products[e][there, :], 0.0)
            full = jnp.where(expert == ids[e], jnp.sum(row, axis=0, keepdims=True), full)
        high = full.astype(bf16)
        low = (full - high.astype(f32)).astype(bf16)
        parts = [part[i : i + 16, :] for part in (high, low) for i in range(0, experts, 16)]
        tail = jnp.concatenate(parts, axis=1)
        grad_blocks[b, rows:, : tail.shape[1]] = tail
        if tail.shape[1] < grad_blocks.shape[2]:
            rest = grad_blocks[b, rows:, tail.shape[1] :]
            grad_blocks[b, rows:, tail.shape[1] :] = jnp.zeros_like(rest)
        grad_copy(b).start()
    for b in range(SIDE):
        mix_copy(b).wait()
        grad_copy(b).wait()
    for e in range(2):
        for n in range(4):
            save(e, n).wait()


def expert_weights_kernel(e, *refs):
    sources, out = refs[: 4 * SIDE], refs[4 * SIDE]
    *scratch, total, sems = refs[4 * SIDE + 1 :]

    def load(i, n):
        return pltpu.make_async_copy(sources[4 * i + n].at[e], scratch[n].at[i], sems.at[i, n])

    for i in range(SIDE):
        for n in range(4):
            load(i, n).start()
    depth = out.shape[1]
    for i in range(SIDE):
        for n in range(4):
            load(i, n).wait()
        rows_in, grads, active, slopes = (ref[i] for ref in scratch)
        upper, lower = dot_cols(rows_in, slopes), dot_cols(active, grads)
        if i:
            upper, lower = total[:depth, :] + upper, total[depth:, :] + lower
        if i < SIDE - 1:
            total[:depth, :] = upper
            total[depth:, :] = lower
        else:
            out[:depth, :] = upper.astype(bf16)
            out[depth:, :] = lower.astype(bf16)


def fold_kernel(own_lo, own_hi, before_lo, before_hi, after_lo, after_hi, *refs):
    outs, (terms, sums, load_sems, store_sems) = refs[:SIDE], refs[SIDE:]
    rows = outs[0].shape[0]

    def load(i, n):
        refs = (own_lo, before_lo, after_lo) if i < 2 else (own_hi, before_hi, after_hi)
        there = refs[n].at[pl.ds(i % 2 * rows, rows), :]
        return pltpu.make_async_copy(there, terms.at[i, n], load_sems.at[i, n])

    def store(i):
        return pltpu.make_async_copy(sums.at[i], outs[i], store_sems.at[i])

    for i in range(SIDE):
        for n in range(3):
            load(i, n).start()
    for i in range(SIDE):
        for n in range(3):
            load(i, n).wait()
        sums[i] = sum(terms[i, n].astype(f32) for n in range(3)).astype(bf16)
        store(i).start()
    for i in range(SIDE):
        store(i).wait()


def fold_mix_kernel(own, before, after_, *outs):
    rows = outs[0].shape[0]
    for i, out in enumerate(outs):
        part = slice(i * rows, (i + 1) * rows)
        out[...] = sum(ref[part, :].astype(f32) for ref in (own, before, after_)).astype(bf16)


def turn_kernel(
    term_0, term_1, term_2, term_3, shares, router, inputs, hidden_in, gain, cotangent, grad_hidden_out, out,
):
    experts, rows = shares.shape
    total = sum(ref[...].astype(f32) for ref in (term_0, term_1, term_2, term_3))
    tail = [total[rows:, i * rows : (i + 1) * rows] for i in range(experts // 8)]
    count = len(tail) // 2
    grad_share = jnp.concatenate([tail[i] + tail[i + count] for i in range(count)], axis=0)
    share = shares[...]
    grad_logits = share * (grad_share - jnp.sum(share * grad_share, axis=0, keepdims=True))
    grad_logits = grad_logits.astype(bf16)
    out[rows : rows + experts, :] = dot(grad_logits, inputs[...]).astype(bf16)
    grad = total[:rows, :] + dot_cols(grad_logits, router[...])
    hidden = hidden_in[...]
    scale = lax.rsqrt(jnp.mean(hidden * hidden, axis=1, keepdims=True) + eps_norm)
    gain_row = jnp.sum(grad * hidden * scale, axis=0, keepdims=True)
    row = lax.broadcasted_iota(jnp.int32, (16, grad.shape[1]), 0)
    out[rows + experts :, :] = jnp.where(row == 0, gain_row, 0.0).astype(bf16)
    grad = grad * gain[...]
    inner = jnp.mean(grad * hidden, axis=1, keepdims=True)
    grad = cotangent[...].astype(f32) + scale * grad - hidden * (scale * scale * scale * inner)
    grad_hidden_out[...] = grad
    out[:rows, :] = grad.astype(bf16)


def finish_kernel(at, g_0, g_1, g_2, g_3, weights, sib_weights, tokens, gain, grad_hidden, out):
    mine = other = None
    for d, part in enumerate((g_0, g_1, g_2, g_3)):
        owner = (at[3] + d) % SIDE
        terms = dot_rows(part[...], weights[owner]), dot_rows(part[...], sib_weights[owner])
        mine, other = terms if d == 0 else (mine + terms[0], other + terms[1])
    first = at[2] == 0
    grad = jnp.concatenate([jnp.where(first, mine, other), jnp.where(first, other, mine)], axis=1)
    grad = grad * gain[...]
    x = tokens[...].astype(f32)
    scale = lax.rsqrt(jnp.mean(x * x, axis=1, keepdims=True) + eps_norm)
    inner = jnp.mean(grad * x, axis=1, keepdims=True)
    out[...] = grad_hidden[...] + scale * grad - x * (scale * scale * scale * inner)


def pack_kernel(
    at, normed, grads, mixed, part_0, part_1, part_2a, part_2b, part_3, w_own, gain, out, smalls,
):
    count, _, half = out.shape
    rows = mixed.shape[0] // SIDE
    cut = part_2a.shape[0]
    inner = dot_cols(normed[...], grads[...])
    outer = jnp.zeros((mixed.shape[1], normed.shape[1]), f32)
    for d, part in ((0, part_0), (1, part_1), (3, part_3)):
        outer = outer + dot_cols(mixed[place(at, d, rows), :], part[:rows, :])
        smalls[(at[3] + d) % SIDE] = part[rows:, :].astype(f32)
    far = (at[3] + 2) % SIDE * rows
    low = pl.ds(pl.multiple_of(far, 16), cut)
    outer = outer + dot_cols(mixed[low, :], part_2a[...])
    high = pl.ds(pl.multiple_of(far + cut, 16), rows - cut)
    outer = outer + dot_cols(mixed[high, :], part_2b[: rows - cut, :])
    smalls[(at[3] + 2) % SIDE] = part_2b[rows - cut :, :].astype(f32)
    small = smalls[0] + smalls[1] + smalls[2] + smalls[3]
    along = inner * w_own[...].astype(f32)
    along_hi = along.astype(bf16)
    along_lo = (along - along_hi.astype(f32)).astype(bf16)
    ones = jnp.ones((8, along.shape[1]), bf16)
    gain_1 = (dot_rows(ones, along_hi) + dot_rows(ones, along_lo)) / gain[...]
    gain_1, gain_2 = gain_1[0:1, :], small[count : count + 1, :]
    row = lax.broadcasted_iota(jnp.int32, (16, half), 0)
    gains = jnp.zeros((16, half), f32)
    for i, part in enumerate((gain_2[:, :half], gain_2[:, half:], gain_1[:, :half], gain_1[:, half:])):
        gains = jnp.where(row == 2 + i, part, gains)
    inner, outer = inner.astype(bf16), outer.astype(bf16)
    tall, short = inner.shape[0] // count, outer.shape[0] // count
    for c in range(count):
        out[c, :tall, :] = inner[c * tall : (c + 1) * tall, :]
        part = outer[c * short : (c + 1) * short, :].astype(f32)
        part = jnp.concatenate([part[:, :half], part[:, half:]], axis=0)
        out[c, tall : tall + 2 * short, :] = part.astype(bf16)
        last = jnp.where(row == 0, small[c : c + 1, :half], gains)
        last = jnp.where(row == 1, small[c : c + 1, half:], last)
        out[c, tall + 2 * short :, :] = last.astype(bf16)


def share_kernel(parts, out, last):
    total = parts[0].astype(f32)
    for i in range(1, parts.shape[0]):
        total = total + parts[i].astype(f32)
    last[...] = total[-16:, :]
    low = total.astype(bf16)
    for i in range(out.shape[0]):
        out[i] = low


def unpack_kernel(
    at, parts, last_0, last_1, last_2, last_3, query_out, key_out, value_out, output_out, router_out, gain_1_out, gain_2_out, lasts,
):
    count, size, half = parts.shape
    tall = query_out.shape[0] // count
    short = output_out.shape[0] // count
    width = query_out.shape[1]
    rows = []
    for c in range(count):
        here = slice(c * tall, (c + 1) * tall)
        part = parts[c].astype(f32)
        query_out[here, :] = part[:tall, :width]
        key_out[here, :] = part[:tall, width : width + key_out.shape[1]]
        value_out[here, :] = part[:tall, width + key_out.shape[1] :]
        here = slice(c * short, (c + 1) * short)
        output_out[here, :half] = part[tall : tall + short, :]
        output_out[here, half:] = part[tall + short : tall + 2 * short, :]
        last = part[tall + 2 * short :, :]
        rows.append(jnp.concatenate([last[0:1, :], last[1:2, :]], axis=1))
    router_out[...] = jnp.concatenate(rows, axis=0)
    for d, part in enumerate((last_0, last_1, last_2, last_3)):
        lasts[(at[3] + d) % SIDE] = part[...]
    total = lasts[0] + lasts[1] + lasts[2] + lasts[3]
    gain_1_out[:, :half] = total[4:5, :]
    gain_1_out[:, half:] = total[5:6, :]
    gain_2_out[:, :half] = last_0[2:3, :]
    gain_2_out[:, half:] = last_0[3:4, :]


def quarters_kernel(at, own, sib, *refs):
    outs, total = refs[:-1], refs[-1]
    total[...] = (own[...].astype(f32) + sib[...].astype(f32)).astype(bf16)
    rows = outs[0].shape[0]
    for d, out in enumerate(outs):
        out[...] = total[place(at, d, rows), :]


def owned_kernel(own, from_before, from_after, out):
    total = own[...].astype(f32) + from_before[...].astype(f32) + from_after[...].astype(f32)
    out[...] = total.astype(bf16)


def expert_unpack_kernel(at, own, from_after, far_lo, far_hi, from_before, gate_out, up_out, down_out, whole):
    rows = own.shape[0]
    half = far_lo.shape[0]
    whole[place(at, 0, rows), :] = own[...]
    whole[place(at, 1, rows), :] = from_after[...]
    whole[place(at, 3, rows), :] = from_before[...]
    far = (at[3] + 2) % SIDE * rows
    whole[pl.ds(pl.multiple_of(far, half), half), :] = far_lo[...]
    whole[pl.ds(pl.multiple_of(far + half, half), half), :] = far_hi[...]
    depth, width = gate_out.shape[1:]
    gate_out[0] = whole[:depth, :width].astype(f32)
    up_out[0] = whole[:depth, width:].astype(f32)
    down_out[0] = whole[depth:, :].astype(f32)


def body(
    tokens,
    cotangent,
    routes,
    lengths,
    gain_attn,
    w_query,
    w_key,
    w_value,
    w_output,
    gain_mix,
    w_router,
    gate_weight,
    up_weight,
    down_weight,
):
    rows, depth = tokens.shape
    picks = routes.shape[1]
    experts = lax.axis_size(PLANE)
    length = rows * SIDE
    width = w_query.shape[1]
    hidden_units = gate_weight.shape[2]
    capacity = min(rows, 3 * rows * picks // (2 * experts))
    core, y = lax.axis_index("core"), lax.axis_index("head")
    z, x = lax.axis_index("z"), lax.axis_index("x")
    at = jnp.stack([z, x, core, y]).astype(jnp.int32)
    gain_1, gain_2 = gain_attn[None, :], gain_mix[None, :]
    smem = pl.BlockSpec(memory_space=pltpu.SMEM)
    vmem = pl.BlockSpec(memory_space=pltpu.VMEM)
    anywhere = pl.BlockSpec(memory_space=pl.ANY)
    hbm = pl.BlockSpec(memory_space=pltpu.HBM)

    ends = jnp.cumsum(lengths[0], dtype=jnp.int32)
    index = jnp.arange(length, dtype=jnp.int32)
    starts = jnp.max(jnp.where(index[:, None] >= ends[None, :], ends[None, :], 0), axis=1)
    column_starts = starts[:, None]
    lane = jnp.arange(LANES)
    frequency = rope_base ** (-2.0 * (lane % (HEAD_DIM // 2)).astype(f32) / HEAD_DIM)
    angles = (index - starts).astype(f32)[:, None] * frequency[None, :]
    cosine = jnp.cos(angles)
    sine = jnp.sin(angles) * jnp.where(lane % HEAD_DIM < HEAD_DIM // 2, -1.0, 1.0)[None, :]

    half = width // 2
    mine = lax.dynamic_slice_in_dim(w_output, core * half, half, axis=0)
    mine = jnp.broadcast_to(mine[None], (SIDE, half, depth))
    token_parts = ring_gather(tokens, line_shift)
    own_weights = [gate_weight, up_weight, down_weight]
    sib_weights = [swap_core(a) for a in own_weights]
    named = jnp.pad(routes.T.astype(bf16), ((0, 16 - picks), (0, depth - rows)))
    marked = jnp.concatenate([cotangent, named], axis=0)
    grads_u = [shift_u(marked, -1), shift_u(marked, 2), shift_u(marked, 1)]
    grads_before, grads_after = shift_w(marked, 1), shift_w(marked, -1)
    mine, *token_parts[2:4] = together(mine, *token_parts[2:4])
    output_mine = swap_all(mine, "head")
    grads_rest = jnp.concatenate(grads_u, axis=0)
    token_parts[2], grads_rest = together(token_parts[2], grads_rest)
    grads_before_rest, grads_after_rest = shift_w(grads_rest, 1), shift_w(grads_rest, -1)

    normed, query, key, value, mixed, log_total, *mixed_out = call(
        attend_kernel,
        [
            array((length, depth), bf16),
            *[array((length, width), bf16)] * 4,
            array((length, LANES), f32),
            *[array((rows, width), bf16)] * SIDE,
        ],
        [at, *token_parts, gain_1, w_query, w_key, w_value, cosine, sine, column_starts],
        specs=[smem] + [vmem] * 12,
        out_specs=[hbm] * 6 + [vmem] * 4,
        scratch=[
            *[pltpu.VMEM((length, depth), bf16)] * 2,
            *[pltpu.VMEM((length, width), bf16)] * 4,
            pltpu.VMEM((length, LANES), f32),
            pltpu.SemaphoreType.DMA((SIDE, 6)),
        ],
        flops=12 * 10**9,
    )
    mixed_in = direct_swap(mixed_out, line_shift)
    output_mine, mixed_in[0] = together(output_mine, mixed_in[0])
    output_sib = swap_core(output_mine)
    router_rows = w_router.T.astype(bf16)
    router_wide = jnp.pad(w_router, ((0, 0), (0, LANES - experts))).astype(bf16)
    at_join, grads_before_rest, grads_after_rest = together(
        at, grads_before_rest, grads_after_rest
    )
    hidden, inputs = call(
        join_kernel,
        [array((rows, depth), f32), array((rows, depth), bf16)],
        [at_join, *mixed_in, output_mine, output_sib, tokens, gain_2],
        specs=[smem] + [vmem] * 8,
        flops=3 * 10**9,
        vmem=40,
    )

    u_parts = [shift_u(inputs, -1), shift_u(inputs, 2), shift_u(inputs, 1)]
    before_own, after_own = shift_w(inputs, 1), shift_w(inputs, -1)
    u_parts[0], grads_before, grads_after_rest, q_late, k_late, v_late = together(
        u_parts[0], grads_before, grads_after_rest, w_query, w_key, w_value
    )
    grads_far_own = shift_w(grads_before, 1)
    grads_far_rest = shift_w(grads_after_rest, -1)
    w_own = jnp.concatenate([q_late, k_late, v_late], axis=1)
    w_mine = lax.dynamic_slice_in_dim(w_own, core * (depth // 2), depth // 2, axis=0)
    w_mine = all_blocks(w_mine, "head")
    u_rest = jnp.concatenate(u_parts, axis=0)
    before_rest, after_rest = shift_w(u_rest, 1), shift_w(u_rest, -1)
    slots = SIDE * capacity
    half = array((length // 2 + 32, depth), bf16)

    def experts_on(at, x_parts, g_parts):
        outs = [
            half,
            half,
            array((experts, rows), f32),
            array((length, depth), bf16),
            array((2, slots, depth), bf16),
            array((2, slots, depth), bf16),
            array((2, slots, hidden_units), bf16),
            array((2, slots, 2 * hidden_units), bf16),
        ]
        args = [at, *x_parts, *g_parts, router_wide, *own_weights, *sib_weights]
        return list(call(
            functools.partial(expert_kernel, capacity),
            outs,
            args,
            specs=[smem, *[anywhere] * 4, vmem, *[anywhere] * 6],
            out_specs=[hbm, hbm, vmem, *[hbm] * 5],
            scratch=[
                pltpu.VMEM((SIDE, rows, depth), bf16),
                pltpu.VMEM((SIDE, rows + 16, depth), bf16),
                pltpu.VMEM((2, depth, hidden_units), bf16),
                pltpu.VMEM((2, depth, hidden_units), bf16),
                pltpu.VMEM((2, hidden_units, depth), bf16),
                *[pltpu.VMEM((2, slots, depth), bf16)] * 3,
                pltpu.VMEM((2, slots, hidden_units), bf16),
                pltpu.VMEM((2, slots, 2 * hidden_units), bf16),
                pltpu.VMEM((SIDE, 2 * capacity, rows), bf16),
                pltpu.VMEM((SIDE, 2 * capacity, depth), bf16),
                pltpu.VMEM((SIDE, 2 * capacity, depth), bf16),
                pltpu.VMEM((SIDE, rows + 16, depth), bf16),
                pltpu.VMEM((SIDE, rows, depth), bf16),
                pltpu.SemaphoreType.DMA((SIDE,)),
                pltpu.SemaphoreType.DMA((SIDE,)),
                pltpu.SemaphoreType.DMA((2, 3)),
                pltpu.SemaphoreType.DMA((SIDE,)),
                pltpu.SemaphoreType.DMA((SIDE,)),
                pltpu.SemaphoreType.DMA((2, 4)),
            ],
            flops=14 * 10**9,
        ))

    column = experts_on(at, [inputs, u_rest], [marked, grads_rest])
    before_own, after_rest, before_rest, column[0] = together(
        before_own, after_rest, before_rest, column[0]
    )
    far_own, far_rest = shift_w(before_own, 1), shift_w(after_rest, -1)
    at_next, column[0], grads_far_own, grads_far_rest = together(
        at, column[0], grads_far_own, grads_far_rest
    )
    right = experts_on(at_next, [after_own, after_rest], [grads_after, grads_after_rest])
    at_next, right[0], w_mine = together(at, right[0], w_mine)
    w_sib = swap_core(w_mine)
    far = experts_on(at_next, [far_own, far_rest], [grads_far_own, grads_far_rest])
    at_next, far[0] = together(at, far[0])
    left = experts_on(at_next, [before_own, before_rest], [grads_before, grads_before_rest])
    results = [column, right, far, left]

    weight_rows = depth + hidden_units
    flat = [a for r in results for a in r[4:]]

    def expert_weights(e):
        return call(
            functools.partial(expert_weights_kernel, e),
            [array((weight_rows, depth), bf16)],
            flat,
            specs=[anywhere] * len(flat),
            scratch=[
                *[pltpu.VMEM((SIDE, *a.shape[1:]), bf16) for a in flat[:4]],
                pltpu.VMEM((weight_rows, depth), f32),
                pltpu.SemaphoreType.DMA((SIDE, 4)),
            ],
            flops=10 * 10**9,
        )[0]

    from_before, from_after, _ = ring_sum([(r[0], r[1]) for r in results], shift_w)
    folded = list(call(
        fold_kernel,
        [array((rows + 16, depth), bf16)] * SIDE,
        [column[0], column[1], *from_before, *from_after],
        specs=[anywhere] * 6,
        out_specs=[hbm] * SIDE,
        scratch=[
            pltpu.VMEM((SIDE, 3, rows + 16, depth), bf16),
            pltpu.VMEM((SIDE, rows + 16, depth), bf16),
            pltpu.SemaphoreType.DMA((SIDE, 3)),
            pltpu.SemaphoreType.DMA((SIDE,)),
        ],
        flops=2 * 10**9,
    ))
    flat[0], folded[0] = together(flat[0], folded[0])
    own_grads = expert_weights(0)
    grad_terms = direct_swap(folded, shift_u)
    grad_terms[0], own_grads = together(grad_terms[0], own_grads)

    grad_hidden, grad_low = call(
        turn_kernel,
        [array((rows, depth), f32), array((rows + experts + 16, depth), bf16)],
        [*grad_terms, column[2], router_rows, inputs, hidden, gain_2, cotangent],
        flops=4 * 10**9,
        vmem=40,
    )
    flat[0], grad_low = together(flat[0], grad_low)
    sib_grads = expert_weights(1)
    grad_parts, (sib_grads,) = ring_gather(grad_low, line_shift, sib_grads)
    sib_sums = swap_core(sib_grads)
    quarters = list(call(
        quarters_kernel,
        [array((weight_rows // SIDE, depth), bf16)] * SIDE,
        [at, own_grads, sib_sums],
        specs=[smem] + [vmem] * 2,
        scratch=[pltpu.VMEM((weight_rows, depth), bf16)],
        flops=3 * 10**9,
    ))
    quarter_far, quarter_after = line_shift(quarters[2], 1), line_shift(quarters[3], -1)
    at_back, quarters[0] = together(at, quarters[0])
    *mixes, grad_hidden = together(*[r[3] for r in results], grad_hidden)
    mix_far, mix_after = shift_w(mixes[2], 1), shift_w(mixes[3], -1)
    grads, *grads_out = call(
        attend_back_kernel,
        [array((length, 2 * width), bf16), *[array((rows, 2 * width), bf16)] * SIDE],
        [
            at_back,
            *grad_parts,
            w_output,
            query,
            key,
            value,
            mixed,
            log_total,
            starts[None, :],
            cosine,
            sine,
        ],
        specs=[smem] + [vmem] * 6 + [anywhere] * 5 + [vmem] + [anywhere] * 2,
        scratch=[
            pltpu.VMEM((length, width), bf16),
            pltpu.VMEM((length, width), f32),
            *[pltpu.VMEM((length, width), bf16)] * 4,
            *[pltpu.VMEM((length, LANES), f32)] * 3,
            pltpu.SemaphoreType.DMA((7,)),
        ],
        flops=12 * 10**9,
    )
    grads_in = direct_swap(grads_out, line_shift)
    tall, short = depth // experts, width // experts
    size = tall + 2 * short + 16
    quarter_up = (quarters[1].astype(f32) + quarter_far.astype(f32)).astype(bf16)
    at_pack, quarter_up, quarter_after, mix_after = together(
        at, quarter_up, quarter_after, mix_after
    )
    quarter_before = line_shift(quarter_up, 1)
    mix_far, grads = together(mix_far, grads)
    mix_up = (mixes[1].astype(f32) + mix_far.astype(f32)).astype(bf16)
    at_pack, mix_up = together(at_pack, mix_up)
    mix_before = shift_w(mix_up, 1)
    packed = call(
        pack_kernel,
        [array((experts, size, depth // 2), bf16)],
        [at_pack, normed, grads, mixed, *grad_parts, w_own, gain_1],
        specs=[smem] + [vmem] * 10,
        scratch=[pltpu.VMEM((SIDE, experts + 16, depth), f32)],
        flops=6 * 10**9,
    )[0]
    packed, *grads_in = together(packed, *grads_in)
    arrived = swap_all(packed, PLANE)
    at_finish, packed, mix_before = together(at, packed, mix_before)
    grad_tokens = call(
        finish_kernel,
        [array((rows, depth), f32)],
        [at_finish, *grads_in, w_mine, w_sib, tokens, gain_1, grad_hidden],
        specs=[smem] + [vmem] * 9,
        flops=4 * 10**9,
    )[0]
    mixes[0], grad_tokens = together(mixes[0], grad_tokens)
    mix_folded = list(call(
        fold_mix_kernel,
        [array((rows, depth), bf16)] * SIDE,
        [mixes[0], mix_before, mix_after],
        flops=2 * 10**9,
    ))
    mix_terms = direct_swap(mix_folded, shift_u)
    arrived, mix_folded[0], mix_terms[1], mix_terms[3] = together(
        arrived, mix_folded[0], mix_terms[1], mix_terms[3]
    )
    shared, last = call(
        share_kernel,
        [array(packed.shape, bf16), array((16, depth // 2), f32)],
        [arrived],
        flops=2 * 10**9,
    )
    quarters[0], last = together(quarters[0], last)
    expert_owned = call(
        owned_kernel,
        [array((weight_rows // SIDE, depth), bf16)],
        [quarters[0], quarter_before, quarter_after],
        flops=10**9,
    )[0]
    expert_parts = ring_gather(expert_owned, line_shift)
    lasts = [last, line_shift(last, -1), line_shift(last, 2), line_shift(last, 1)]
    output = (hidden + sum(term.astype(f32) for term in mix_terms)).astype(bf16)
    mix_terms[1], mix_terms[2], mix_terms[3], expert_parts[2] = together(
        mix_terms[1], mix_terms[2], mix_terms[3], expert_parts[2]
    )
    expert_totals = call(
        expert_unpack_kernel,
        [
            array((1, depth, hidden_units), f32),
            array((1, depth, hidden_units), f32),
            array((1, hidden_units, depth), f32),
        ],
        [at, *expert_parts],
        specs=[smem] + [vmem] * 5,
        scratch=[pltpu.VMEM((weight_rows, depth), bf16)],
        flops=4 * 10**9,
    )
    gathered, output, *expert_totals = together(swap_all(shared, PLANE), output, *expert_totals)
    grad_query, grad_key, grad_value, grad_output, grad_router, grad_gain_1, grad_gain_2 = call(
        unpack_kernel,
        [
            array((depth, width), f32),
            array((depth, LANES), f32),
            array((depth, LANES), f32),
            array((width, depth), f32),
            array((experts, depth), f32),
            array((1, depth), f32),
            array((1, depth), f32),
        ],
        [at, gathered, *lasts],
        specs=[smem] + [vmem] * 5,
        scratch=[pltpu.VMEM((SIDE, 16, depth // 2), f32)],
        flops=4 * 10**9,
    )

    return (
        output,
        grad_tokens,
        grad_gain_1[0],
        grad_query,
        grad_key,
        grad_value,
        grad_output,
        grad_gain_2[0],
        grad_router.T,
        *expert_totals,
    )


def solution(mesh):
    axes = (*PLANE, "head")
    mesh = jax.sharding.Mesh(mesh.devices.reshape(SIDE, SIDE, 2, SIDE), axes)
    rows = P(axes, None)
    per_expert = P(PLANE, None, None)
    columns = P(None, "head")
    in_specs = (
        rows,
        rows,
        rows,
        P(PLANE, None),
        P(),
        columns,
        columns,
        columns,
        P("head", None),
        P(),
        P(),
        per_expert,
        per_expert,
        per_expert,
    )
    out_specs = (
        rows,
        rows,
        P(),
        columns,
        columns,
        columns,
        P("head", None),
        P(),
        P(),
        per_expert,
        per_expert,
        per_expert,
    )
    return jax.shard_map(body, mesh=mesh, in_specs=in_specs, out_specs=out_specs, check_vma=False)
```
